32 devices in a mesh: chan: 8 (over z, x), rep: 4 (over y, core).
Axes of the slice: x: 2, y: 2, z: 4, core: 2. Of those that a mesh axis runs over, the one named last changes fastest.
Arguments:
- strain: bfloat16 [128, 131072], P('chan', 'rep'), may hold values from -60 to 60
- fir_taps: float32 [60], replicated, may hold values from -0.75 to 0.75
- spatial: float32 [9], replicated, may hold values from -2 to 2
Outputs:
- cross_tiles: float32 [128, 5, 32, 32], P('chan', None, 'rep')
The draws below stay inside these ranges and needn't reach their ends.
All inputs are finite; a program needn't handle non-finite values.
Results may differ from the reference program's by a relative error of at most 0.0023.
Values may be sent and summed in bfloat16 or wider, within the bound.
No kernel may reach another device: no remote copies, remote signals or barrier semaphores. Data moves between devices by JAX's collectives and lax.ppermute only.
A program may use at most 64 MiB of HBM per device.

```python
import math
import jax
import jax.numpy as jnp
from jax import lax

CB = 16
TAPS = 60
SPAN = 9
NFFT = 1024
BINS = 32
FIRST_BIN = 16
BLOCKS = 8
CHANNELS = 128
WINDOWS = 128
SAMPLES = 131072
OFFSETS = 5


def draw_strain(key, part):
    noise_key = jax.random.fold_in(key, 11)
    level_key = jax.random.fold_in(key, 23)
    window_count = SAMPLES // NFFT
    raw_noise = jnp.clip(jax.random.normal(noise_key, (CHANNELS, window_count, NFFT), jnp.float32), -6.0, 6.0)
    level_grid = jnp.exp(jax.random.uniform(level_key, (CHANNELS, window_count, 1), jnp.float32, 0.0, jnp.log(10.0)))
    return (raw_noise * level_grid).reshape(CHANNELS, SAMPLES).astype(jnp.bfloat16)


def centred(own_key, dims, scale, limit, kind=jnp.bfloat16):
    entries = jax.random.normal(own_key, dims, jnp.float32) * scale
    return jnp.minimum(jnp.maximum(entries, -limit), limit).astype(kind)


def setup_inputs(seed: int = 0) -> dict:
    seeds = jax.random.split(jax.random.key(seed), 4)
    return {
        "strain": draw_strain(jax.random.fold_in(seeds[3], 71), 0),
        "fir_taps": centred(seeds[1], (TAPS,), TAPS ** -0.5, 0.75, jnp.float32),
        "spatial": centred(seeds[2], (SPAN,), SPAN ** -0.5, 2.0, jnp.float32),
    }


epsilon = 1e-05

def toeplitz_pair(fir_taps):
    source_pos = jnp.arange(128, dtype=jnp.int32)[:, None]
    target_pos = jnp.arange(128, dtype=jnp.int32)[None, :]
    tap_slots = jnp.arange(fir_taps.shape[0], dtype=jnp.int32)
    lag_now = (target_pos - source_pos)[:, :, None]
    lag_before = (target_pos + 128 - source_pos)[:, :, None]
    zero_value = jnp.zeros((), fir_taps.dtype)
    taps_now = lax.optimization_barrier(jnp.sum(jnp.where(lag_now == tap_slots, fir_taps, zero_value), axis=2))
    taps_before = lax.optimization_barrier(jnp.sum(jnp.where(lag_before == tap_slots, fir_taps, zero_value), axis=2))
    return (taps_now, taps_before)

def dft_table(bin_count, first_bin, dft_length, float_type):
    sample_pos = jnp.arange(dft_length, dtype=jnp.int32)[:, None]
    freq_bins = (first_bin + jnp.arange(bin_count, dtype=jnp.int32))[None, :]
    phase_index = sample_pos * freq_bins % dft_length
    phase_angle = phase_index.astype(float_type) * (2.0 * math.pi / dft_length)
    inverse_root = 1.0 / math.sqrt(dft_length)
    return jnp.concatenate([jnp.cos(phase_angle), -jnp.sin(phase_angle)], axis=1) * inverse_root

def window_spectra(channel_rows, spatial, taps_now, taps_before, dft_matrix):
    filter_span = spatial.shape[0]
    row_count = channel_rows.shape[0] - filter_span + 1
    mixed_rows = spatial[0] * channel_rows[0:row_count]
    for offset in range(1, filter_span):
        mixed_rows = mixed_rows + spatial[offset] * channel_rows[offset:offset + row_count]
    time_blocks = mixed_rows.reshape(row_count, -1, 128)
    band_pass = jnp.einsum('cbj,ji->cbi', time_blocks[:, 1:], taps_now, precision=lax.Precision.HIGHEST)
    band_pass = band_pass + jnp.einsum('cbj,ji->cbi', time_blocks[:, :-1], taps_before, precision=lax.Precision.HIGHEST)
    window_data = band_pass.reshape(row_count, -1, dft_matrix.shape[0])
    window_power = lax.optimization_barrier(jnp.mean(window_data * window_data, axis=2, keepdims=True))
    normalized = window_data / jnp.sqrt(window_power + epsilon)
    spectra = jnp.einsum('cwn,nm->cwm', normalized, dft_matrix, precision=lax.Precision.HIGHEST)
    return spectra.reshape(row_count, spectra.shape[1], 2, -1).astype(jnp.bfloat16)

def cross_tile(own_spec, other_spec):
    own_real, own_imag = (own_spec[:, :, 0], own_spec[:, :, 1])
    other_real, other_imag = (other_spec[:, :, 0], other_spec[:, :, 1])
    cross_real = jnp.einsum('cwf,kwf->cfk', own_real, other_real, preferred_element_type=jnp.float32, precision=lax.Precision.HIGHEST)
    cross_real = cross_real + jnp.einsum('cwf,kwf->cfk', own_imag, other_imag, preferred_element_type=jnp.float32, precision=lax.Precision.HIGHEST)
    cross_imag = jnp.einsum('cwf,kwf->cfk', own_imag, other_real, preferred_element_type=jnp.float32, precision=lax.Precision.HIGHEST)
    cross_imag = cross_imag - jnp.einsum('cwf,kwf->cfk', own_real, other_imag, preferred_element_type=jnp.float32, precision=lax.Precision.HIGHEST)
    return jnp.concatenate([cross_real, cross_imag], axis=2)

def reference(strain, fir_taps, spatial):
    taps_now, taps_before = toeplitz_pair(fir_taps)
    dft_matrix = dft_table(BINS, FIRST_BIN, NFFT, fir_taps.dtype)
    rim_width = (SPAN - 1) // 2
    padded = jnp.pad(strain, ((rim_width, rim_width), (128, 0)))

    def one_block(block_index):
        channel_rows = lax.dynamic_slice_in_dim(padded, (block_index * CB).astype(jnp.int32), CB + 2 * rim_width, 0)
        return window_spectra(channel_rows.astype(jnp.float32), spatial, taps_now, taps_before, dft_matrix)
    spectra = lax.map(one_block, jnp.arange(BLOCKS, dtype=jnp.int32))
    inverse = 1.0 / WINDOWS

    def one_tile_row(block_index):
        own_spec = spectra[block_index].astype(jnp.float32)
        tile_list = []
        for offset in range(OFFSETS):
            partner = spectra[(block_index + offset) % BLOCKS].astype(jnp.float32)
            tile_list.append(cross_tile(own_spec, partner))
        return jnp.stack(tile_list, axis=1) * inverse
    cross_tiles = lax.map(one_tile_row, jnp.arange(BLOCKS, dtype=jnp.int32))
    return cross_tiles.reshape(CHANNELS, OFFSETS, BINS, 2 * CB)
```

```python
import math

import jax
import jax.numpy as jnp
import numpy as np
from jax import lax
from jax.experimental import pallas as pl
from jax.experimental.pallas import tpu as pltpu
from jax.sharding import PartitionSpec as P

NFFT = 1024
BINS = 32
FIRST_BIN = 16
STEPS = 4
LANES = 128
HALO = 4
GROUP = 8

epsilon = 1e-05

f32 = jnp.float32
bf16 = jnp.bfloat16


def dot(a, b):
    return lax.dot_general(a, b, (((1,), (0,)), ((), ())), preferred_element_type=f32)


def dot_t(a, b):
    return lax.dot_general(a, b, (((1,), (1,)), ((), ())), preferred_element_type=f32)


def halves(values):
    high = values.astype(bf16)
    low = (values - high.astype(f32)).astype(bf16)
    return high, low


def dft_table():
    sample = np.arange(NFFT)[:, None]
    bins = FIRST_BIN + np.arange(BINS)[None, :]
    angle = (sample * bins % NFFT) * (2.0 * math.pi / NFFT)
    scale = 1.0 / math.sqrt(NFFT)
    real = (np.cos(angle) * scale).reshape(NFFT, BINS // GROUP, GROUP)
    imag = (-np.sin(angle) * scale).reshape(NFFT, BINS // GROUP, GROUP)
    table = np.concatenate([real, imag], axis=2).reshape(NFFT, 2 * BINS).astype(np.float32)
    high = table.astype(jnp.bfloat16)
    low = (table - high.astype(np.float32)).astype(jnp.bfloat16)
    return np.concatenate([high, low], axis=1)


def rounded_halves(values):
    high = lax.reduce_precision(values, exponent_bits=8, mantissa_bits=7)
    return high.astype(bf16), (values - high).astype(bf16)


def toeplitz(fir_taps):
    source = jnp.arange(2 * LANES, dtype=jnp.int32)[:, None]
    target = jnp.arange(LANES, dtype=jnp.int32)[None, :]
    lag = (target + LANES - source)[:, :, None]
    slots = jnp.arange(fir_taps.shape[0], dtype=jnp.int32)
    taps = jnp.sum(jnp.where(lag == slots, fir_taps, 0.0), axis=2)
    return jnp.concatenate(rounded_halves(taps), axis=1)


def mixing(spatial, rows):
    span = spatial.shape[0]
    offset = (jnp.arange(rows + span - 1, dtype=jnp.int32)[None, :] - jnp.arange(rows, dtype=jnp.int32)[:, None])[:, :, None]
    return jnp.sum(jnp.where(offset == jnp.arange(span, dtype=jnp.int32), spatial, 0.0), axis=2)


def filtered(mixed_ref, first, count, rows, toeplitz_ref):
    parts = []
    for block in range(count):
        start = pl.multiple_of((first + block) * LANES, LANES)
        parts.append(mixed_ref[:, pl.ds(start, 2 * LANES)])
    out = dot(jnp.concatenate(parts, axis=0), toeplitz_ref[...])
    out = out[:, :LANES] + out[:, LANES:]
    out = out.reshape(count, 2, rows, LANES)
    return out[:, 0] + out[:, 1]


def windowed(band, first_window, rows, split_ref, scale_ref):
    per = NFFT // LANES
    count = band.shape[0] // per
    squares = band * band
    for window in range(count):
        total = squares[window * per]
        for block in range(1, per):
            total = total + squares[window * per + block]
        power = jnp.sum(total, axis=1, keepdims=True) * (1.0 / NFFT)
        scale_ref[first_window + window] = jnp.broadcast_to(1.0 / jnp.sqrt(power + epsilon), (rows, LANES))
    high = band.astype(bf16).astype(f32)
    low = band - high
    both = jnp.concatenate([high, low], axis=1).astype(bf16)
    for window in range(count):
        for block in range(per):
            split_ref[first_window + window, :, block * LANES : (block + 1) * LANES] = both[window * per + block]


def spectra_of(split_ref, scale_ref, dft_ref, rows):
    windows = split_ref.shape[0]
    out = dot(split_ref[...].reshape(windows * 2 * rows, NFFT), dft_ref[...])
    out = out + pltpu.roll(out, LANES // 2, 1)
    out = out.reshape(windows, 2, rows, LANES)
    return (out[:, 0] + out[:, 1]) * scale_ref[...]


def own_kernel(strain_ref, history_ref, mix_ref, toeplitz_ref, dft_ref, edge_ref, spectra_ref, mixed_ref, split_ref, scale_ref):
    rows, samples = strain_ref.shape

    def mix(columns):
        out = dot(mix_ref[...], columns)
        high, low = halves(out[:rows] + out[rows:])
        return jnp.concatenate([high, low], axis=0)

    mixed_ref[:, :LANES] = mix(history_ref[...])
    step = 4 * NFFT

    def mix_step(i, _):
        start = pl.multiple_of(i * step, step)
        mixed_ref[:, pl.ds(pl.multiple_of(start + LANES, LANES), step)] = mix(strain_ref[:, pl.ds(start, step)])
        return 0

    lax.fori_loop(0, samples // step, mix_step, 0)
    count = step // LANES
    near = lax.broadcasted_iota(jnp.int32, (count, rows // 2, LANES), 1) < HALO

    def filter_step(i, _):
        band = filtered(mixed_ref, i * count, count, rows, toeplitz_ref)
        edge_ref[pl.ds(i * count, count)] = jnp.where(near, band[:, : rows // 2], band[:, rows // 2 :])
        windowed(band, i * (step // NFFT), rows, split_ref, scale_ref)
        return 0

    lax.fori_loop(0, samples // step, filter_step, 0)
    spectra_ref[...] = spectra_of(split_ref, scale_ref, dft_ref, rows)


def edge_kernel(
    before_ref, after_ref, edge_ref, own_ref, mix_ref, toeplitz_ref, dft_ref, out_ref, mixed_ref, split_ref, scale_ref
):
    rows = 2 * HALO
    width = before_ref.shape[1]
    step = 4 * NFFT

    def mix(start, size):
        near = before_ref[:, pl.ds(start, size)].astype(f32)
        far = after_ref[:, pl.ds(start, size)].astype(f32)
        out = dot(mix_ref[...], jnp.concatenate([near, far], axis=0).astype(bf16))
        out = out[:rows] + out[rows:]
        high = out.astype(bf16).astype(f32)
        mixed_ref[:, pl.ds(start, size)] = jnp.concatenate([high, out - high], axis=0).astype(bf16)

    mix(0, LANES)
    lax.fori_loop(0, width // step, lambda i, _: (mix(pl.multiple_of(i * step + LANES, LANES), step), 0)[1], 0)
    count = step // LANES

    def filter_step(i, _):
        band = filtered(mixed_ref, i * count, count, rows, toeplitz_ref) + edge_ref[pl.ds(i * count, count)]
        windowed(band, i * (step // NFFT), rows, split_ref, scale_ref)
        return 0

    lax.fori_loop(0, width // step, filter_step, 0)
    edges = spectra_of(split_ref, scale_ref, dft_ref, rows)
    near = lax.broadcasted_iota(jnp.int32, edges.shape, 1) < HALO
    own = own_ref[...]
    first = jnp.where(near, edges, own[:, :rows])
    second = jnp.where(near, own[:, rows:], edges)
    spectra = jnp.concatenate([first, second], axis=1)
    width_group = 2 * GROUP
    across = LANES // width_group
    slot = lax.broadcasted_iota(jnp.int32, spectra.shape[1:], 1) // width_group
    for group in range(out_ref.shape[0]):
        for outer in range(out_ref.shape[1]):
            tile = jnp.zeros(spectra.shape[1:], f32)
            for inner in range(across):
                shift = (inner - group) * width_group % LANES
                value = spectra[outer * across + inner]
                if shift:
                    value = pltpu.roll(value, shift, 1)
                tile = jnp.where(slot == inner, value, tile)
            out_ref[group, outer] = tile.astype(bf16)


def left_kernel(own_ref, left_ref):
    parts, rows, _ = own_ref.shape
    lane = lax.broadcasted_iota(jnp.int32, (GROUP, LANES), 1)
    mask = lane % GROUP == lax.broadcasted_iota(jnp.int32, (GROUP, LANES), 0)
    real_lane = lax.broadcasted_iota(jnp.int32, (rows, LANES), 1) % (2 * GROUP) < GROUP

    for part in range(parts):
        value = own_ref[part].astype(f32)
        turned = jnp.where(real_lane, pltpu.roll(value, LANES - GROUP, 1), -pltpu.roll(value, GROUP, 1))
        for half, source in enumerate((value, turned)):
            spread = [jnp.where(mask, jnp.broadcast_to(source[c : c + 1], (GROUP, LANES)), 0.0) for c in range(rows)]
            left_ref[half, :, part * LANES : (part + 1) * LANES] = jnp.concatenate(spread, axis=0).astype(bf16)


def tile_kernel(scale, left_ref, *refs):
    partner_refs, out_ref = refs[:-1], refs[-1]
    parts, rows, _ = partner_refs[0].shape
    right = jnp.concatenate(
        [jnp.concatenate([ref[part] for part in range(parts)], axis=1) for ref in partner_refs], axis=0
    )
    real = dot_t(left_ref[0], right) * scale
    imag = dot_t(left_ref[1], right) * scale
    for c in range(rows):
        for s in range(len(partner_refs)):
            a = real[c * GROUP : (c + 1) * GROUP, s * rows : (s + 1) * rows]
            b = imag[c * GROUP : (c + 1) * GROUP, s * rows : (s + 1) * rows]
            out_ref[c, s] = jnp.concatenate([a, b], axis=1)


def call(kernel, out_shape, scratch=(), flops=0, bytes_accessed=0):
    return pl.pallas_call(
        kernel,
        out_shape=out_shape,
        scratch_shapes=list(scratch),
        compiler_params=pltpu.CompilerParams(vmem_limit_bytes=32 * 2**20),
        cost_estimate=pl.CostEstimate(flops=flops, bytes_accessed=bytes_accessed, transcendentals=0),
    )


def per_device(strain, fir_taps, spatial):
    rows, samples = strain.shape
    windows = samples // NFFT
    blocks = samples // LANES
    rep = lax.axis_size("rep")
    chan = lax.axis_size("chan")
    history = lax.ppermute(strain[:, samples - LANES :], "rep", [(i, i + 1) for i in range(rep - 1)])
    tail = jnp.concatenate([history[rows - HALO :], strain[rows - HALO :]], axis=1)
    head = jnp.concatenate([history[:HALO], strain[:HALO]], axis=1)
    before = lax.ppermute(tail, "chan", [(i, i + 1) for i in range(chan - 1)])
    after = lax.ppermute(head, "chan", [(i + 1, i) for i in range(chan - 1)])

    filter_matrix = toeplitz(fir_taps)
    table = jnp.asarray(dft_table())
    mix = mixing(spatial, rows)
    own_mix = jnp.concatenate(rounded_halves(mix[:, HALO : HALO + rows]), axis=0)
    edge_rows = jnp.concatenate([mix[:HALO], mix[rows - HALO :]], axis=0)
    edge_mix = jnp.concatenate([edge_rows[:, :HALO], edge_rows[:, HALO + rows :]], axis=1)
    edge_mix = jnp.concatenate(rounded_halves(edge_mix), axis=0)

    edge, own = call(
        own_kernel,
        (jax.ShapeDtypeStruct((blocks, 2 * HALO, LANES), f32), jax.ShapeDtypeStruct((windows, rows, LANES), f32)),
        [
            pltpu.VMEM((2 * rows, LANES + samples), bf16),
            pltpu.VMEM((windows, 2 * rows, NFFT), bf16),
            pltpu.VMEM((windows, rows, LANES), f32),
        ],
        flops=2 * 2 * rows * samples * 512,
        bytes_accessed=4 * 2**20,
    )(strain, history, own_mix, filter_matrix, table)
    pieces = call(
        edge_kernel,
        jax.ShapeDtypeStruct((rep, windows * 2 * GROUP // LANES, rows, LANES), bf16),
        [
            pltpu.VMEM((4 * HALO, LANES + samples), bf16),
            pltpu.VMEM((windows, 4 * HALO, NFFT), bf16),
            pltpu.VMEM((windows, 2 * HALO, LANES), f32),
        ],
        flops=2 * 2 * rows * samples * 256,
        bytes_accessed=2 * 2**20,
    )(before, after, edge, own, edge_mix, filter_matrix, table)
    gathered = lax.all_to_all(pieces, "rep", split_axis=0, concat_axis=0, tiled=True)
    gathered = gathered.reshape(-1, rows, LANES)
    partners = [gathered]
    for step in range(1, STEPS + 1):
        partners.append(lax.ppermute(gathered, "chan", [((i + step) % chan, i) for i in range(chan)]))
    parts = gathered.shape[0]
    left = call(
        left_kernel,
        jax.ShapeDtypeStruct((2, rows * GROUP, parts * LANES), bf16),
        flops=2**20,
        bytes_accessed=2**20,
    )(gathered)
    scale = 1.0 / (windows * rep)
    return call(
        lambda *refs: tile_kernel(scale, *refs),
        jax.ShapeDtypeStruct((rows, STEPS + 1, BINS // rep, 2 * rows), f32),
        flops=2**24,
        bytes_accessed=2**20,
    )(left, *partners)


def solution(mesh):
    in_specs = (P("chan", "rep"), P(), P())
    out_specs = P("chan", None, "rep", None)
    return jax.shard_map(
        per_device, mesh=mesh, in_specs=in_specs, out_specs=out_specs, check_vma=False
    )
```

```python
import math

import jax
import jax.numpy as jnp
import numpy as np
from jax import lax
from jax.experimental import pallas as pl
from jax.experimental.pallas import tpu as pltpu
from jax.sharding import PartitionSpec as P

NFFT = 1024
BINS = 32
FIRST_BIN = 16
STEPS = 4
LANES = 128
HALO = 4
GROUP = 8

epsilon = 1e-05

f32 = jnp.float32
bf16 = jnp.bfloat16


def dot(a, b):
    return lax.dot_general(a, b, (((1,), (0,)), ((), ())), preferred_element_type=f32)


def dot_t(a, b):
    return lax.dot_general(a, b, (((1,), (1,)), ((), ())), preferred_element_type=f32)


def halves(values):
    high = values.astype(bf16)
    low = (values - high.astype(f32)).astype(bf16)
    return high, low


def dft_table():
    sample = np.arange(NFFT)[:, None]
    bins = FIRST_BIN + np.arange(BINS)[None, :]
    angle = (sample * bins % NFFT) * (2.0 * math.pi / NFFT)
    scale = 1.0 / math.sqrt(NFFT)
    real = (np.cos(angle) * scale).reshape(NFFT, BINS // GROUP, GROUP)
    imag = (-np.sin(angle) * scale).reshape(NFFT, BINS // GROUP, GROUP)
    table = np.concatenate([real, imag], axis=2).reshape(NFFT, 2 * BINS).astype(np.float32)
    high = table.astype(jnp.bfloat16)
    low = (table - high.astype(np.float32)).astype(jnp.bfloat16)
    return np.concatenate([high, low], axis=1)


def rounded_halves(values):
    high = lax.reduce_precision(values, exponent_bits=8, mantissa_bits=7)
    return high.astype(bf16), (values - high).astype(bf16)


def toeplitz(fir_taps):
    source = jnp.arange(2 * LANES, dtype=jnp.int32)[:, None]
    target = jnp.arange(LANES, dtype=jnp.int32)[None, :]
    lag = (target + LANES - source)[:, :, None]
    slots = jnp.arange(fir_taps.shape[0], dtype=jnp.int32)
    taps = jnp.sum(jnp.where(lag == slots, fir_taps, 0.0), axis=2)
    return jnp.concatenate(rounded_halves(taps), axis=1)


def mixing(spatial, rows):
    span = spatial.shape[0]
    offset = (jnp.arange(rows + span - 1, dtype=jnp.int32)[None, :] - jnp.arange(rows, dtype=jnp.int32)[:, None])[:, :, None]
    return jnp.sum(jnp.where(offset == jnp.arange(span, dtype=jnp.int32), spatial, 0.0), axis=2)


def filtered(mixed_ref, first, count, rows, toeplitz_ref):
    parts = []
    for block in range(count):
        start = pl.multiple_of((first + block) * LANES, LANES)
        parts.append(mixed_ref[:, pl.ds(start, 2 * LANES)])
    out = dot(jnp.concatenate(parts, axis=0), toeplitz_ref[...])
    out = out[:, :LANES] + out[:, LANES:]
    out = out.reshape(count, 2, rows, LANES)
    return out[:, 0] + out[:, 1]


def windowed(band, first_window, rows, split_ref, scale_ref):
    per = NFFT // LANES
    count = band.shape[0] // per
    squares = band * band
    for window in range(count):
        total = squares[window * per]
        for block in range(1, per):
            total = total + squares[window * per + block]
        power = jnp.sum(total, axis=1, keepdims=True) * (1.0 / NFFT)
        scale_ref[first_window + window] = jnp.broadcast_to(1.0 / jnp.sqrt(power + epsilon), (rows, LANES))
    high = band.astype(bf16).astype(f32)
    low = band - high
    both = jnp.concatenate([high, low], axis=1).astype(bf16)
    for window in range(count):
        for block in range(per):
            split_ref[first_window + window, :, block * LANES : (block + 1) * LANES] = both[window * per + block]


def spectra_of(split_ref, scale_ref, dft_ref, rows):
    windows = split_ref.shape[0]
    out = dot(split_ref[...].reshape(windows * 2 * rows, NFFT), dft_ref[...])
    out = out + pltpu.roll(out, LANES // 2, 1)
    out = out.reshape(windows, 2, rows, LANES)
    return (out[:, 0] + out[:, 1]) * scale_ref[...]


def own_kernel(strain_ref, history_ref, mix_ref, toeplitz_ref, dft_ref, edge_ref, spectra_ref, mixed_ref, split_ref, scale_ref):
    rows, samples = strain_ref.shape

    def mix(columns):
        out = dot(mix_ref[...], columns)
        high, low = halves(out[:rows] + out[rows:])
        return jnp.concatenate([high, low], axis=0)

    mixed_ref[:, :LANES] = mix(history_ref[...])
    step = samples // 2

    def mix_step(i, _):
        start = pl.multiple_of(i * step, step)
        mixed_ref[:, pl.ds(pl.multiple_of(start + LANES, LANES), step)] = mix(strain_ref[:, pl.ds(start, step)])
        return 0

    lax.fori_loop(0, samples // step, mix_step, 0)
    count = step // LANES
    near = lax.broadcasted_iota(jnp.int32, (count, rows // 2, LANES), 1) < HALO

    def filter_step(i, _):
        band = filtered(mixed_ref, i * count, count, rows, toeplitz_ref)
        edge_ref[pl.ds(i * count, count)] = jnp.where(near, band[:, : rows // 2], band[:, rows // 2 :])
        windowed(band, i * (step // NFFT), rows, split_ref, scale_ref)
        return 0

    lax.fori_loop(0, samples // step, filter_step, 0)
    spectra_ref[...] = spectra_of(split_ref, scale_ref, dft_ref, rows)


def edge_kernel(
    before_ref, after_ref, edge_ref, own_ref, mix_ref, toeplitz_ref, dft_ref, out_ref, mixed_ref, split_ref, scale_ref
):
    rows = 2 * HALO
    width = before_ref.shape[1]
    step = width // LANES * LANES - LANES

    def mix(start, size):
        near = before_ref[:, pl.ds(start, size)].astype(f32)
        far = after_ref[:, pl.ds(start, size)].astype(f32)
        out = dot(mix_ref[...], jnp.concatenate([near, far], axis=0).astype(bf16))
        out = out[:rows] + out[rows:]
        high = out.astype(bf16).astype(f32)
        mixed_ref[:, pl.ds(start, size)] = jnp.concatenate([high, out - high], axis=0).astype(bf16)

    mix(0, LANES)
    lax.fori_loop(0, width // step, lambda i, _: (mix(pl.multiple_of(i * step + LANES, LANES), step), 0)[1], 0)
    count = step // LANES

    def filter_step(i, _):
        band = filtered(mixed_ref, i * count, count, rows, toeplitz_ref) + edge_ref[pl.ds(i * count, count)]
        windowed(band, i * (step // NFFT), rows, split_ref, scale_ref)
        return 0

    lax.fori_loop(0, width // step, filter_step, 0)
    edges = spectra_of(split_ref, scale_ref, dft_ref, rows)
    near = lax.broadcasted_iota(jnp.int32, edges.shape, 1) < HALO
    own = own_ref[...]
    first = jnp.where(near, edges, own[:, :rows])
    second = jnp.where(near, own[:, rows:], edges)
    spectra = jnp.concatenate([first, second], axis=1)
    width_group = 2 * GROUP
    across = LANES // width_group
    slot = lax.broadcasted_iota(jnp.int32, spectra.shape[1:], 1) // width_group
    for group in range(out_ref.shape[0]):
        for outer in range(out_ref.shape[1]):
            tile = jnp.zeros(spectra.shape[1:], f32)
            for inner in range(across):
                shift = (inner - group) * width_group % LANES
                value = spectra[outer * across + inner]
                if shift:
                    value = pltpu.roll(value, shift, 1)
                tile = jnp.where(slot == inner, value, tile)
            out_ref[group, outer] = tile.astype(bf16)


def left_kernel(own_ref, left_ref):
    parts, rows, _ = own_ref.shape
    lane = lax.broadcasted_iota(jnp.int32, (GROUP, LANES), 1)
    mask = lane % GROUP == lax.broadcasted_iota(jnp.int32, (GROUP, LANES), 0)
    real_lane = lax.broadcasted_iota(jnp.int32, (rows, LANES), 1) % (2 * GROUP) < GROUP

    for part in range(parts):
        value = own_ref[part].astype(f32)
        turned = jnp.where(real_lane, pltpu.roll(value, LANES - GROUP, 1), -pltpu.roll(value, GROUP, 1))
        for half, source in enumerate((value, turned)):
            spread = [jnp.where(mask, jnp.broadcast_to(source[c : c + 1], (GROUP, LANES)), 0.0) for c in range(rows)]
            left_ref[half, :, part * LANES : (part + 1) * LANES] = jnp.concatenate(spread, axis=0).astype(bf16)


def tile_kernel(scale, left_ref, *refs):
    partner_refs, out_ref = refs[:-1], refs[-1]
    parts, rows, _ = partner_refs[0].shape
    right = jnp.concatenate(
        [jnp.concatenate([ref[part] for part in range(parts)], axis=1) for ref in partner_refs], axis=0
    )
    real = dot_t(left_ref[0], right) * scale
    imag = dot_t(left_ref[1], right) * scale
    for c in range(rows):
        for s in range(len(partner_refs)):
            a = real[c * GROUP : (c + 1) * GROUP, s * rows : (s + 1) * rows]
            b = imag[c * GROUP : (c + 1) * GROUP, s * rows : (s + 1) * rows]
            out_ref[c, s] = jnp.concatenate([a, b], axis=1)


def call(kernel, out_shape, scratch=(), flops=0, bytes_accessed=0):
    return pl.pallas_call(
        kernel,
        out_shape=out_shape,
        scratch_shapes=list(scratch),
        compiler_params=pltpu.CompilerParams(vmem_limit_bytes=32 * 2**20),
        cost_estimate=pl.CostEstimate(flops=flops, bytes_accessed=bytes_accessed, transcendentals=0),
    )


def per_device(strain, fir_taps, spatial):
    rows, samples = strain.shape
    windows = samples // NFFT
    blocks = samples // LANES
    rep = lax.axis_size("rep")
    chan = lax.axis_size("chan")
    history = lax.ppermute(strain[:, samples - LANES :], "rep", [(i, i + 1) for i in range(rep - 1)])
    tail = jnp.concatenate([history[rows - HALO :], strain[rows - HALO :]], axis=1)
    head = jnp.concatenate([history[:HALO], strain[:HALO]], axis=1)
    tail, head, fir_taps, spatial = lax.optimization_barrier((tail, head, fir_taps, spatial))
    before = lax.ppermute(tail, "chan", [(i, i + 1) for i in range(chan - 1)])
    after = lax.ppermute(head, "chan", [(i + 1, i) for i in range(chan - 1)])

    filter_matrix = toeplitz(fir_taps)
    table = jnp.asarray(dft_table())
    mix = mixing(spatial, rows)
    own_mix = jnp.concatenate(rounded_halves(mix[:, HALO : HALO + rows]), axis=0)
    edge_rows = jnp.concatenate([mix[:HALO], mix[rows - HALO :]], axis=0)
    edge_mix = jnp.concatenate([edge_rows[:, :HALO], edge_rows[:, HALO + rows :]], axis=1)
    edge_mix = jnp.concatenate(rounded_halves(edge_mix), axis=0)

    edge, own = call(
        own_kernel,
        (jax.ShapeDtypeStruct((blocks, 2 * HALO, LANES), f32), jax.ShapeDtypeStruct((windows, rows, LANES), f32)),
        [
            pltpu.VMEM((2 * rows, LANES + samples), bf16),
            pltpu.VMEM((windows, 2 * rows, NFFT), bf16),
            pltpu.VMEM((windows, rows, LANES), f32),
        ],
        flops=2 * 2 * rows * samples * 512,
        bytes_accessed=4 * 2**20,
    )(strain, history, own_mix, filter_matrix, table)
    pieces = call(
        edge_kernel,
        jax.ShapeDtypeStruct((rep, windows * 2 * GROUP // LANES, rows, LANES), bf16),
        [
            pltpu.VMEM((4 * HALO, LANES + samples), bf16),
            pltpu.VMEM((windows, 4 * HALO, NFFT), bf16),
            pltpu.VMEM((windows, 2 * HALO, LANES), f32),
        ],
        flops=2 * 2 * rows * samples * 256,
        bytes_accessed=2 * 2**20,
    )(before, after, edge, own, edge_mix, filter_matrix, table)
    gathered = lax.all_to_all(pieces, "rep", split_axis=0, concat_axis=0, tiled=True)
    gathered = gathered.reshape(-1, rows, LANES)
    partners = [gathered]
    for step in range(1, STEPS + 1):
        partners.append(lax.ppermute(gathered, "chan", [((i + step) % chan, i) for i in range(chan)]))
    parts = gathered.shape[0]
    left = call(
        left_kernel,
        jax.ShapeDtypeStruct((2, rows * GROUP, parts * LANES), bf16),
        flops=2**20,
        bytes_accessed=2**20,
    )(gathered)
    scale = 1.0 / (windows * rep)
    return call(
        lambda *refs: tile_kernel(scale, *refs),
        jax.ShapeDtypeStruct((rows, STEPS + 1, BINS // rep, 2 * rows), f32),
        flops=2**24,
        bytes_accessed=2**20,
    )(left, *partners)


def solution(mesh):
    in_specs = (P("chan", "rep"), P(), P())
    out_specs = P("chan", None, "rep", None)
    return jax.shard_map(
        per_device, mesh=mesh, in_specs=in_specs, out_specs=out_specs, check_vma=False
    )
```

```python
import math

import jax
import jax.numpy as jnp
import numpy as np
from jax import lax
from jax.experimental import pallas as pl
from jax.experimental.pallas import tpu as pltpu
from jax.sharding import PartitionSpec as P

NFFT = 1024
BINS = 32
FIRST_BIN = 16
STEPS = 4
LANES = 128
HALO = 4
GROUP = 8

epsilon = 1e-05

f32 = jnp.float32
bf16 = jnp.bfloat16


def dot(a, b):
    return lax.dot_general(a, b, (((1,), (0,)), ((), ())), preferred_element_type=f32)


def dot_t(a, b):
    return lax.dot_general(a, b, (((1,), (1,)), ((), ())), preferred_element_type=f32)


def halves(values):
    high = values.astype(bf16)
    low = (values - high.astype(f32)).astype(bf16)
    return high, low


def dft_table():
    sample = np.arange(NFFT)[:, None]
    bins = FIRST_BIN + np.arange(BINS)[None, :]
    angle = (sample * bins % NFFT) * (2.0 * math.pi / NFFT)
    scale = 1.0 / math.sqrt(NFFT)
    real = (np.cos(angle) * scale).reshape(NFFT, BINS // GROUP, GROUP)
    imag = (-np.sin(angle) * scale).reshape(NFFT, BINS // GROUP, GROUP)
    table = np.concatenate([real, imag], axis=2).reshape(NFFT, 2 * BINS).astype(np.float32)
    high = table.astype(jnp.bfloat16)
    low = (table - high.astype(np.float32)).astype(jnp.bfloat16)
    return np.concatenate([high, low], axis=1)


def rounded_halves(values):
    high = lax.reduce_precision(values, exponent_bits=8, mantissa_bits=7)
    return high.astype(bf16), (values - high).astype(bf16)


def toeplitz(fir_taps):
    source = jnp.arange(2 * LANES, dtype=jnp.int32)[:, None]
    target = jnp.arange(LANES, dtype=jnp.int32)[None, :]
    lag = (target + LANES - source)[:, :, None]
    slots = jnp.arange(fir_taps.shape[0], dtype=jnp.int32)
    taps = jnp.sum(jnp.where(lag == slots, fir_taps, 0.0), axis=2)
    return jnp.concatenate(rounded_halves(taps), axis=1)


def mixing(spatial, rows):
    span = spatial.shape[0]
    offset = (jnp.arange(rows + span - 1, dtype=jnp.int32)[None, :] - jnp.arange(rows, dtype=jnp.int32)[:, None])[:, :, None]
    return jnp.sum(jnp.where(offset == jnp.arange(span, dtype=jnp.int32), spatial, 0.0), axis=2)


def filtered(mixed_ref, first, count, rows, toeplitz_ref):
    parts = []
    for block in range(count):
        start = pl.multiple_of((first + block) * LANES, LANES)
        parts.append(mixed_ref[:, pl.ds(start, 2 * LANES)])
    out = dot(jnp.concatenate(parts, axis=0), toeplitz_ref[...])
    out = out[:, :LANES] + out[:, LANES:]
    out = out.reshape(count, 2, rows, LANES)
    return out[:, 0] + out[:, 1]


def windowed(band, first_window, rows, split_ref, scale_ref):
    per = NFFT // LANES
    count = band.shape[0] // per
    squares = band * band
    for window in range(count):
        total = squares[window * per]
        for block in range(1, per):
            total = total + squares[window * per + block]
        power = jnp.sum(total, axis=1, keepdims=True) * (1.0 / NFFT)
        scale_ref[first_window + window] = jnp.broadcast_to(1.0 / jnp.sqrt(power + epsilon), (rows, LANES))
    high = band.astype(bf16).astype(f32)
    low = band - high
    both = jnp.concatenate([high, low], axis=1).astype(bf16)
    for window in range(count):
        for block in range(per):
            split_ref[first_window + window, :, block * LANES : (block + 1) * LANES] = both[window * per + block]


def spectra_of(split_ref, scale_ref, dft_ref, rows):
    windows = split_ref.shape[0]
    out = dot(split_ref[...].reshape(windows * 2 * rows, NFFT), dft_ref[...])
    out = out + pltpu.roll(out, LANES // 2, 1)
    out = out.reshape(windows, 2, rows, LANES)
    return (out[:, 0] + out[:, 1]) * scale_ref[...]


def own_kernel(strain_ref, history_ref, mix_ref, toeplitz_ref, dft_ref, edge_ref, spectra_ref, mixed_ref, split_ref, scale_ref):
    rows, samples = strain_ref.shape

    def mix(columns):
        out = dot(mix_ref[...], columns)
        high, low = halves(out[:rows] + out[rows:])
        return jnp.concatenate([high, low], axis=0)

    mixed_ref[:, :LANES] = mix(history_ref[...])
    step = samples // 2

    def mix_step(i, _):
        start = pl.multiple_of(i * step, step)
        mixed_ref[:, pl.ds(pl.multiple_of(start + LANES, LANES), step)] = mix(strain_ref[:, pl.ds(start, step)])
        return 0

    lax.fori_loop(0, samples // step, mix_step, 0)
    count = step // LANES
    near = lax.broadcasted_iota(jnp.int32, (count, rows // 2, LANES), 1) < HALO

    def filter_step(i, _):
        band = filtered(mixed_ref, i * count, count, rows, toeplitz_ref)
        edge_ref[pl.ds(i * count, count)] = jnp.where(near, band[:, : rows // 2], band[:, rows // 2 :])
        windowed(band, i * (step // NFFT), rows, split_ref, scale_ref)
        return 0

    lax.fori_loop(0, samples // step, filter_step, 0)
    spectra_ref[...] = spectra_of(split_ref, scale_ref, dft_ref, rows)


def edge_kernel(
    near_ref,
    far_ref,
    edge_ref,
    own_ref,
    mix_ref,
    toeplitz_ref,
    dft_ref,
    out_ref,
    mixed_ref,
    split_ref,
    scale_ref,
):
    rows = 2 * HALO
    step = near_ref.shape[1] - LANES

    def mix(near, far):
        both = jnp.concatenate([near.astype(f32), far.astype(f32)], axis=0).astype(bf16)
        out = dot(mix_ref[...], both)
        out = out[:rows] + out[rows:]
        high = out.astype(bf16).astype(f32)
        return jnp.concatenate([high, out - high], axis=0).astype(bf16)

    mixed_ref[...] = mix(near_ref[...], far_ref[...])
    band = filtered(mixed_ref, 0, step // LANES, rows, toeplitz_ref) + edge_ref[...]
    windowed(band, 0, rows, split_ref, scale_ref)
    edges = spectra_of(split_ref, scale_ref, dft_ref, rows)
    near = lax.broadcasted_iota(jnp.int32, edges.shape, 1) < HALO
    own = own_ref[...]
    first = jnp.where(near, edges, own[:, :rows])
    second = jnp.where(near, own[:, rows:], edges)
    spectra = jnp.concatenate([first, second], axis=1)
    width_group = 2 * GROUP
    across = LANES // width_group
    slot = lax.broadcasted_iota(jnp.int32, spectra.shape[1:], 1) // width_group
    for group in range(out_ref.shape[0]):
        for outer in range(out_ref.shape[1]):
            tile = jnp.zeros(spectra.shape[1:], f32)
            for inner in range(across):
                shift = (inner - group) * width_group % LANES
                value = spectra[outer * across + inner]
                if shift:
                    value = pltpu.roll(value, shift, 1)
                tile = jnp.where(slot == inner, value, tile)
            out_ref[group, outer] = tile.astype(bf16)


def left_kernel(own_ref, left_ref):
    parts, rows, _ = own_ref.shape
    lane = lax.broadcasted_iota(jnp.int32, (GROUP, LANES), 1)
    mask = lane % GROUP == lax.broadcasted_iota(jnp.int32, (GROUP, LANES), 0)
    real_lane = lax.broadcasted_iota(jnp.int32, (rows, LANES), 1) % (2 * GROUP) < GROUP

    for part in range(parts):
        value = own_ref[part].astype(f32)
        turned = jnp.where(real_lane, pltpu.roll(value, LANES - GROUP, 1), -pltpu.roll(value, GROUP, 1))
        for half, source in enumerate((value, turned)):
            spread = [jnp.where(mask, jnp.broadcast_to(source[c : c + 1], (GROUP, LANES)), 0.0) for c in range(rows)]
            left_ref[half, :, part * LANES : (part + 1) * LANES] = jnp.concatenate(spread, axis=0).astype(bf16)


def tile_kernel(scale, left_ref, *refs):
    partner_refs, out_ref = refs[:-1], refs[-1]
    parts, rows, _ = partner_refs[0].shape
    right = jnp.concatenate(
        [jnp.concatenate([ref[part] for part in range(parts)], axis=1) for ref in partner_refs], axis=0
    )
    real = dot_t(left_ref[0], right) * scale
    imag = dot_t(left_ref[1], right) * scale
    for c in range(rows):
        for s in range(len(partner_refs)):
            a = real[c * GROUP : (c + 1) * GROUP, s * rows : (s + 1) * rows]
            b = imag[c * GROUP : (c + 1) * GROUP, s * rows : (s + 1) * rows]
            out_ref[c, s] = jnp.concatenate([a, b], axis=1)


def call(kernel, out_shape, scratch=(), flops=0, bytes_accessed=0):
    return pl.pallas_call(
        kernel,
        out_shape=out_shape,
        scratch_shapes=list(scratch),
        compiler_params=pltpu.CompilerParams(vmem_limit_bytes=32 * 2**20),
        cost_estimate=pl.CostEstimate(flops=flops, bytes_accessed=bytes_accessed, transcendentals=0),
    )


def per_device(strain, fir_taps, spatial):
    rows, samples = strain.shape
    windows = samples // NFFT
    blocks = samples // LANES
    rep = lax.axis_size("rep")
    chan = lax.axis_size("chan")
    even = lax.axis_index("chan") % 2 == 0
    pairs_within = [(i, i ^ 1) for i in range(chan) if i ^ 1 < chan]
    pairs_across = [(i, j) for i in range(chan) for j in (i + 1 if i % 2 else i - 1,) if 0 <= j < chan]

    def rims(block):
        head, tail = block[:HALO], block[rows - HALO :]
        return jnp.where(even, tail, head), jnp.where(even, head, tail)

    history = lax.ppermute(strain[:, samples - LANES :], "rep", [(i, i + 1) for i in range(rep - 1)])
    now = lax.optimization_barrier(rims(strain))
    within, across = (jnp.concatenate(pair, axis=1) for pair in zip(rims(history), now))
    within, across, fir_taps, spatial = lax.optimization_barrier((within, across, fir_taps, spatial))
    near = lax.ppermute(within, "chan", pairs_within)
    far = lax.ppermute(across, "chan", pairs_across)

    filter_matrix = toeplitz(fir_taps)
    table = jnp.asarray(dft_table())
    mix = mixing(spatial, rows)
    own_mix = jnp.concatenate(rounded_halves(mix[:, HALO : HALO + rows]), axis=0)
    edge_rows = jnp.concatenate([mix[:HALO], mix[rows - HALO :]], axis=0)
    before_mix, after_mix = edge_rows[:, :HALO], edge_rows[:, HALO + rows :]
    edge_mix = jnp.concatenate([jnp.where(even, after_mix, before_mix), jnp.where(even, before_mix, after_mix)], axis=1)
    edge_mix = jnp.concatenate(rounded_halves(edge_mix), axis=0)

    edge, own = call(
        own_kernel,
        (jax.ShapeDtypeStruct((blocks, 2 * HALO, LANES), f32), jax.ShapeDtypeStruct((windows, rows, LANES), f32)),
        [
            pltpu.VMEM((2 * rows, LANES + samples), bf16),
            pltpu.VMEM((windows, 2 * rows, NFFT), bf16),
            pltpu.VMEM((windows, rows, LANES), f32),
        ],
        flops=2 * 2 * rows * samples * 512,
        bytes_accessed=4 * 2**20,
    )(strain, history, own_mix, filter_matrix, table)
    pieces = call(
        edge_kernel,
        jax.ShapeDtypeStruct((rep, windows * 2 * GROUP // LANES, rows, LANES), bf16),
        [
            pltpu.VMEM((4 * HALO, LANES + samples), bf16),
            pltpu.VMEM((windows, 4 * HALO, NFFT), bf16),
            pltpu.VMEM((windows, 2 * HALO, LANES), f32),
        ],
        flops=2 * 2 * rows * samples * 256,
        bytes_accessed=2 * 2**20,
    )(near, far, edge, own, edge_mix, filter_matrix, table)
    gathered = lax.all_to_all(pieces, "rep", split_axis=0, concat_axis=0, tiled=True)
    gathered = gathered.reshape(-1, rows, LANES)
    partners = [gathered]
    for step in range(1, STEPS + 1):
        partners.append(lax.ppermute(gathered, "chan", [((i + step) % chan, i) for i in range(chan)]))
    parts = gathered.shape[0]
    left = call(
        left_kernel,
        jax.ShapeDtypeStruct((2, rows * GROUP, parts * LANES), bf16),
        flops=2**20,
        bytes_accessed=2**20,
    )(gathered)
    scale = 1.0 / (windows * rep)
    return call(
        lambda *refs: tile_kernel(scale, *refs),
        jax.ShapeDtypeStruct((rows, STEPS + 1, BINS // rep, 2 * rows), f32),
        flops=2**24,
        bytes_accessed=2**20,
    )(left, *partners)


def solution(mesh):
    in_specs = (P("chan", "rep"), P(), P())
    out_specs = P("chan", None, "rep", None)
    return jax.shard_map(
        per_device, mesh=mesh, in_specs=in_specs, out_specs=out_specs, check_vma=False
    )
```

```python
import math

import jax
import jax.numpy as jnp
import numpy as np
from jax import lax
from jax.experimental import pallas as pl
from jax.experimental.pallas import tpu as pltpu
from jax.sharding import PartitionSpec as P

NFFT = 1024
BINS = 32
FIRST_BIN = 16
STEPS = 4
LANES = 128
HALO = 4
GROUP = 8

epsilon = 1e-05

f32 = jnp.float32
bf16 = jnp.bfloat16


def dot(a, b):
    return lax.dot_general(a, b, (((1,), (0,)), ((), ())), preferred_element_type=f32)


def dot_t(a, b):
    return lax.dot_general(a, b, (((1,), (1,)), ((), ())), preferred_element_type=f32)


def halves(values):
    high = values.astype(bf16)
    low = (values - high.astype(f32)).astype(bf16)
    return high, low


def dft_table():
    sample = np.arange(NFFT)[:, None]
    bins = FIRST_BIN + np.arange(BINS)[None, :]
    angle = (sample * bins % NFFT) * (2.0 * math.pi / NFFT)
    scale = 1.0 / math.sqrt(NFFT)
    real = (np.cos(angle) * scale).reshape(NFFT, BINS // GROUP, GROUP)
    imag = (-np.sin(angle) * scale).reshape(NFFT, BINS // GROUP, GROUP)
    table = np.concatenate([real, imag], axis=2).reshape(NFFT, 2 * BINS).astype(np.float32)
    high = table.astype(jnp.bfloat16)
    low = (table - high.astype(np.float32)).astype(jnp.bfloat16)
    return np.concatenate([high, low], axis=1)


def rounded_halves(values):
    high = lax.reduce_precision(values, exponent_bits=8, mantissa_bits=7)
    return high.astype(bf16), (values - high).astype(bf16)


def toeplitz(fir_taps):
    source = jnp.arange(2 * LANES, dtype=jnp.int32)[:, None]
    target = jnp.arange(LANES, dtype=jnp.int32)[None, :]
    lag = (target + LANES - source)[:, :, None]
    slots = jnp.arange(fir_taps.shape[0], dtype=jnp.int32)
    taps = jnp.sum(jnp.where(lag == slots, fir_taps, 0.0), axis=2)
    return jnp.concatenate(rounded_halves(taps), axis=1)


def mixing(spatial, rows):
    span = spatial.shape[0]
    offset = (jnp.arange(rows + span - 1, dtype=jnp.int32)[None, :] - jnp.arange(rows, dtype=jnp.int32)[:, None])[:, :, None]
    return jnp.sum(jnp.where(offset == jnp.arange(span, dtype=jnp.int32), spatial, 0.0), axis=2)


def filtered(mixed_ref, first, count, rows, toeplitz_ref):
    parts = []
    for block in range(count):
        start = pl.multiple_of((first + block) * LANES, LANES)
        parts.append(mixed_ref[:, pl.ds(start, 2 * LANES)])
    out = dot(jnp.concatenate(parts, axis=0), toeplitz_ref[...])
    out = out[:, :LANES] + out[:, LANES:]
    out = out.reshape(count, 2, rows, LANES)
    return out[:, 0] + out[:, 1]


def windowed(band, first_window, rows, split_ref, scale_ref):
    per = NFFT // LANES
    count = band.shape[0] // per
    squares = band * band
    for window in range(count):
        total = squares[window * per]
        for block in range(1, per):
            total = total + squares[window * per + block]
        power = jnp.sum(total, axis=1, keepdims=True) * (1.0 / NFFT)
        scale_ref[first_window + window] = jnp.broadcast_to(1.0 / jnp.sqrt(power + epsilon), (rows, LANES))
    high = band.astype(bf16).astype(f32)
    low = band - high
    both = jnp.concatenate([high, low], axis=1).astype(bf16)
    for window in range(count):
        for block in range(per):
            split_ref[first_window + window, :, block * LANES : (block + 1) * LANES] = both[window * per + block]


def spectra_of(split_ref, scale_ref, dft_ref, rows):
    windows = split_ref.shape[0]
    out = dot(split_ref[...].reshape(windows * 2 * rows, NFFT), dft_ref[...])
    out = out + pltpu.roll(out, LANES // 2, 1)
    out = out.reshape(windows, 2, rows, LANES)
    return (out[:, 0] + out[:, 1]) * scale_ref[...]


def own_kernel(strain_ref, history_ref, mix_ref, toeplitz_ref, dft_ref, edge_ref, spectra_ref, mixed_ref, split_ref, scale_ref):
    rows, samples = strain_ref.shape

    def mix(columns):
        out = dot(mix_ref[...], columns)
        high, low = halves(out[:rows] + out[rows:])
        return jnp.concatenate([high, low], axis=0)

    mixed_ref[:, :LANES] = mix(history_ref[...])
    step = samples // 2

    def mix_step(i, _):
        start = pl.multiple_of(i * step, step)
        mixed_ref[:, pl.ds(pl.multiple_of(start + LANES, LANES), step)] = mix(strain_ref[:, pl.ds(start, step)])
        return 0

    lax.fori_loop(0, samples // step, mix_step, 0)
    count = step // LANES
    near = lax.broadcasted_iota(jnp.int32, (count, rows // 2, LANES), 1) < HALO

    def filter_step(i, _):
        band = filtered(mixed_ref, i * count, count, rows, toeplitz_ref)
        edge_ref[pl.ds(i * count, count)] = jnp.where(near, band[:, : rows // 2], band[:, rows // 2 :])
        windowed(band, i * (step // NFFT), rows, split_ref, scale_ref)
        return 0

    lax.fori_loop(0, samples // step, filter_step, 0)
    spectra_ref[...] = spectra_of(split_ref, scale_ref, dft_ref, rows)


def edge_kernel(
    near_ref,
    far_ref,
    edge_ref,
    own_ref,
    mix_ref,
    toeplitz_ref,
    dft_ref,
    out_ref,
    mixed_ref,
    split_ref,
    scale_ref,
):
    rows = 2 * HALO
    step = near_ref.shape[1] - LANES

    def mix(near, far):
        both = jnp.concatenate([near.astype(f32), far.astype(f32)], axis=0).astype(bf16)
        out = dot(mix_ref[...], both)
        out = out[:rows] + out[rows:]
        high = out.astype(bf16).astype(f32)
        return jnp.concatenate([high, out - high], axis=0).astype(bf16)

    mixed_ref[...] = mix(near_ref[...], far_ref[...])
    band = filtered(mixed_ref, 0, step // LANES, rows, toeplitz_ref) + edge_ref[...]
    windowed(band, 0, rows, split_ref, scale_ref)
    edges = spectra_of(split_ref, scale_ref, dft_ref, rows)
    near = lax.broadcasted_iota(jnp.int32, edges.shape, 1) < HALO
    own = own_ref[...]
    first = jnp.where(near, edges, own[:, :rows])
    second = jnp.where(near, own[:, rows:], edges)
    spectra = jnp.concatenate([first, second], axis=1)
    width_group = 2 * GROUP
    across = LANES // width_group
    slot = lax.broadcasted_iota(jnp.int32, spectra.shape[1:], 1) // width_group
    groups = out_ref.shape[0]
    here = lax.axis_index("rep")
    for group in range(groups):
        place = jnp.bitwise_xor(group, here) if groups & (groups - 1) == 0 else lax.rem(group - here + groups, groups)
        for outer in range(out_ref.shape[1]):
            tile = jnp.zeros(spectra.shape[1:], f32)
            for inner in range(across):
                shift = (inner - group) * width_group % LANES
                value = spectra[outer * across + inner]
                if shift:
                    value = pltpu.roll(value, shift, 1)
                tile = jnp.where(slot == inner, value, tile)
            out_ref[place, outer] = tile.astype(bf16)


def left_kernel(own_ref, left_ref):
    parts, rows, _ = own_ref.shape
    lane = lax.broadcasted_iota(jnp.int32, (GROUP, LANES), 1)
    mask = lane % GROUP == lax.broadcasted_iota(jnp.int32, (GROUP, LANES), 0)
    real_lane = lax.broadcasted_iota(jnp.int32, (rows, LANES), 1) % (2 * GROUP) < GROUP

    for part in range(parts):
        value = own_ref[part].astype(f32)
        turned = jnp.where(real_lane, pltpu.roll(value, LANES - GROUP, 1), -pltpu.roll(value, GROUP, 1))
        for half, source in enumerate((value, turned)):
            spread = [jnp.where(mask, jnp.broadcast_to(source[c : c + 1], (GROUP, LANES)), 0.0) for c in range(rows)]
            left_ref[half, :, part * LANES : (part + 1) * LANES] = jnp.concatenate(spread, axis=0).astype(bf16)


def tile_kernel(scale, left_ref, *refs):
    partner_refs, out_ref = refs[:-1], refs[-1]
    parts, rows, _ = partner_refs[0].shape
    right = jnp.concatenate(
        [jnp.concatenate([ref[part] for part in range(parts)], axis=1) for ref in partner_refs], axis=0
    )
    real = dot_t(left_ref[0], right) * scale
    imag = dot_t(left_ref[1], right) * scale
    for c in range(rows):
        for s in range(len(partner_refs)):
            a = real[c * GROUP : (c + 1) * GROUP, s * rows : (s + 1) * rows]
            b = imag[c * GROUP : (c + 1) * GROUP, s * rows : (s + 1) * rows]
            out_ref[c, s] = jnp.concatenate([a, b], axis=1)


def call(kernel, out_shape, scratch=(), flops=0, bytes_accessed=0):
    return pl.pallas_call(
        kernel,
        out_shape=out_shape,
        scratch_shapes=list(scratch),
        compiler_params=pltpu.CompilerParams(vmem_limit_bytes=32 * 2**20),
        cost_estimate=pl.CostEstimate(flops=flops, bytes_accessed=bytes_accessed, transcendentals=0),
    )


def per_device(strain, fir_taps, spatial):
    rows, samples = strain.shape
    windows = samples // NFFT
    blocks = samples // LANES
    rep = lax.axis_size("rep")
    chan = lax.axis_size("chan")
    even = lax.axis_index("chan") % 2 == 0
    pairs_within = [(i, i ^ 1) for i in range(chan) if i ^ 1 < chan]
    pairs_across = [(i, j) for i in range(chan) for j in (i + 1 if i % 2 else i - 1,) if 0 <= j < chan]

    def rims(block):
        head, tail = block[:HALO], block[rows - HALO :]
        return jnp.where(even, tail, head), jnp.where(even, head, tail)

    history = lax.ppermute(strain[:, samples - LANES :], "rep", [(i, i + 1) for i in range(rep - 1)])
    now = lax.optimization_barrier(rims(strain))
    within, across = (jnp.concatenate(pair, axis=1) for pair in zip(rims(history), now))
    within, across, fir_taps, spatial = lax.optimization_barrier((within, across, fir_taps, spatial))
    near = lax.ppermute(within, "chan", pairs_within)
    far = lax.ppermute(across, "chan", pairs_across)

    filter_matrix = toeplitz(fir_taps)
    table = jnp.asarray(dft_table())
    mix = mixing(spatial, rows)
    own_mix = jnp.concatenate(rounded_halves(mix[:, HALO : HALO + rows]), axis=0)
    edge_rows = jnp.concatenate([mix[:HALO], mix[rows - HALO :]], axis=0)
    before_mix, after_mix = edge_rows[:, :HALO], edge_rows[:, HALO + rows :]
    edge_mix = jnp.concatenate([jnp.where(even, after_mix, before_mix), jnp.where(even, before_mix, after_mix)], axis=1)
    edge_mix = jnp.concatenate(rounded_halves(edge_mix), axis=0)

    edge, own = call(
        own_kernel,
        (jax.ShapeDtypeStruct((blocks, 2 * HALO, LANES), f32), jax.ShapeDtypeStruct((windows, rows, LANES), f32)),
        [
            pltpu.VMEM((2 * rows, LANES + samples), bf16),
            pltpu.VMEM((windows, 2 * rows, NFFT), bf16),
            pltpu.VMEM((windows, rows, LANES), f32),
        ],
        flops=2 * 2 * rows * samples * 512,
        bytes_accessed=4 * 2**20,
    )(strain, history, own_mix, filter_matrix, table)
    pieces = call(
        edge_kernel,
        jax.ShapeDtypeStruct((rep, windows * 2 * GROUP // LANES, rows, LANES), bf16),
        [
            pltpu.VMEM((4 * HALO, LANES + samples), bf16),
            pltpu.VMEM((windows, 4 * HALO, NFFT), bf16),
            pltpu.VMEM((windows, 2 * HALO, LANES), f32),
        ],
        flops=2 * 2 * rows * samples * 256,
        bytes_accessed=2 * 2**20,
    )(near, far, edge, own, edge_mix, filter_matrix, table)
    arrived = [pieces[0]]
    for step in range(1, rep):
        to = [(i, i ^ step if rep & (rep - 1) == 0 else (i + step) % rep) for i in range(rep)]
        arrived.append(lax.ppermute(pieces[step], "rep", to))
    gathered = jnp.concatenate(arrived, axis=0)
    partners = [gathered]
    for step in range(1, STEPS + 1):
        partners.append(lax.ppermute(gathered, "chan", [((i + step) % chan, i) for i in range(chan)]))
    parts = gathered.shape[0]
    left = call(
        left_kernel,
        jax.ShapeDtypeStruct((2, rows * GROUP, parts * LANES), bf16),
        flops=2**20,
        bytes_accessed=2**20,
    )(gathered)
    scale = 1.0 / (windows * rep)
    return call(
        lambda *refs: tile_kernel(scale, *refs),
        jax.ShapeDtypeStruct((rows, STEPS + 1, BINS // rep, 2 * rows), f32),
        flops=2**24,
        bytes_accessed=2**20,
    )(left, *partners)


def solution(mesh):
    in_specs = (P("chan", "rep"), P(), P())
    out_specs = P("chan", None, "rep", None)
    return jax.shard_map(
        per_device, mesh=mesh, in_specs=in_specs, out_specs=out_specs, check_vma=False
    )
```

```python
import math

import jax
import jax.numpy as jnp
import numpy as np
from jax import lax
from jax.experimental import pallas as pl
from jax.experimental.pallas import tpu as pltpu
from jax.sharding import PartitionSpec as P

NFFT = 1024
BINS = 32
FIRST_BIN = 16
STEPS = 4
LANES = 128
HALO = 4
GROUP = 8

epsilon = 1e-05

f32 = jnp.float32
bf16 = jnp.bfloat16


def dot(a, b):
    return lax.dot_general(a, b, (((1,), (0,)), ((), ())), preferred_element_type=f32)


def dot_t(a, b):
    return lax.dot_general(a, b, (((1,), (1,)), ((), ())), preferred_element_type=f32)


def halves(values):
    high = values.astype(bf16)
    low = (values - high.astype(f32)).astype(bf16)
    return high, low


def dft_table():
    sample = np.arange(NFFT)[:, None]
    bins = FIRST_BIN + np.arange(BINS)[None, :]
    angle = (sample * bins % NFFT) * (2.0 * math.pi / NFFT)
    scale = 1.0 / math.sqrt(NFFT)
    real = (np.cos(angle) * scale).reshape(NFFT, BINS // GROUP, GROUP)
    imag = (-np.sin(angle) * scale).reshape(NFFT, BINS // GROUP, GROUP)
    table = np.concatenate([real, imag], axis=2).reshape(NFFT, 2 * BINS).astype(np.float32)
    high = table.astype(jnp.bfloat16)
    low = (table - high.astype(np.float32)).astype(jnp.bfloat16)
    return np.concatenate([high, low], axis=1)


def toeplitz(taps_ref):
    lane = lax.broadcasted_iota(jnp.int32, (LANES, LANES), 1)
    row = lax.broadcasted_iota(jnp.int32, (LANES, LANES), 0)
    taps = jnp.zeros((1, LANES), f32)
    for k in range(taps_ref.shape[0]):
        taps = jnp.where(lane[:1] == k, taps_ref[k], taps)
    turned = pltpu.roll(jnp.broadcast_to(taps, (LANES, LANES)), 0, 1, stride=1, stride_axis=0)
    parts = [jnp.where(lane < row, turned, 0.0), jnp.where(lane >= row, turned, 0.0)]
    return jnp.concatenate(halves(jnp.concatenate(parts, axis=0)), axis=1)


def mixing(spatial_ref, lag):
    weight = jnp.zeros(lag.shape, f32)
    for j in range(spatial_ref.shape[0]):
        weight = jnp.where(lag == j, spatial_ref[j], weight)
    high = weight.astype(bf16).astype(f32)
    return jnp.concatenate([high, weight - high], axis=0).astype(bf16)


def edge_lags(count):
    shape = (2 * HALO, 2 * HALO)
    target = lax.broadcasted_iota(jnp.int32, shape, 0)
    target = jnp.where(target < HALO, target, target + count - 2 * HALO)
    source = lax.broadcasted_iota(jnp.int32, shape, 1)
    before = (source < HALO) == (lax.axis_index("chan") % 2 != 0)
    return source % HALO + jnp.where(before, 0, count + HALO) - target


def filtered(mixed_ref, first, count, rows, toeplitz_ref):
    parts = []
    for block in range(count):
        start = pl.multiple_of((first + block) * LANES, LANES)
        parts.append(mixed_ref[:, pl.ds(start, 2 * LANES)])
    out = dot(jnp.concatenate(parts, axis=0), toeplitz_ref[...])
    out = out[:, :LANES] + out[:, LANES:]
    out = out.reshape(count, 2, rows, LANES)
    return out[:, 0] + out[:, 1]


def windowed(band, first_window, rows, split_ref, scale_ref):
    per = NFFT // LANES
    count = band.shape[0] // per
    squares = band * band
    for window in range(count):
        total = squares[window * per]
        for block in range(1, per):
            total = total + squares[window * per + block]
        power = jnp.sum(total, axis=1, keepdims=True) * (1.0 / NFFT)
        scale_ref[first_window + window] = jnp.broadcast_to(1.0 / jnp.sqrt(power + epsilon), (rows, LANES))
    high = band.astype(bf16).astype(f32)
    low = band - high
    both = jnp.concatenate([high, low], axis=1).astype(bf16)
    for window in range(count):
        for block in range(per):
            split_ref[first_window + window, :, block * LANES : (block + 1) * LANES] = both[window * per + block]


def spectra_of(split_ref, scale_ref, dft_ref, rows):
    windows = split_ref.shape[0]
    out = dot(split_ref[...].reshape(windows * 2 * rows, NFFT), dft_ref[...])
    out = out + pltpu.roll(out, LANES // 2, 1)
    out = out.reshape(windows, 2, rows, LANES)
    return (out[:, 0] + out[:, 1]) * scale_ref[...]


def own_kernel(
    strain_ref,
    history_ref,
    taps_ref,
    spatial_ref,
    dft_ref,
    edge_ref,
    spectra_ref,
    toeplitz_ref,
    edge_mix_ref,
    mixed_ref,
    split_ref,
    scale_ref,
):
    rows, samples = strain_ref.shape
    source = lax.broadcasted_iota(jnp.int32, (rows, rows), 1)
    weights = mixing(spatial_ref, source + HALO - lax.broadcasted_iota(jnp.int32, (rows, rows), 0))
    toeplitz_ref[...] = toeplitz(taps_ref)
    edge_mix_ref[...] = mixing(spatial_ref, edge_lags(rows))

    def mix(columns):
        out = dot(weights, columns)
        high, low = halves(out[:rows] + out[rows:])
        return jnp.concatenate([high, low], axis=0)

    mixed_ref[:, :LANES] = mix(history_ref[...])
    step = samples // 2

    def mix_step(i, _):
        start = pl.multiple_of(i * step, step)
        mixed_ref[:, pl.ds(pl.multiple_of(start + LANES, LANES), step)] = mix(strain_ref[:, pl.ds(start, step)])
        return 0

    lax.fori_loop(0, samples // step, mix_step, 0)
    count = step // LANES
    near = lax.broadcasted_iota(jnp.int32, (count, rows // 2, LANES), 1) < HALO

    def filter_step(i, _):
        band = filtered(mixed_ref, i * count, count, rows, toeplitz_ref)
        edge_ref[pl.ds(i * count, count)] = jnp.where(near, band[:, : rows // 2], band[:, rows // 2 :])
        windowed(band, i * (step // NFFT), rows, split_ref, scale_ref)
        return 0

    lax.fori_loop(0, samples // step, filter_step, 0)
    spectra_ref[...] = spectra_of(split_ref, scale_ref, dft_ref, rows)


def edge_kernel(
    near_ref,
    far_ref,
    edge_ref,
    own_ref,
    mix_ref,
    toeplitz_ref,
    dft_ref,
    out_ref,
    mixed_ref,
    split_ref,
    scale_ref,
):
    rows = 2 * HALO
    step = near_ref.shape[1] - LANES
    weights = mix_ref[...]

    def mix(near, far):
        both = jnp.concatenate([near.astype(f32), far.astype(f32)], axis=0).astype(bf16)
        out = dot(weights, both)
        out = out[:rows] + out[rows:]
        high = out.astype(bf16).astype(f32)
        return jnp.concatenate([high, out - high], axis=0).astype(bf16)

    mixed_ref[...] = mix(near_ref[...], far_ref[...])
    band = filtered(mixed_ref, 0, step // LANES, rows, toeplitz_ref) + edge_ref[...]
    windowed(band, 0, rows, split_ref, scale_ref)
    edges = spectra_of(split_ref, scale_ref, dft_ref, rows)
    near = lax.broadcasted_iota(jnp.int32, edges.shape, 1) < HALO
    own = own_ref[...]
    first = jnp.where(near, edges, own[:, :rows])
    second = jnp.where(near, own[:, rows:], edges)
    spectra = jnp.concatenate([first, second], axis=1)
    width_group = 2 * GROUP
    across = LANES // width_group
    slot = lax.broadcasted_iota(jnp.int32, spectra.shape[1:], 1) // width_group
    groups = out_ref.shape[0]
    here = lax.axis_index("rep")
    for group in range(groups):
        place = jnp.bitwise_xor(group, here) if groups & (groups - 1) == 0 else lax.rem(group - here + groups, groups)
        for outer in range(out_ref.shape[1]):
            tile = jnp.zeros(spectra.shape[1:], f32)
            for inner in range(across):
                shift = (inner - group) * width_group % LANES
                value = spectra[outer * across + inner]
                if shift:
                    value = pltpu.roll(value, shift, 1)
                tile = jnp.where(slot == inner, value, tile)
            out_ref[place, outer] = tile.astype(bf16)


def rim_kernel(strain_ref, within_ref, across_ref, last_ref):
    rows, samples = strain_ref.shape
    even = lax.axis_index("chan") % 2 == 0
    head, tail = strain_ref[:HALO], strain_ref[rows - HALO :]
    within_ref[...] = jnp.where(even, tail, head)
    across_ref[...] = jnp.where(even, head, tail)
    last_ref[...] = strain_ref[:, samples - LANES :]


def prefix_kernel(history_ref, within_ref, across_ref, near_ref, far_ref):
    rows = history_ref.shape[0]
    even = lax.axis_index("chan") % 2 == 0
    head, tail = history_ref[:HALO], history_ref[rows - HALO :]
    near_ref[:, :LANES] = jnp.where(even, tail, head)
    near_ref[:, LANES:] = within_ref[...]
    far_ref[:, :LANES] = jnp.where(even, head, tail)
    far_ref[:, LANES:] = across_ref[...]


def left_kernel(own_ref, left_ref):
    parts, rows, _ = own_ref.shape
    lane = lax.broadcasted_iota(jnp.int32, (GROUP, LANES), 1)
    mask = lane % GROUP == lax.broadcasted_iota(jnp.int32, (GROUP, LANES), 0)
    real_lane = lax.broadcasted_iota(jnp.int32, (rows, LANES), 1) % (2 * GROUP) < GROUP

    for part in range(parts):
        value = own_ref[part].astype(f32)
        turned = jnp.where(real_lane, pltpu.roll(value, LANES - GROUP, 1), -pltpu.roll(value, GROUP, 1))
        for half, source in enumerate((value, turned)):
            spread = [jnp.where(mask, jnp.broadcast_to(source[c : c + 1], (GROUP, LANES)), 0.0) for c in range(rows)]
            left_ref[half, :, part * LANES : (part + 1) * LANES] = jnp.concatenate(spread, axis=0).astype(bf16)


def tile_kernel(scale, left_ref, *refs):
    partner_refs, out_ref = refs[:-1], refs[-1]
    parts, rows, _ = partner_refs[0].shape
    right = jnp.concatenate(
        [jnp.concatenate([ref[part] for part in range(parts)], axis=1) for ref in partner_refs], axis=0
    )
    real = dot_t(left_ref[0], right) * scale
    imag = dot_t(left_ref[1], right) * scale
    for c in range(rows):
        for s in range(len(partner_refs)):
            a = real[c * GROUP : (c + 1) * GROUP, s * rows : (s + 1) * rows]
            b = imag[c * GROUP : (c + 1) * GROUP, s * rows : (s + 1) * rows]
            out_ref[c, s] = jnp.concatenate([a, b], axis=1)


def call(kernel, out_shape, scratch=(), flops=0, bytes_accessed=0, places="v"):
    whole = {"v": pl.BlockSpec(memory_space=pltpu.VMEM), "s": pl.BlockSpec(memory_space=pltpu.SMEM)}
    return pl.pallas_call(
        kernel,
        out_shape=out_shape,
        in_specs=[whole[place] for place in places],
        scratch_shapes=list(scratch),
        compiler_params=pltpu.CompilerParams(vmem_limit_bytes=32 * 2**20),
        cost_estimate=pl.CostEstimate(flops=flops, bytes_accessed=bytes_accessed, transcendentals=0),
    )


def per_device(strain, fir_taps, spatial):
    rows, samples = strain.shape
    windows = samples // NFFT
    blocks = samples // LANES
    rep = lax.axis_size("rep")
    chan = lax.axis_size("chan")
    even = lax.axis_index("chan") % 2 == 0
    pairs_within = [(i, i ^ 1) for i in range(chan) if i ^ 1 < chan]
    pairs_across = [(i, j) for i in range(chan) for j in (i + 1 if i % 2 else i - 1,) if 0 <= j < chan]

    rim = jax.ShapeDtypeStruct((HALO, samples), bf16)
    last = jax.ShapeDtypeStruct((rows, LANES), bf16)
    within, across, last = call(rim_kernel, [rim, rim, last], bytes_accessed=2**20)(strain)
    history = lax.ppermute(last, "rep", [(i, i + 1) for i in range(rep - 1)])
    rim = jax.ShapeDtypeStruct((HALO, LANES + samples), bf16)
    within, across = call(prefix_kernel, [rim, rim], bytes_accessed=2**20, places="vvv")(history, within, across)
    near = lax.ppermute(within, "chan", pairs_within)
    far = lax.ppermute(across, "chan", pairs_across)

    table = jnp.asarray(dft_table())
    edge, own, filter_matrix, edge_mix = call(
        own_kernel,
        [
            jax.ShapeDtypeStruct((blocks, 2 * HALO, LANES), f32),
            jax.ShapeDtypeStruct((windows, rows, LANES), f32),
            jax.ShapeDtypeStruct((2 * LANES, 2 * LANES), bf16),
            jax.ShapeDtypeStruct((4 * HALO, 2 * HALO), bf16),
        ],
        [
            pltpu.VMEM((2 * rows, LANES + samples), bf16),
            pltpu.VMEM((windows, 2 * rows, NFFT), bf16),
            pltpu.VMEM((windows, rows, LANES), f32),
        ],
        flops=2 * 2 * rows * samples * 512,
        bytes_accessed=4 * 2**20,
        places="vvssv",
    )(strain, history, fir_taps, spatial, table)
    pieces = call(
        edge_kernel,
        jax.ShapeDtypeStruct((rep, windows * 2 * GROUP // LANES, rows, LANES), bf16),
        [
            pltpu.VMEM((4 * HALO, LANES + samples), bf16),
            pltpu.VMEM((windows, 4 * HALO, NFFT), bf16),
            pltpu.VMEM((windows, 2 * HALO, LANES), f32),
        ],
        flops=2 * 2 * rows * samples * 256,
        bytes_accessed=2 * 2**20,
        places="v" * 7,
    )(near, far, edge, own, edge_mix, filter_matrix, table)
    arrived = [pieces[0]]
    for step in range(1, rep):
        to = [(i, i ^ step if rep & (rep - 1) == 0 else (i + step) % rep) for i in range(rep)]
        arrived.append(lax.ppermute(pieces[step], "rep", to))
    gathered = jnp.concatenate(arrived, axis=0)
    partners = [gathered]
    for step in range(1, STEPS + 1):
        partners.append(lax.ppermute(gathered, "chan", [((i + step) % chan, i) for i in range(chan)]))
    parts = gathered.shape[0]
    left = call(
        left_kernel,
        jax.ShapeDtypeStruct((2, rows * GROUP, parts * LANES), bf16),
        flops=2**20,
        bytes_accessed=2**20,
    )(gathered)
    scale = 1.0 / (windows * rep)
    return call(
        lambda *refs: tile_kernel(scale, *refs),
        jax.ShapeDtypeStruct((rows, STEPS + 1, BINS // rep, 2 * rows), f32),
        flops=2**24,
        bytes_accessed=2**20,
        places="v" * (STEPS + 2),
    )(left, *partners)


def solution(mesh):
    in_specs = (P("chan", "rep"), P(), P())
    out_specs = P("chan", None, "rep", None)
    return jax.shard_map(
        per_device, mesh=mesh, in_specs=in_specs, out_specs=out_specs, check_vma=False
    )
```

```python
import math

import jax
import jax.numpy as jnp
import numpy as np
from jax import lax
from jax.experimental import pallas as pl
from jax.experimental.pallas import tpu as pltpu
from jax.sharding import PartitionSpec as P

NFFT = 1024
BINS = 32
FIRST_BIN = 16
STEPS = 4
LANES = 128
HALO = 4
GROUP = 8

epsilon = 1e-05

f32 = jnp.float32
bf16 = jnp.bfloat16


def dot(a, b):
    return lax.dot_general(a, b, (((1,), (0,)), ((), ())), preferred_element_type=f32)


def dot_t(a, b):
    return lax.dot_general(a, b, (((1,), (1,)), ((), ())), preferred_element_type=f32)


def halves(values):
    high = values.astype(bf16)
    low = (values - high.astype(f32)).astype(bf16)
    return high, low


def dft_table():
    sample = np.arange(NFFT)[:, None]
    bins = FIRST_BIN + np.arange(BINS)[None, :]
    angle = (sample * bins % NFFT) * (2.0 * math.pi / NFFT)
    scale = 1.0 / math.sqrt(NFFT)
    real = (np.cos(angle) * scale).reshape(NFFT, BINS // GROUP, GROUP)
    imag = (-np.sin(angle) * scale).reshape(NFFT, BINS // GROUP, GROUP)
    table = np.concatenate([real, imag], axis=2).reshape(NFFT, 2 * BINS).astype(np.float32)
    high = table.astype(jnp.bfloat16)
    low = (table - high.astype(np.float32)).astype(jnp.bfloat16)
    return np.concatenate([high, low], axis=1)


def toeplitz(taps_ref):
    lane = lax.broadcasted_iota(jnp.int32, (LANES, LANES), 1)
    row = lax.broadcasted_iota(jnp.int32, (LANES, LANES), 0)
    taps = jnp.zeros((1, LANES), f32)
    for k in range(taps_ref.shape[0]):
        taps = jnp.where(lane[:1] == k, taps_ref[k], taps)
    turned = pltpu.roll(jnp.broadcast_to(taps, (LANES, LANES)), 0, 1, stride=1, stride_axis=0)
    parts = [jnp.where(lane < row, turned, 0.0), jnp.where(lane >= row, turned, 0.0)]
    return jnp.concatenate(halves(jnp.concatenate(parts, axis=0)), axis=1)


def mixing(spatial_ref, lag):
    weight = jnp.zeros(lag.shape, f32)
    for j in range(spatial_ref.shape[0]):
        weight = jnp.where(lag == j, spatial_ref[j], weight)
    high = weight.astype(bf16).astype(f32)
    return jnp.concatenate([high, weight - high], axis=0).astype(bf16)


def received_row(source, count):
    before = (source < HALO) == (lax.axis_index("chan") % 2 != 0)
    return source % HALO + jnp.where(before, -HALO, count)


def edge_lags(count):
    shape = (2 * HALO, 2 * HALO)
    target = lax.broadcasted_iota(jnp.int32, shape, 0)
    target = jnp.where(target < HALO, target, target + count - 2 * HALO)
    return received_row(lax.broadcasted_iota(jnp.int32, shape, 1), count) + HALO - target


def tail_lags(count):
    shape = (count, 2 * count)
    source = lax.broadcasted_iota(jnp.int32, shape, 1)
    row = jnp.where(source < count, source, received_row(source - count, count))
    lag = row + HALO - lax.broadcasted_iota(jnp.int32, shape, 0)
    return jnp.where(source < count + 2 * HALO, lag, -1)


def filtered(mixed_ref, first, count, rows, toeplitz_ref):
    parts = []
    for block in range(count):
        start = pl.multiple_of((first + block) * LANES, LANES)
        parts.append(mixed_ref[:, pl.ds(start, 2 * LANES)])
    out = dot(jnp.concatenate(parts, axis=0), toeplitz_ref[...])
    out = out[:, :LANES] + out[:, LANES:]
    out = out.reshape(count, 2, rows, LANES)
    return out[:, 0] + out[:, 1]


def windowed(band, first_window, rows, split_ref, scale_ref):
    per = NFFT // LANES
    count = band.shape[0] // per
    squares = band * band
    for window in range(count):
        total = squares[window * per]
        for block in range(1, per):
            total = total + squares[window * per + block]
        power = jnp.sum(total, axis=1, keepdims=True) * (1.0 / NFFT)
        scale_ref[first_window + window] = jnp.broadcast_to(1.0 / jnp.sqrt(power + epsilon), (rows, LANES))
    high = band.astype(bf16).astype(f32)
    low = band - high
    both = jnp.concatenate([high, low], axis=1).astype(bf16)
    for window in range(count):
        for block in range(per):
            split_ref[first_window + window, :, block * LANES : (block + 1) * LANES] = both[window * per + block]


def spectra_of(split_ref, scale_ref, dft_ref, rows):
    windows = split_ref.shape[0]
    out = dot(split_ref[...].reshape(windows * 2 * rows, NFFT), dft_ref[...])
    out = out + pltpu.roll(out, LANES // 2, 1)
    out = out.reshape(windows, 2, rows, LANES)
    return (out[:, 0] + out[:, 1]) * scale_ref[...]


def own_kernel(
    strain_ref,
    taps_ref,
    spatial_ref,
    dft_ref,
    edge_ref,
    spectra_ref,
    first_ref,
    toeplitz_ref,
    edge_mix_ref,
    tail_mix_ref,
    mixed_ref,
    split_ref,
    scale_ref,
):
    rows, samples = strain_ref.shape
    source = lax.broadcasted_iota(jnp.int32, (rows, rows), 1)
    weights = mixing(spatial_ref, source + HALO - lax.broadcasted_iota(jnp.int32, (rows, rows), 0))
    toeplitz_ref[...] = toeplitz(taps_ref)
    edge_mix_ref[...] = mixing(spatial_ref, edge_lags(rows))
    tail_mix_ref[...] = mixing(spatial_ref, tail_lags(rows))

    def mix(columns):
        out = dot(weights, columns)
        high, low = halves(out[:rows] + out[rows:])
        return jnp.concatenate([high, low], axis=0)

    mixed_ref[:, :LANES] = jnp.zeros((2 * rows, LANES), bf16)
    step = samples // 2

    def mix_step(i, _):
        start = pl.multiple_of(i * step, step)
        mixed_ref[:, pl.ds(pl.multiple_of(start + LANES, LANES), step)] = mix(strain_ref[:, pl.ds(start, step)])
        return 0

    lax.fori_loop(0, samples // step, mix_step, 0)
    count = step // LANES
    near = lax.broadcasted_iota(jnp.int32, (count, rows // 2, LANES), 1) < HALO

    def filter_step(i, _):
        band = filtered(mixed_ref, i * count, count, rows, toeplitz_ref)
        edge_ref[pl.ds(i * count, count)] = jnp.where(near, band[:, : rows // 2], band[:, rows // 2 :])
        windowed(band, i * (step // NFFT), rows, split_ref, scale_ref)

        @pl.when(i == 0)
        def _():
            first_ref[...] = band[: NFFT // LANES]

        return 0

    lax.fori_loop(0, samples // step, filter_step, 0)
    spectra_ref[...] = spectra_of(split_ref, scale_ref, dft_ref, rows)


def whole_block(edges, own):
    rows = edges.shape[1]
    near = lax.broadcasted_iota(jnp.int32, edges.shape, 1) < HALO
    return jnp.concatenate([jnp.where(near, edges, own[:, :rows]), jnp.where(near, own[:, rows:], edges)], axis=1)


def place_of(group, groups):
    here = lax.axis_index("rep")
    return jnp.bitwise_xor(group, here) if groups & (groups - 1) == 0 else lax.rem(group - here + groups, groups)


def edge_kernel(
    near_ref,
    far_ref,
    edge_ref,
    own_ref,
    mix_ref,
    toeplitz_ref,
    dft_ref,
    out_ref,
    first_ref,
    mixed_ref,
    split_ref,
    scale_ref,
):
    rows = 2 * HALO
    step = near_ref.shape[1]
    weights = mix_ref[...]

    def mix(near, far):
        both = jnp.concatenate([near.astype(f32), far.astype(f32)], axis=0).astype(bf16)
        out = dot(weights, both)
        out = out[:rows] + out[rows:]
        high = out.astype(bf16).astype(f32)
        return jnp.concatenate([high, out - high], axis=0).astype(bf16)

    mixed_ref[:, :LANES] = jnp.zeros((2 * rows, LANES), bf16)
    mixed_ref[:, LANES:] = mix(near_ref[...], far_ref[...])
    band = filtered(mixed_ref, 0, step // LANES, rows, toeplitz_ref) + edge_ref[...]
    first_ref[...] = band[: NFFT // LANES]
    windowed(band, 0, rows, split_ref, scale_ref)
    edges = spectra_of(split_ref, scale_ref, dft_ref, rows)
    spectra = whole_block(edges, own_ref[...])
    width_group = 2 * GROUP
    across = LANES // width_group
    slot = lax.broadcasted_iota(jnp.int32, spectra.shape[1:], 1) // width_group
    groups = out_ref.shape[0]
    for group in range(groups):
        place = place_of(group, groups)
        for outer in range(out_ref.shape[1]):
            tile = jnp.zeros(spectra.shape[1:], f32)
            for inner in range(across):
                shift = (inner - group) * width_group % LANES
                value = spectra[outer * across + inner]
                if shift:
                    value = pltpu.roll(value, shift, 1)
                tile = jnp.where(slot == inner, value, tile)
            out_ref[place, outer] = tile.astype(bf16)


def first_kernel(
    odd_ref, even_ref, mix_ref, toeplitz_ref, dft_ref, own_ref, edge_ref, pieces_ref, out_ref, split_ref, scale_ref
):
    rows = own_ref.shape[1]
    here = lax.axis_index("rep")
    tail = jnp.where(here % 2 == 1, odd_ref[...], even_ref[...])
    mixed = dot(mix_ref[...], jnp.where(here == 0, jnp.zeros_like(tail), tail))
    mixed = jnp.concatenate(halves(mixed[:rows] + mixed[rows:]), axis=0)
    spill = dot(mixed, toeplitz_ref[:LANES, :])
    spill = spill[:, :LANES] + spill[:, LANES:]
    spill = spill[:rows] + spill[rows:]
    band = whole_block(edge_ref[...], own_ref[...])
    first = lax.broadcasted_iota(jnp.int32, band.shape, 0) == 0
    windowed(jnp.where(first, band + spill, band), 0, rows, split_ref, scale_ref)
    spectra = spectra_of(split_ref, scale_ref, dft_ref, rows)[0]
    width_group = 2 * GROUP
    groups = out_ref.shape[0]
    out_ref[...] = pieces_ref[...]
    here = lax.broadcasted_iota(jnp.int32, spectra.shape, 1) < width_group
    for group in range(groups):
        place = place_of(group, groups)
        value = pltpu.roll(spectra, LANES - group * width_group, 1) if group else spectra
        out_ref[place, 0] = jnp.where(here, value, pieces_ref[place, 0].astype(f32)).astype(bf16)


def rim_kernel(strain_ref, within_ref, across_ref):
    rows = strain_ref.shape[0]
    even = lax.axis_index("chan") % 2 == 0
    head, tail = strain_ref[:HALO], strain_ref[rows - HALO :]
    within_ref[...] = jnp.where(even, tail, head)
    across_ref[...] = jnp.where(even, head, tail)


def tail_kernel(strain_ref, near_ref, far_ref, tail_ref):
    rows, samples = strain_ref.shape
    last = slice(samples - LANES, samples)
    received = [near_ref[:, last].astype(f32), far_ref[:, last].astype(f32), jnp.zeros((rows - 2 * HALO, LANES), f32)]
    tail_ref[:rows] = strain_ref[:, last]
    tail_ref[rows:] = jnp.concatenate(received, axis=0).astype(bf16)


def left_kernel(own_ref, left_ref):
    parts, rows, _ = own_ref.shape
    lane = lax.broadcasted_iota(jnp.int32, (GROUP, LANES), 1)
    mask = lane % GROUP == lax.broadcasted_iota(jnp.int32, (GROUP, LANES), 0)
    real_lane = lax.broadcasted_iota(jnp.int32, (rows, LANES), 1) % (2 * GROUP) < GROUP

    for part in range(parts):
        value = own_ref[part].astype(f32)
        turned = jnp.where(real_lane, pltpu.roll(value, LANES - GROUP, 1), -pltpu.roll(value, GROUP, 1))
        for half, source in enumerate((value, turned)):
            spread = [jnp.where(mask, jnp.broadcast_to(source[c : c + 1], (GROUP, LANES)), 0.0) for c in range(rows)]
            left_ref[half, :, part * LANES : (part + 1) * LANES] = jnp.concatenate(spread, axis=0).astype(bf16)


def tile_kernel(scale, left_ref, *refs):
    partner_refs, out_ref = refs[-2::-1], refs[-1]
    parts, rows, _ = partner_refs[0].shape
    right = jnp.concatenate(
        [jnp.concatenate([ref[part] for part in range(parts)], axis=1) for ref in partner_refs], axis=0
    )
    real = dot_t(left_ref[0], right) * scale
    imag = dot_t(left_ref[1], right) * scale
    for c in range(rows):
        for s in range(len(partner_refs)):
            a = real[c * GROUP : (c + 1) * GROUP, s * rows : (s + 1) * rows]
            b = imag[c * GROUP : (c + 1) * GROUP, s * rows : (s + 1) * rows]
            out_ref[c, s] = jnp.concatenate([a, b], axis=1)


def call(kernel, out_shape, scratch=(), flops=0, bytes_accessed=0, places="v"):
    whole = {"v": pl.BlockSpec(memory_space=pltpu.VMEM), "s": pl.BlockSpec(memory_space=pltpu.SMEM)}
    return pl.pallas_call(
        kernel,
        out_shape=out_shape,
        in_specs=[whole[place] for place in places],
        scratch_shapes=list(scratch),
        compiler_params=pltpu.CompilerParams(vmem_limit_bytes=32 * 2**20),
        cost_estimate=pl.CostEstimate(flops=flops, bytes_accessed=bytes_accessed, transcendentals=0),
    )


def per_device(strain, fir_taps, spatial):
    rows, samples = strain.shape
    windows = samples // NFFT
    blocks = samples // LANES
    rep = lax.axis_size("rep")
    chan = lax.axis_size("chan")
    even = lax.axis_index("chan") % 2 == 0
    pairs_within = [(i, i ^ 1) for i in range(chan) if i ^ 1 < chan]
    pairs_across = [(i, j) for i in range(chan) for j in (i + 1 if i % 2 else i - 1,) if 0 <= j < chan]

    rim = jax.ShapeDtypeStruct((HALO, samples), bf16)
    within, across = call(rim_kernel, [rim, rim], bytes_accessed=2**20)(strain)
    near = lax.ppermute(within, "chan", pairs_within)
    far = lax.ppermute(across, "chan", pairs_across)

    table = jnp.asarray(dft_table())
    edge, own, own_first, filter_matrix, edge_mix, tail_mix = call(
        own_kernel,
        [
            jax.ShapeDtypeStruct((blocks, 2 * HALO, LANES), f32),
            jax.ShapeDtypeStruct((windows, rows, LANES), f32),
            jax.ShapeDtypeStruct((NFFT // LANES, rows, LANES), f32),
            jax.ShapeDtypeStruct((2 * LANES, 2 * LANES), bf16),
            jax.ShapeDtypeStruct((4 * HALO, 2 * HALO), bf16),
            jax.ShapeDtypeStruct((2 * rows, 2 * rows), bf16),
        ],
        [
            pltpu.VMEM((2 * rows, LANES + samples), bf16),
            pltpu.VMEM((windows, 2 * rows, NFFT), bf16),
            pltpu.VMEM((windows, rows, LANES), f32),
        ],
        flops=2 * 2 * rows * samples * 512,
        bytes_accessed=4 * 2**20,
        places="vssv",
    )(strain, fir_taps, spatial, table)
    tail = jax.ShapeDtypeStruct((2 * rows, LANES), bf16)
    tail = call(tail_kernel, tail, places="vvv")(strain, near, far)
    if rep == 4:
        tails = [lax.ppermute(tail, "rep", [(i, i ^ turn) for i in range(rep)]) for turn in (1, 3)]
    else:
        tails = [lax.ppermute(tail, "rep", [(i, i + 1) for i in range(rep - 1)])] * 2
    pieces = jax.ShapeDtypeStruct((rep, windows * 2 * GROUP // LANES, rows, LANES), bf16)
    pieces_made, edge_first = call(
        edge_kernel,
        [pieces, jax.ShapeDtypeStruct((NFFT // LANES, 2 * HALO, LANES), f32)],
        [
            pltpu.VMEM((4 * HALO, LANES + samples), bf16),
            pltpu.VMEM((windows, 4 * HALO, NFFT), bf16),
            pltpu.VMEM((windows, 2 * HALO, LANES), f32),
        ],
        flops=2 * 2 * rows * samples * 256,
        bytes_accessed=2 * 2**20,
        places="v" * 7,
    )(near, far, edge, own, edge_mix, filter_matrix, table)
    pieces = call(
        first_kernel,
        pieces,
        [pltpu.VMEM((1, 2 * rows, NFFT), bf16), pltpu.VMEM((1, rows, LANES), f32)],
        flops=2**22,
        bytes_accessed=2**19,
        places="v" * 8,
    )(*tails, tail_mix, filter_matrix, table, own_first, edge_first, pieces_made)
    arrived = [pieces[0]]
    for step in range(1, rep):
        to = [(i, i ^ step if rep & (rep - 1) == 0 else (i + step) % rep) for i in range(rep)]
        arrived.append(lax.ppermute(pieces[step], "rep", to))
    gathered = jnp.concatenate(arrived, axis=0)
    partners = [gathered]
    for step in range(1, STEPS + 1):
        partners.append(lax.ppermute(gathered, "chan", [((i + step) % chan, i) for i in range(chan)]))
    parts = gathered.shape[0]
    left = call(
        left_kernel,
        jax.ShapeDtypeStruct((2, rows * GROUP, parts * LANES), bf16),
        flops=2**20,
        bytes_accessed=2**20,
    )(gathered)
    scale = 1.0 / (windows * rep)
    return call(
        lambda *refs: tile_kernel(scale, *refs),
        jax.ShapeDtypeStruct((rows, STEPS + 1, BINS // rep, 2 * rows), f32),
        flops=2**24,
        bytes_accessed=2**20,
        places="v" * (STEPS + 2),
    )(left, *partners[::-1])


def solution(mesh):
    in_specs = (P("chan", "rep"), P(), P())
    out_specs = P("chan", None, "rep", None)
    return jax.shard_map(
        per_device, mesh=mesh, in_specs=in_specs, out_specs=out_specs, check_vma=False
    )
```

```python
import math

import jax
import jax.numpy as jnp
import numpy as np
from jax import lax
from jax.experimental import pallas as pl
from jax.experimental.pallas import tpu as pltpu
from jax.sharding import PartitionSpec as P

NFFT = 1024
BINS = 32
FIRST_BIN = 16
STEPS = 4
LANES = 128
HALO = 4
GROUP = 8

epsilon = 1e-05

f32 = jnp.float32
bf16 = jnp.bfloat16


def dot(a, b):
    return lax.dot_general(a, b, (((1,), (0,)), ((), ())), preferred_element_type=f32)


def dot_t(a, b):
    return lax.dot_general(a, b, (((1,), (1,)), ((), ())), preferred_element_type=f32)


def halves(values):
    high = values.astype(bf16)
    low = (values - high.astype(f32)).astype(bf16)
    return high, low


def dft_table():
    sample = np.arange(NFFT)[:, None]
    bins = FIRST_BIN + np.arange(BINS)[None, :]
    angle = (sample * bins % NFFT) * (2.0 * math.pi / NFFT)
    scale = 1.0 / math.sqrt(NFFT)
    real = (np.cos(angle) * scale).reshape(NFFT, BINS // GROUP, GROUP)
    imag = (-np.sin(angle) * scale).reshape(NFFT, BINS // GROUP, GROUP)
    table = np.concatenate([real, imag], axis=2).reshape(NFFT, 2 * BINS).astype(np.float32)
    high = table.astype(jnp.bfloat16)
    low = (table - high.astype(np.float32)).astype(jnp.bfloat16)
    return np.concatenate([high, low], axis=1)


def toeplitz(taps_ref):
    lane = lax.broadcasted_iota(jnp.int32, (LANES, LANES), 1)
    row = lax.broadcasted_iota(jnp.int32, (LANES, LANES), 0)
    taps = jnp.zeros((1, LANES), f32)
    for k in range(taps_ref.shape[0]):
        taps = jnp.where(lane[:1] == k, taps_ref[k], taps)
    turned = pltpu.roll(jnp.broadcast_to(taps, (LANES, LANES)), 0, 1, stride=1, stride_axis=0)
    parts = [jnp.where(lane < row, turned, 0.0), jnp.where(lane >= row, turned, 0.0)]
    return jnp.concatenate(halves(jnp.concatenate(parts, axis=0)), axis=1)


def mixing(spatial_ref, lag):
    weight = jnp.zeros(lag.shape, f32)
    for j in range(spatial_ref.shape[0]):
        weight = jnp.where(lag == j, spatial_ref[j], weight)
    high = weight.astype(bf16).astype(f32)
    return jnp.concatenate([high, weight - high], axis=0).astype(bf16)


def received_row(source, count):
    before = (source < HALO) == (lax.axis_index("chan") % 2 != 0)
    return source % HALO + jnp.where(before, -HALO, count)


def edge_lags(count):
    shape = (2 * HALO, 2 * HALO)
    target = lax.broadcasted_iota(jnp.int32, shape, 0)
    target = jnp.where(target < HALO, target, target + count - 2 * HALO)
    return received_row(lax.broadcasted_iota(jnp.int32, shape, 1), count) + HALO - target


def filtered(mixed_ref, first, count, rows, toeplitz_ref):
    parts = []
    for block in range(count):
        start = pl.multiple_of((first + block) * LANES, LANES)
        parts.append(mixed_ref[:, pl.ds(start, 2 * LANES)])
    out = dot(jnp.concatenate(parts, axis=0), toeplitz_ref[...])
    out = out[:, :LANES] + out[:, LANES:]
    out = out.reshape(count, 2, rows, LANES)
    return out[:, 0] + out[:, 1]


def windowed(band, first_window, rows, split_ref, scale_ref):
    per = NFFT // LANES
    count = band.shape[0] // per
    squares = band * band
    for window in range(count):
        total = squares[window * per]
        for block in range(1, per):
            total = total + squares[window * per + block]
        power = jnp.sum(total, axis=1, keepdims=True) * (1.0 / NFFT)
        scale_ref[first_window + window] = jnp.broadcast_to(1.0 / jnp.sqrt(power + epsilon), (rows, LANES))
    high = band.astype(bf16).astype(f32)
    low = band - high
    both = jnp.concatenate([high, low], axis=1).astype(bf16)
    for window in range(count):
        for block in range(per):
            split_ref[first_window + window, :, block * LANES : (block + 1) * LANES] = both[window * per + block]


def remainder(band):
    squares = band * band
    lane = lax.broadcasted_iota(jnp.int32, squares.shape[1:], 1)
    total = jnp.where(lane < LANES // 2, 0.0, squares[0])
    for block in range(1, NFFT // LANES):
        total = total + squares[block]
    return jnp.broadcast_to(jnp.sum(total, axis=1, keepdims=True), total.shape)


def spill_of(mixed, toeplitz_ref):
    rows = mixed.shape[0] // 2
    out = dot(mixed, toeplitz_ref[:LANES, :])
    out = out[:, :LANES] + out[:, LANES:]
    return out[:rows] + out[rows:]


def spectra_of(split_ref, scale_ref, dft_ref, rows):
    windows = split_ref.shape[0]
    out = dot(split_ref[...].reshape(windows * 2 * rows, NFFT), dft_ref[...])
    out = out + pltpu.roll(out, LANES // 2, 1)
    out = out.reshape(windows, 2, rows, LANES)
    return (out[:, 0] + out[:, 1]) * scale_ref[...]


def own_kernel(
    strain_ref,
    taps_ref,
    spatial_ref,
    dft_ref,
    edge_ref,
    spectra_ref,
    lead_ref,
    toeplitz_ref,
    edge_mix_ref,
    mixed_ref,
    split_ref,
    scale_ref,
):
    rows, samples = strain_ref.shape
    source = lax.broadcasted_iota(jnp.int32, (rows, rows), 1)
    weights = mixing(spatial_ref, source + HALO - lax.broadcasted_iota(jnp.int32, (rows, rows), 0))
    toeplitz_ref[...] = toeplitz(taps_ref)
    edge_mix_ref[...] = mixing(spatial_ref, edge_lags(rows))

    def mix(columns):
        out = dot(weights, columns)
        high, low = halves(out[:rows] + out[rows:])
        return jnp.concatenate([high, low], axis=0)

    mixed_ref[:, :LANES] = jnp.zeros((2 * rows, LANES), bf16)
    step = samples // 2

    def mix_step(i, _):
        start = pl.multiple_of(i * step, step)
        mixed_ref[:, pl.ds(pl.multiple_of(start + LANES, LANES), step)] = mix(strain_ref[:, pl.ds(start, step)])
        return 0

    lax.fori_loop(0, samples // step, mix_step, 0)
    count = step // LANES
    near = lax.broadcasted_iota(jnp.int32, (count, rows // 2, LANES), 1) < HALO

    def filter_step(i, _):
        band = filtered(mixed_ref, i * count, count, rows, toeplitz_ref)
        edge_ref[pl.ds(i * count, count)] = jnp.where(near, band[:, : rows // 2], band[:, rows // 2 :])
        windowed(band, i * (step // NFFT), rows, split_ref, scale_ref)

        @pl.when(i == 0)
        def _():
            lead_ref[0] = band[0]
            lead_ref[1] = remainder(band[: NFFT // LANES])
            scale_ref[0] = jnp.ones((rows, LANES), f32)

        return 0

    lax.fori_loop(0, samples // step, filter_step, 0)
    spectra_ref[...] = spectra_of(split_ref, scale_ref, dft_ref, rows)
    lead_ref[2] = spill_of(mixed_ref[:, samples:], toeplitz_ref)


def whole_block(edges, own):
    rows = edges.shape[1]
    near = lax.broadcasted_iota(jnp.int32, edges.shape, 1) < HALO
    return jnp.concatenate([jnp.where(near, edges, own[:, :rows]), jnp.where(near, own[:, rows:], edges)], axis=1)


def place_of(group, groups):
    here = lax.axis_index("rep")
    return jnp.bitwise_xor(group, here) if groups & (groups - 1) == 0 else lax.rem(group - here + groups, groups)


def edge_kernel(
    near_ref,
    far_ref,
    edge_ref,
    own_ref,
    lead_ref,
    mix_ref,
    toeplitz_ref,
    dft_ref,
    out_ref,
    mixed_ref,
    split_ref,
    scale_ref,
):
    rows = 2 * HALO
    step = near_ref.shape[1]
    both = jnp.concatenate([near_ref[...].astype(f32), far_ref[...].astype(f32)], axis=0).astype(bf16)
    mixed = dot(mix_ref[...], both)
    mixed = mixed[:rows] + mixed[rows:]
    high = mixed.astype(bf16).astype(f32)
    mixed_ref[:, :LANES] = jnp.zeros((2 * rows, LANES), bf16)
    mixed_ref[:, LANES:] = jnp.concatenate([high, mixed - high], axis=0).astype(bf16)
    band = filtered(mixed_ref, 0, step // LANES, rows, toeplitz_ref) + edge_ref[...]
    windowed(band, 0, rows, split_ref, scale_ref)
    scale_ref[0] = jnp.ones((rows, LANES), f32)
    edges = spectra_of(split_ref, scale_ref, dft_ref, rows)
    spectra = whole_block(edges, own_ref[...])

    lead = whole_block(jnp.stack([band[0], remainder(band[: NFFT // LANES])]), lead_ref[:2])
    spill = spill_of(mixed_ref[:, step:], toeplitz_ref)
    near = lax.broadcasted_iota(jnp.int32, spill.shape, 0) < HALO
    spill = lead_ref[2] + jnp.concatenate([jnp.where(near, spill, 0.0), jnp.where(near, 0.0, spill)], axis=0)
    change = dot(jnp.concatenate(halves(spill), axis=0), dft_ref[:LANES, :])
    change = change[: 2 * rows] + change[2 * rows :]
    change = change + pltpu.roll(change, LANES // 2, 1)

    def parted(values):
        high = values.astype(bf16).astype(f32)
        return high, values - high

    width = 2 * GROUP
    across = LANES // width
    lane = lax.broadcasted_iota(jnp.int32, spectra.shape[1:], 1)
    slot = lane // width
    samples = parted(jnp.where(lane < LANES // 2, lead[0], pltpu.roll(spill, LANES // 2, 1)))
    change = parted(change)
    rest = parted(lead[1])
    groups = out_ref.shape[0]
    for group in range(groups):
        place = place_of(group, groups)

        def moved(value, to):
            shift = (to - group) * width % LANES
            return pltpu.roll(value, shift, 1) if shift else value

        for outer in range(out_ref.shape[1] - 3):
            tile = moved(spectra[outer * across], 0)
            for inner in range(1, across):
                tile = jnp.where(slot == inner, moved(spectra[outer * across + inner], inner), tile)
            out_ref[place, outer] = tile.astype(bf16)
        extra = [parted(moved(spectra[0], 0))[1], moved(change[0], 1), moved(change[1], 2), *rest]
        tile = extra[0]
        for inner in range(1, len(extra)):
            tile = jnp.where(slot == inner, extra[inner], tile)
        for index, value in enumerate((*samples, tile)):
            out_ref[place, out_ref.shape[1] - 3 + index] = value.astype(bf16)


def merge_kernel(pieces_ref, *refs):
    out_ref = refs[-1]
    parts = [pieces_ref.at[0], *refs[:-1]]
    count = pieces_ref.shape[1] - 3
    groups = len(parts)
    here = lax.axis_index("rep")
    lane = lax.broadcasted_iota(jnp.int32, pieces_ref.shape[2:], 1)
    width = 2 * GROUP
    reps, leads, spills, rests, raws, changes = [], [], [], [], [], []
    for step, part in enumerate(parts):
        reps.append(jnp.bitwise_xor(here, step) if groups & (groups - 1) == 0 else lax.rem(here - step + groups, groups))
        samples = part[count].astype(f32) + part[count + 1].astype(f32)
        extra = part[count + 2].astype(f32)
        leads.append(jnp.where(lane < LANES // 2, samples, 0.0))
        spills.append(jnp.where(lane < LANES // 2, pltpu.roll(samples, LANES // 2, 1), 0.0))
        raws.append(part[0].astype(f32))
        changes.append(pltpu.roll(extra, LANES - width, 1) + pltpu.roll(extra, LANES - 2 * width, 1))
        rests.append(extra[:, 3 * width : 3 * width + 1] + extra[:, 4 * width : 4 * width + 1])
        raws[-1] = jnp.where(lane < width, raws[-1] + extra, raws[-1])
    for step, part in enumerate(parts):
        spill = jnp.zeros_like(leads[step])
        change = jnp.zeros_like(leads[step])
        for other in range(groups):
            if other != step:
                before = reps[other] == reps[step] - 1
                spill = jnp.where(before, spills[other], spill)
                change = jnp.where(before, changes[other], change)
        lead = leads[step] + spill
        power = (rests[step] + jnp.sum(lead * lead, axis=1, keepdims=True)) * (1.0 / NFFT)
        first = (raws[step] + change) * (1.0 / jnp.sqrt(power + epsilon))
        out_ref[step * count] = jnp.where(lane < width, first, raws[step]).astype(bf16)
        for index in range(1, count):
            out_ref[step * count + index] = part[index]


def rim_kernel(strain_ref, within_ref, across_ref):
    rows = strain_ref.shape[0]
    even = lax.axis_index("chan") % 2 == 0
    head, tail = strain_ref[:HALO], strain_ref[rows - HALO :]
    within_ref[...] = jnp.where(even, tail, head)
    across_ref[...] = jnp.where(even, head, tail)


def left_kernel(own_ref, left_ref):
    parts, rows, _ = own_ref.shape
    lane = lax.broadcasted_iota(jnp.int32, (GROUP, LANES), 1)
    mask = lane % GROUP == lax.broadcasted_iota(jnp.int32, (GROUP, LANES), 0)
    real_lane = lax.broadcasted_iota(jnp.int32, (rows, LANES), 1) % (2 * GROUP) < GROUP

    for part in range(parts):
        value = own_ref[part].astype(f32)
        turned = jnp.where(real_lane, pltpu.roll(value, LANES - GROUP, 1), -pltpu.roll(value, GROUP, 1))
        for half, source in enumerate((value, turned)):
            spread = [jnp.where(mask, jnp.broadcast_to(source[c : c + 1], (GROUP, LANES)), 0.0) for c in range(rows)]
            left_ref[half, :, part * LANES : (part + 1) * LANES] = jnp.concatenate(spread, axis=0).astype(bf16)


def tile_kernel(scale, left_ref, *refs):
    partner_refs, out_ref = refs[:-1], refs[-1]
    parts, rows, _ = partner_refs[0].shape
    right = jnp.concatenate(
        [jnp.concatenate([ref[part] for part in range(parts)], axis=1) for ref in partner_refs], axis=0
    )
    real = dot_t(left_ref[0], right) * scale
    imag = dot_t(left_ref[1], right) * scale
    for c in range(rows):
        for s in range(len(partner_refs)):
            a = real[c * GROUP : (c + 1) * GROUP, s * rows : (s + 1) * rows]
            b = imag[c * GROUP : (c + 1) * GROUP, s * rows : (s + 1) * rows]
            out_ref[c, s] = jnp.concatenate([a, b], axis=1)


def call(kernel, out_shape, scratch=(), flops=0, bytes_accessed=0, places="v"):
    whole = {"v": pl.BlockSpec(memory_space=pltpu.VMEM), "s": pl.BlockSpec(memory_space=pltpu.SMEM)}
    return pl.pallas_call(
        kernel,
        out_shape=out_shape,
        in_specs=[whole[place] for place in places],
        scratch_shapes=list(scratch),
        compiler_params=pltpu.CompilerParams(vmem_limit_bytes=32 * 2**20),
        cost_estimate=pl.CostEstimate(flops=flops, bytes_accessed=bytes_accessed, transcendentals=0),
    )


def per_device(strain, fir_taps, spatial):
    rows, samples = strain.shape
    windows = samples // NFFT
    blocks = samples // LANES
    rep = lax.axis_size("rep")
    chan = lax.axis_size("chan")
    even = lax.axis_index("chan") % 2 == 0
    pairs_within = [(i, i ^ 1) for i in range(chan) if i ^ 1 < chan]
    pairs_across = [(i, j) for i in range(chan) for j in (i + 1 if i % 2 else i - 1,) if 0 <= j < chan]

    rim = jax.ShapeDtypeStruct((HALO, samples), bf16)
    within, across = call(rim_kernel, [rim, rim], bytes_accessed=2**20)(strain)
    near = lax.ppermute(within, "chan", pairs_within)
    far = lax.ppermute(across, "chan", pairs_across)

    table = jnp.asarray(dft_table())
    edge, own, lead, filter_matrix, edge_mix = call(
        own_kernel,
        [
            jax.ShapeDtypeStruct((blocks, 2 * HALO, LANES), f32),
            jax.ShapeDtypeStruct((windows, rows, LANES), f32),
            jax.ShapeDtypeStruct((3, rows, LANES), f32),
            jax.ShapeDtypeStruct((2 * LANES, 2 * LANES), bf16),
            jax.ShapeDtypeStruct((4 * HALO, 2 * HALO), bf16),
        ],
        [
            pltpu.VMEM((2 * rows, LANES + samples), bf16),
            pltpu.VMEM((windows, 2 * rows, NFFT), bf16),
            pltpu.VMEM((windows, rows, LANES), f32),
        ],
        flops=2 * 2 * rows * samples * 512,
        bytes_accessed=4 * 2**20,
        places="vssv",
    )(strain, fir_taps, spatial, table)
    count = windows * 2 * GROUP // LANES
    pieces = call(
        edge_kernel,
        jax.ShapeDtypeStruct((rep, count + 3, rows, LANES), bf16),
        [
            pltpu.VMEM((4 * HALO, LANES + samples), bf16),
            pltpu.VMEM((windows, 4 * HALO, NFFT), bf16),
            pltpu.VMEM((windows, 2 * HALO, LANES), f32),
        ],
        flops=2 * 2 * rows * samples * 256,
        bytes_accessed=2 * 2**20,
        places="v" * 8,
    )(near, far, edge, own, lead, edge_mix, filter_matrix, table)
    arrived = []
    for step in range(1, rep):
        to = [(i, i ^ step if rep & (rep - 1) == 0 else (i + step) % rep) for i in range(rep)]
        arrived.append(lax.ppermute(pieces[step], "rep", to))
    gathered = call(
        merge_kernel,
        jax.ShapeDtypeStruct((rep * count, rows, LANES), bf16),
        flops=2**16,
        bytes_accessed=2**18,
        places="v" * rep,
    )(pieces, *arrived)
    partners = [gathered]
    for step in range(1, STEPS + 1):
        partners.append(lax.ppermute(gathered, "chan", [((i + step) % chan, i) for i in range(chan)]))
    parts = gathered.shape[0]
    left = call(
        left_kernel,
        jax.ShapeDtypeStruct((2, rows * GROUP, parts * LANES), bf16),
        flops=2**20,
        bytes_accessed=2**20,
    )(gathered)
    scale = 1.0 / (windows * rep)
    return call(
        lambda *refs: tile_kernel(scale, *refs),
        jax.ShapeDtypeStruct((rows, STEPS + 1, BINS // rep, 2 * rows), f32),
        flops=2**24,
        bytes_accessed=2**20,
        places="v" * (STEPS + 2),
    )(left, *partners)


def solution(mesh):
    in_specs = (P("chan", "rep"), P(), P())
    out_specs = P("chan", None, "rep", None)
    return jax.shard_map(
        per_device, mesh=mesh, in_specs=in_specs, out_specs=out_specs, check_vma=False
    )
```

```python
import math

import jax
import jax.numpy as jnp
import numpy as np
from jax import lax
from jax.experimental import pallas as pl
from jax.experimental.pallas import tpu as pltpu
from jax.sharding import PartitionSpec as P

NFFT = 1024
BINS = 32
FIRST_BIN = 16
STEPS = 4
LANES = 128
HALO = 4
GROUP = 8

epsilon = 1e-05

f32 = jnp.float32
bf16 = jnp.bfloat16


def dot(a, b):
    return lax.dot_general(a, b, (((1,), (0,)), ((), ())), preferred_element_type=f32)


def dot_t(a, b):
    return lax.dot_general(a, b, (((1,), (1,)), ((), ())), preferred_element_type=f32)


def halves(values):
    high = values.astype(bf16)
    low = (values - high.astype(f32)).astype(bf16)
    return high, low


def dft_table():
    sample = np.arange(NFFT)[:, None]
    bins = FIRST_BIN + np.arange(BINS)[None, :]
    angle = (sample * bins % NFFT) * (2.0 * math.pi / NFFT)
    scale = 1.0 / math.sqrt(NFFT)
    real = (np.cos(angle) * scale).reshape(NFFT, BINS // GROUP, GROUP)
    imag = (-np.sin(angle) * scale).reshape(NFFT, BINS // GROUP, GROUP)
    table = np.concatenate([real, imag], axis=2).reshape(NFFT, 2 * BINS).astype(np.float32)
    high = table.astype(jnp.bfloat16)
    low = (table - high.astype(np.float32)).astype(jnp.bfloat16)
    return np.concatenate([high, low], axis=1)


def toeplitz(taps_ref):
    lane = lax.broadcasted_iota(jnp.int32, (LANES, LANES), 1)
    row = lax.broadcasted_iota(jnp.int32, (LANES, LANES), 0)
    taps = jnp.zeros((1, LANES), f32)
    for k in range(taps_ref.shape[0]):
        taps = jnp.where(lane[:1] == k, taps_ref[k], taps)
    turned = pltpu.roll(jnp.broadcast_to(taps, (LANES, LANES)), 0, 1, stride=1, stride_axis=0)
    parts = [jnp.where(lane < row, turned, 0.0), jnp.where(lane >= row, turned, 0.0)]
    return jnp.concatenate(halves(jnp.concatenate(parts, axis=0)), axis=1)


def mixing(spatial_ref, lag):
    weight = jnp.zeros(lag.shape, f32)
    for j in range(spatial_ref.shape[0]):
        weight = jnp.where(lag == j, spatial_ref[j], weight)
    high = weight.astype(bf16).astype(f32)
    return jnp.concatenate([high, weight - high], axis=0).astype(bf16)


def direct(toeplitz_ref, dft_ref, out_ref):
    lane = lax.broadcasted_iota(jnp.int32, (LANES, LANES), 1)
    left = [toeplitz_ref[:LANES, :LANES], toeplitz_ref[:LANES, LANES:], toeplitz_ref[LANES:, :LANES], toeplitz_ref[LANES:, LANES:]]
    left = jnp.concatenate(left, axis=0)
    carried = jnp.zeros((LANES, LANES), f32)
    for block in range(NFFT // LANES + 1):
        weights = carried
        if block < NFFT // LANES:
            out = dot(left, dft_ref[block * LANES : (block + 1) * LANES, :])
            out = out + pltpu.roll(out, LANES // 2, 1)
            weights = weights + out[:LANES] + out[LANES : 2 * LANES]
            carried = out[2 * LANES : 3 * LANES] + out[3 * LANES :]
        high = weights.astype(bf16).astype(f32)
        part = jnp.where(lane < LANES // 2, high, weights - high)
        out_ref[block * LANES : (block + 1) * LANES, :] = part.astype(bf16)


def edge_weights(spatial_ref, out_ref):
    row = lax.broadcasted_iota(jnp.int32, out_ref.shape[1:], 0)
    span = 2 * HALO
    out_ref[0] = jnp.where(row < HALO, spatial_ref[0], spatial_ref[span])
    for lag in range(1, HALO):
        out_ref[lag] = jnp.where(row < HALO - lag, spatial_ref[lag], 0.0)
        out_ref[HALO - 1 + lag] = jnp.where(row >= HALO + lag, spatial_ref[span - lag], 0.0)


def filtered(mixed_ref, first, count, rows, toeplitz_ref):
    parts = []
    for block in range(count):
        start = pl.multiple_of((first + block) * LANES, LANES)
        parts.append(mixed_ref[:, pl.ds(start, 2 * LANES)])
    out = dot(jnp.concatenate(parts, axis=0), toeplitz_ref[...])
    out = out[:, :LANES] + out[:, LANES:]
    out = out.reshape(count, 2, rows, LANES)
    return out[:, 0] + out[:, 1]


def windowed(band, first_window, rows, split_ref, scale_ref):
    per = NFFT // LANES
    count = band.shape[0] // per
    squares = band * band
    for window in range(count):
        total = squares[window * per]
        for block in range(1, per):
            total = total + squares[window * per + block]
        power = jnp.sum(total, axis=1, keepdims=True) * (1.0 / NFFT)
        scale_ref[first_window + window] = jnp.broadcast_to(1.0 / jnp.sqrt(power + epsilon), (rows, LANES))
    high = band.astype(bf16).astype(f32)
    low = band - high
    both = jnp.concatenate([high, low], axis=1).astype(bf16)
    for window in range(count):
        for block in range(per):
            split_ref[first_window + window, :, block * LANES : (block + 1) * LANES] = both[window * per + block]


def remainder(band):
    squares = band * band
    lane = lax.broadcasted_iota(jnp.int32, squares.shape[1:], 1)
    total = jnp.where(lane < LANES // 2, 0.0, squares[0])
    for block in range(1, NFFT // LANES):
        total = total + squares[block]
    return jnp.broadcast_to(jnp.sum(total, axis=1, keepdims=True), total.shape)


def spill_of(mixed, toeplitz_ref):
    rows = mixed.shape[0] // 2
    out = dot(mixed, toeplitz_ref[:LANES, :])
    out = out[:, :LANES] + out[:, LANES:]
    return out[:rows] + out[rows:]


def spectra_of(split_ref, scale_ref, dft_ref, rows):
    windows = split_ref.shape[0]
    out = dot(split_ref[...].reshape(windows * 2 * rows, NFFT), dft_ref[...])
    out = out + pltpu.roll(out, LANES // 2, 1)
    out = out.reshape(windows, 2, rows, LANES)
    return (out[:, 0] + out[:, 1]) * scale_ref[...]


def own_kernel(
    strain_ref,
    taps_ref,
    spatial_ref,
    dft_ref,
    edge_ref,
    spectra_ref,
    lead_ref,
    toeplitz_ref,
    edge_mix_ref,
    direct_ref,
    mixed_ref,
    split_ref,
    scale_ref,
):
    rows, samples = strain_ref.shape
    source = lax.broadcasted_iota(jnp.int32, (rows, rows), 1)
    weights = mixing(spatial_ref, source + HALO - lax.broadcasted_iota(jnp.int32, (rows, rows), 0))
    toeplitz_ref[...] = toeplitz(taps_ref)
    edge_weights(spatial_ref, edge_mix_ref)
    direct(toeplitz_ref, dft_ref, direct_ref)

    def mix(columns):
        out = dot(weights, columns)
        high, low = halves(out[:rows] + out[rows:])
        return jnp.concatenate([high, low], axis=0)

    mixed_ref[:, :LANES] = jnp.zeros((2 * rows, LANES), bf16)
    step = samples // 2

    def mix_step(i, _):
        start = pl.multiple_of(i * step, step)
        mixed_ref[:, pl.ds(pl.multiple_of(start + LANES, LANES), step)] = mix(strain_ref[:, pl.ds(start, step)])
        return 0

    lax.fori_loop(0, samples // step, mix_step, 0)
    count = step // LANES
    near = lax.broadcasted_iota(jnp.int32, (count, rows // 2, LANES), 1) < HALO

    def filter_step(i, _):
        band = filtered(mixed_ref, i * count, count, rows, toeplitz_ref)
        edge = jnp.where(near, band[:, : rows // 2], band[:, rows // 2 :])
        edge_ref[:, pl.ds(pl.multiple_of(i * (rows // 2), rows // 2), rows // 2)] = edge
        windowed(band, i * (step // NFFT), rows, split_ref, scale_ref)

        @pl.when(i == 0)
        def _():
            lead_ref[0] = band[0]
            lead_ref[1] = remainder(band[: NFFT // LANES])
            scale_ref[0] = jnp.ones((rows, LANES), f32)

        return 0

    lax.fori_loop(0, samples // step, filter_step, 0)
    row = lax.broadcasted_iota(jnp.int32, scale_ref.shape, 1)
    inside = (row >= HALO) & (row < rows - HALO)
    scale_ref[...] = jnp.where(inside, scale_ref[...], 1.0)
    spectra_ref[...] = spectra_of(split_ref, scale_ref, dft_ref, rows)
    lead_ref[2] = spill_of(mixed_ref[:, samples:], toeplitz_ref)


def whole_block(edges, own):
    rows = edges.shape[1]
    near = lax.broadcasted_iota(jnp.int32, edges.shape, 1) < HALO
    return jnp.concatenate([jnp.where(near, edges, own[:, :rows]), jnp.where(near, own[:, rows:], edges)], axis=1)


def place_of(group, groups):
    here = lax.axis_index("rep")
    return jnp.bitwise_xor(group, here) if groups & (groups - 1) == 0 else lax.rem(group - here + groups, groups)


def edge_kernel(
    near_ref,
    far_ref,
    edge_ref,
    own_ref,
    lead_ref,
    mix_ref,
    toeplitz_ref,
    dft_ref,
    direct_ref,
    out_ref,
    received_ref,
):
    rows = 2 * HALO
    half = near_ref.shape[1] // 2
    even = lax.axis_index("chan") % 2 == 0
    near, far = near_ref[...].astype(f32), far_ref[...].astype(f32)
    both = jnp.concatenate([jnp.where(even, far, near), jnp.where(even, near, far)], axis=0)
    both = jnp.concatenate([jnp.zeros((rows, LANES), f32), both], axis=1)
    received_ref[...] = jnp.concatenate([both[:, : half + LANES], both[:, half:]], axis=0).astype(bf16)

    def mixed(samples):
        out = samples * mix_ref[0]
        for lag in range(1, HALO):
            out = out + pltpu.roll(samples, rows - lag, 1) * mix_ref[lag]
            out = out + pltpu.roll(samples, lag, 1) * mix_ref[HALO - 1 + lag]
        return out

    parts = [received_ref[:, start : start + 2 * LANES] for start in range(0, half, LANES)]
    out = dot(jnp.concatenate(parts, axis=0), toeplitz_ref[...])
    out = (out[:, :LANES] + out[:, LANES:]).reshape(-1, rows, LANES)
    band = (mixed(out) + edge_ref[...].reshape(out.shape)).reshape(edge_ref.shape)
    power = jnp.sum((band * band).reshape(-1, NFFT // LANES, 2 * rows, LANES), axis=1)
    power = jnp.sum(power, axis=2, keepdims=True) * (1.0 / NFFT)
    scale = 1.0 / jnp.sqrt(power + epsilon)
    scale = jnp.concatenate([scale[:, :rows], scale[:, rows:]], axis=0)
    window = lax.broadcasted_iota(jnp.int32, scale.shape, 0)
    scale = jnp.where(window == 0, 1.0, scale)

    parts = [received_ref[:, start : start + NFFT + LANES] for start in range(0, half, NFFT)]
    out = dot(jnp.concatenate(parts, axis=0), direct_ref[...])
    out = (out + pltpu.roll(out, LANES // 2, 1)).reshape(-1, 2 * rows, LANES)
    edges = mixed(jnp.concatenate([out[:, :rows], out[:, rows:]], axis=0))
    own = own_ref[...]
    near = lax.broadcasted_iota(jnp.int32, edges.shape, 1) < HALO
    edges = (edges + jnp.where(near, own[:, :rows], own[:, rows:])) * scale
    spectra = whole_block(edges, own)
    band = band[: NFFT // LANES, :rows]

    lead = whole_block(jnp.stack([band[0], remainder(band)]), lead_ref[:2])
    spill = dot(received_ref[:, half:], toeplitz_ref[:LANES, :])[rows:]
    spill = mixed((spill[:, :LANES] + spill[:, LANES:])[None])[0]
    near = lax.broadcasted_iota(jnp.int32, spill.shape, 0) < HALO
    spill = lead_ref[2] + jnp.concatenate([jnp.where(near, spill, 0.0), jnp.where(near, 0.0, spill)], axis=0)
    change = dot(jnp.concatenate(halves(spill), axis=0), dft_ref[:LANES, :])
    change = change[: 2 * rows] + change[2 * rows :]
    change = change + pltpu.roll(change, LANES // 2, 1)

    def parted(values):
        high = values.astype(bf16).astype(f32)
        return high, values - high

    width = 2 * GROUP
    across = LANES // width
    lane = lax.broadcasted_iota(jnp.int32, spectra.shape[1:], 1)
    slot = lane // width
    samples = parted(jnp.where(lane < LANES // 2, lead[0], pltpu.roll(spill, LANES // 2, 1)))
    change = parted(change)
    rest = parted(lead[1])
    groups = out_ref.shape[0]
    for group in range(groups):
        place = place_of(group, groups)

        def moved(value, to):
            shift = (to - group) * width % LANES
            return pltpu.roll(value, shift, 1) if shift else value

        for outer in range(out_ref.shape[1] - 3):
            tile = moved(spectra[outer * across], 0)
            for inner in range(1, across):
                tile = jnp.where(slot == inner, moved(spectra[outer * across + inner], inner), tile)
            out_ref[place, outer] = tile.astype(bf16)
        extra = [parted(moved(spectra[0], 0))[1], moved(change[0], 1), moved(change[1], 2), *rest]
        tile = extra[0]
        for inner in range(1, len(extra)):
            tile = jnp.where(slot == inner, extra[inner], tile)
        for index, value in enumerate((*samples, tile)):
            out_ref[place, out_ref.shape[1] - 3 + index] = value.astype(bf16)


def merge_kernel(pieces_ref, *refs):
    out_ref = refs[-1]
    parts = [pieces_ref.at[0], *refs[:-1]]
    count = pieces_ref.shape[1] - 3
    groups = len(parts)
    here = lax.axis_index("rep")
    lane = lax.broadcasted_iota(jnp.int32, pieces_ref.shape[2:], 1)
    width = 2 * GROUP
    reps, leads, spills, rests, raws, changes = [], [], [], [], [], []
    for step, part in enumerate(parts):
        reps.append(jnp.bitwise_xor(here, step) if groups & (groups - 1) == 0 else lax.rem(here - step + groups, groups))
        samples = part[count].astype(f32) + part[count + 1].astype(f32)
        extra = part[count + 2].astype(f32)
        leads.append(jnp.where(lane < LANES // 2, samples, 0.0))
        spills.append(jnp.where(lane < LANES // 2, pltpu.roll(samples, LANES // 2, 1), 0.0))
        raws.append(part[0].astype(f32))
        changes.append(pltpu.roll(extra, LANES - width, 1) + pltpu.roll(extra, LANES - 2 * width, 1))
        rests.append(extra[:, 3 * width : 3 * width + 1] + extra[:, 4 * width : 4 * width + 1])
        raws[-1] = jnp.where(lane < width, raws[-1] + extra, raws[-1])
    for step, part in enumerate(parts):
        spill = jnp.zeros_like(leads[step])
        change = jnp.zeros_like(leads[step])
        for other in range(groups):
            if other != step:
                before = reps[other] == reps[step] - 1
                spill = jnp.where(before, spills[other], spill)
                change = jnp.where(before, changes[other], change)
        lead = leads[step] + spill
        power = (rests[step] + jnp.sum(lead * lead, axis=1, keepdims=True)) * (1.0 / NFFT)
        first = (raws[step] + change) * (1.0 / jnp.sqrt(power + epsilon))
        out_ref[step * count] = jnp.where(lane < width, first, raws[step]).astype(bf16)
        for index in range(1, count):
            out_ref[step * count + index] = part[index]


def rim_kernel(strain_ref, within_ref, across_ref):
    rows = strain_ref.shape[0]
    even = lax.axis_index("chan") % 2 == 0
    head, tail = strain_ref[:HALO], strain_ref[rows - HALO :]
    within_ref[...] = jnp.where(even, tail, head)
    across_ref[...] = jnp.where(even, head, tail)


def left_kernel(own_ref, left_ref):
    parts, rows, _ = own_ref.shape
    lane = lax.broadcasted_iota(jnp.int32, (GROUP, LANES), 1)
    mask = lane % GROUP == lax.broadcasted_iota(jnp.int32, (GROUP, LANES), 0)
    real_lane = lax.broadcasted_iota(jnp.int32, (rows, LANES), 1) % (2 * GROUP) < GROUP

    for part in range(parts):
        value = own_ref[part].astype(f32)
        turned = jnp.where(real_lane, pltpu.roll(value, LANES - GROUP, 1), -pltpu.roll(value, GROUP, 1))
        for half, source in enumerate((value, turned)):
            spread = [jnp.where(mask, jnp.broadcast_to(source[c : c + 1], (GROUP, LANES)), 0.0) for c in range(rows)]
            left_ref[half, :, part * LANES : (part + 1) * LANES] = jnp.concatenate(spread, axis=0).astype(bf16)


def tile_kernel(scale, left_ref, *refs):
    partner_refs, out_ref = refs[:-1], refs[-1]
    parts, rows, _ = partner_refs[0].shape
    right = jnp.concatenate(
        [jnp.concatenate([ref[part] for part in range(parts)], axis=1) for ref in partner_refs], axis=0
    )
    real = dot_t(left_ref[0], right) * scale
    imag = dot_t(left_ref[1], right) * scale
    for c in range(rows):
        for s in range(len(partner_refs)):
            a = real[c * GROUP : (c + 1) * GROUP, s * rows : (s + 1) * rows]
            b = imag[c * GROUP : (c + 1) * GROUP, s * rows : (s + 1) * rows]
            out_ref[c, s] = jnp.concatenate([a, b], axis=1)


def call(kernel, out_shape, scratch=(), flops=0, bytes_accessed=0, places="v"):
    whole = {"v": pl.BlockSpec(memory_space=pltpu.VMEM), "s": pl.BlockSpec(memory_space=pltpu.SMEM)}
    return pl.pallas_call(
        kernel,
        out_shape=out_shape,
        in_specs=[whole[place] for place in places],
        scratch_shapes=list(scratch),
        compiler_params=pltpu.CompilerParams(vmem_limit_bytes=32 * 2**20),
        cost_estimate=pl.CostEstimate(flops=flops, bytes_accessed=bytes_accessed, transcendentals=0),
    )


def per_device(strain, fir_taps, spatial):
    rows, samples = strain.shape
    windows = samples // NFFT
    blocks = samples // LANES
    rep = lax.axis_size("rep")
    chan = lax.axis_size("chan")
    even = lax.axis_index("chan") % 2 == 0
    pairs_within = [(i, i ^ 1) for i in range(chan) if i ^ 1 < chan]
    pairs_across = [(i, j) for i in range(chan) for j in (i + 1 if i % 2 else i - 1,) if 0 <= j < chan]

    rim = jax.ShapeDtypeStruct((HALO, samples), bf16)
    within, across = call(rim_kernel, [rim, rim], bytes_accessed=2**20)(strain)
    near = lax.ppermute(within, "chan", pairs_within)
    far = lax.ppermute(across, "chan", pairs_across)

    table = jnp.asarray(dft_table())
    edge, own, lead, filter_matrix, edge_mix, direct_matrix = call(
        own_kernel,
        [
            jax.ShapeDtypeStruct((blocks // 2, rows, LANES), f32),
            jax.ShapeDtypeStruct((windows, rows, LANES), f32),
            jax.ShapeDtypeStruct((3, rows, LANES), f32),
            jax.ShapeDtypeStruct((2 * LANES, 2 * LANES), bf16),
            jax.ShapeDtypeStruct((2 * HALO - 1, 2 * HALO, LANES), f32),
            jax.ShapeDtypeStruct((LANES + NFFT, LANES), bf16),
        ],
        [
            pltpu.VMEM((2 * rows, LANES + samples), bf16),
            pltpu.VMEM((windows, 2 * rows, NFFT), bf16),
            pltpu.VMEM((windows, rows, LANES), f32),
        ],
        flops=2 * 2 * rows * samples * 512,
        bytes_accessed=4 * 2**20,
        places="vssv",
    )(strain, fir_taps, spatial, table)
    count = windows * 2 * GROUP // LANES
    pieces = call(
        edge_kernel,
        jax.ShapeDtypeStruct((rep, count + 3, rows, LANES), bf16),
        [
            pltpu.VMEM((4 * HALO, LANES + samples // 2), bf16),
        ],
        flops=2 * 2 * rows * samples * 256,
        bytes_accessed=2 * 2**20,
        places="v" * 9,
    )(near, far, edge, own, lead, edge_mix, filter_matrix, table, direct_matrix)
    arrived = []
    for step in range(1, rep):
        to = [(i, i ^ step if rep & (rep - 1) == 0 else (i + step) % rep) for i in range(rep)]
        arrived.append(lax.ppermute(pieces[step], "rep", to))
    gathered = call(
        merge_kernel,
        jax.ShapeDtypeStruct((rep * count, rows, LANES), bf16),
        flops=2**16,
        bytes_accessed=2**18,
        places="v" * rep,
    )(pieces, *arrived)
    partners = [gathered]
    for step in range(1, STEPS + 1):
        partners.append(lax.ppermute(gathered, "chan", [((i + step) % chan, i) for i in range(chan)]))
    parts = gathered.shape[0]
    left = call(
        left_kernel,
        jax.ShapeDtypeStruct((2, rows * GROUP, parts * LANES), bf16),
        flops=2**20,
        bytes_accessed=2**20,
    )(gathered)
    scale = 1.0 / (windows * rep)
    return call(
        lambda *refs: tile_kernel(scale, *refs),
        jax.ShapeDtypeStruct((rows, STEPS + 1, BINS // rep, 2 * rows), f32),
        flops=2**24,
        bytes_accessed=2**20,
        places="v" * (STEPS + 2),
    )(left, *partners)


def solution(mesh):
    in_specs = (P("chan", "rep"), P(), P())
    out_specs = P("chan", None, "rep", None)
    return jax.shard_map(
        per_device, mesh=mesh, in_specs=in_specs, out_specs=out_specs, check_vma=False
    )
```

```python
import math

import jax
import jax.numpy as jnp
import numpy as np
from jax import lax
from jax.experimental import pallas as pl
from jax.experimental.pallas import tpu as pltpu
from jax.sharding import PartitionSpec as P

NFFT = 1024
BINS = 32
FIRST_BIN = 16
STEPS = 4
LANES = 128
HALO = 4
GROUP = 8

epsilon = 1e-05

f32 = jnp.float32
bf16 = jnp.bfloat16


def dot(a, b):
    return lax.dot_general(a, b, (((1,), (0,)), ((), ())), preferred_element_type=f32)


def dot_t(a, b):
    return lax.dot_general(a, b, (((1,), (1,)), ((), ())), preferred_element_type=f32)


def halves(values):
    high = values.astype(bf16)
    low = (values - high.astype(f32)).astype(bf16)
    return high, low


def dft_table():
    sample = np.arange(NFFT)[:, None]
    bins = FIRST_BIN + np.arange(BINS)[None, :]
    angle = (sample * bins % NFFT) * (2.0 * math.pi / NFFT)
    scale = 1.0 / math.sqrt(NFFT)
    real = (np.cos(angle) * scale).reshape(NFFT, BINS // GROUP, GROUP)
    imag = (-np.sin(angle) * scale).reshape(NFFT, BINS // GROUP, GROUP)
    table = np.concatenate([real, imag], axis=2).reshape(NFFT, 2 * BINS).astype(np.float32)
    high = table.astype(jnp.bfloat16)
    low = (table - high.astype(np.float32)).astype(jnp.bfloat16)
    return np.concatenate([high, low], axis=1)


def toeplitz(taps_ref):
    lane = lax.broadcasted_iota(jnp.int32, (LANES, LANES), 1)
    row = lax.broadcasted_iota(jnp.int32, (LANES, LANES), 0)
    taps = jnp.zeros((1, LANES), f32)
    for k in range(taps_ref.shape[0]):
        taps = jnp.where(lane[:1] == k, taps_ref[k], taps)
    turned = pltpu.roll(jnp.broadcast_to(taps, (LANES, LANES)), 0, 1, stride=1, stride_axis=0)
    parts = [jnp.where(lane < row, turned, 0.0), jnp.where(lane >= row, turned, 0.0)]
    return jnp.concatenate(halves(jnp.concatenate(parts, axis=0)), axis=1)


def mixing(spatial_ref, lag):
    weight = jnp.zeros(lag.shape, f32)
    for j in range(spatial_ref.shape[0]):
        weight = jnp.where(lag == j, spatial_ref[j], weight)
    high = weight.astype(bf16).astype(f32)
    return jnp.concatenate([high, weight - high], axis=0).astype(bf16)


def direct(toeplitz_ref, dft_ref, out_ref):
    lane = lax.broadcasted_iota(jnp.int32, (LANES, LANES), 1)
    left = [toeplitz_ref[:LANES, :LANES], toeplitz_ref[:LANES, LANES:], toeplitz_ref[LANES:, :LANES], toeplitz_ref[LANES:, LANES:]]
    left = jnp.concatenate(left, axis=0)
    carried = jnp.zeros((LANES, LANES), f32)
    for block in range(NFFT // LANES + 1):
        weights = carried
        if block < NFFT // LANES:
            out = dot(left, dft_ref[block * LANES : (block + 1) * LANES, :])
            out = out + pltpu.roll(out, LANES // 2, 1)
            weights = weights + out[:LANES] + out[LANES : 2 * LANES]
            carried = out[2 * LANES : 3 * LANES] + out[3 * LANES :]
        high = weights.astype(bf16).astype(f32)
        part = jnp.where(lane < LANES // 2, high, weights - high)
        out_ref[block * LANES : (block + 1) * LANES, :] = part.astype(bf16)


def edge_weights(spatial_ref, out_ref):
    row = lax.broadcasted_iota(jnp.int32, out_ref.shape[1:], 0) % HALO
    for lag in range(HALO):
        out_ref[lag] = jnp.where(row < HALO - lag, spatial_ref[lag], 0.0)
        out_ref[HALO + lag] = jnp.where(row >= lag, spatial_ref[2 * HALO - lag], 0.0)


def filtered(mixed_ref, first, count, rows, toeplitz_ref):
    parts = []
    for block in range(count):
        start = pl.multiple_of((first + block) * LANES, LANES)
        parts.append(mixed_ref[:, pl.ds(start, 2 * LANES)])
    out = dot(jnp.concatenate(parts, axis=0), toeplitz_ref[...])
    out = out[:, :LANES] + out[:, LANES:]
    out = out.reshape(count, 2, rows, LANES)
    return out[:, 0] + out[:, 1]


def windowed(band, first_window, rows, split_ref, scale_ref):
    per = NFFT // LANES
    count = band.shape[0] // per
    squares = band * band
    for window in range(count):
        total = squares[window * per]
        for block in range(1, per):
            total = total + squares[window * per + block]
        power = jnp.sum(total, axis=1, keepdims=True) * (1.0 / NFFT)
        scale_ref[first_window + window] = jnp.broadcast_to(1.0 / jnp.sqrt(power + epsilon), (rows, LANES))
    high = band.astype(bf16).astype(f32)
    low = band - high
    both = jnp.concatenate([high, low], axis=1).astype(bf16)
    for window in range(count):
        for block in range(per):
            split_ref[first_window + window, :, block * LANES : (block + 1) * LANES] = both[window * per + block]


def remainder(band):
    squares = band * band
    lane = lax.broadcasted_iota(jnp.int32, squares.shape[1:], 1)
    total = jnp.where(lane < LANES // 2, 0.0, squares[0])
    for block in range(1, NFFT // LANES):
        total = total + squares[block]
    return jnp.broadcast_to(jnp.sum(total, axis=1, keepdims=True), total.shape)


def spill_of(mixed, toeplitz_ref):
    rows = mixed.shape[0] // 2
    out = dot(mixed, toeplitz_ref[:LANES, :])
    out = out[:, :LANES] + out[:, LANES:]
    return out[:rows] + out[rows:]


def spectra_of(split_ref, scale_ref, dft_ref, rows):
    windows = split_ref.shape[0]
    out = dot(split_ref[...].reshape(windows * 2 * rows, NFFT), dft_ref[...])
    out = out + pltpu.roll(out, LANES // 2, 1)
    out = out.reshape(windows, 2, rows, LANES)
    return (out[:, 0] + out[:, 1]) * scale_ref[...]


def own_kernel(
    strain_ref,
    taps_ref,
    spatial_ref,
    dft_ref,
    edge_ref,
    spectra_ref,
    lead_ref,
    toeplitz_ref,
    edge_mix_ref,
    direct_ref,
    mixed_ref,
    split_ref,
    scale_ref,
):
    rows, samples = strain_ref.shape
    source = lax.broadcasted_iota(jnp.int32, (rows, rows), 1)
    weights = mixing(spatial_ref, source + HALO - lax.broadcasted_iota(jnp.int32, (rows, rows), 0))
    toeplitz_ref[...] = toeplitz(taps_ref)
    edge_weights(spatial_ref, edge_mix_ref)
    direct(toeplitz_ref, dft_ref, direct_ref)

    def mix(columns):
        out = dot(weights, columns)
        high, low = halves(out[:rows] + out[rows:])
        return jnp.concatenate([high, low], axis=0)

    mixed_ref[:, :LANES] = jnp.zeros((2 * rows, LANES), bf16)
    step = samples // 2

    def mix_step(i, _):
        start = pl.multiple_of(i * step, step)
        mixed_ref[:, pl.ds(pl.multiple_of(start + LANES, LANES), step)] = mix(strain_ref[:, pl.ds(start, step)])
        return 0

    lax.fori_loop(0, samples // step, mix_step, 0)
    count = step // LANES
    near = lax.broadcasted_iota(jnp.int32, (count, rows // 2, LANES), 1) < HALO

    def filter_step(i, _):
        band = filtered(mixed_ref, i * count, count, rows, toeplitz_ref)
        first, last = band[:, : rows // 2], band[:, rows // 2 :]

        @pl.when(i == 0)
        def _():
            edge_ref[:, : rows // 2] = first
            edge_ref[:, rows // 2 :] = pltpu.roll(last, HALO, 1)

        @pl.when(i > 0)
        def _():
            edge_ref[:, : rows // 2] = jnp.where(near, edge_ref[:, : rows // 2], pltpu.roll(first, HALO, 1))
            edge_ref[:, rows // 2 :] = jnp.where(near, edge_ref[:, rows // 2 :], last)

        windowed(band, i * (step // NFFT), rows, split_ref, scale_ref)

        @pl.when(i == 0)
        def _():
            lead_ref[0] = band[0]
            lead_ref[1] = remainder(band[: NFFT // LANES])
            scale_ref[0] = jnp.ones((rows, LANES), f32)

        return 0

    lax.fori_loop(0, samples // step, filter_step, 0)
    row = lax.broadcasted_iota(jnp.int32, scale_ref.shape, 1)
    inside = (row >= HALO) & (row < rows - HALO)
    scale_ref[...] = jnp.where(inside, scale_ref[...], 1.0)
    spectra_ref[...] = spectra_of(split_ref, scale_ref, dft_ref, rows)
    lead_ref[2] = spill_of(mixed_ref[:, samples:], toeplitz_ref)


def whole_block(edges, own):
    rows = edges.shape[1]
    near = lax.broadcasted_iota(jnp.int32, edges.shape, 1) < HALO
    return jnp.concatenate([jnp.where(near, edges, own[:, :rows]), jnp.where(near, own[:, rows:], edges)], axis=1)


def place_of(group, groups):
    here = lax.axis_index("rep")
    return jnp.bitwise_xor(group, here) if groups & (groups - 1) == 0 else lax.rem(group - here + groups, groups)


def edge_kernel(
    near_ref,
    far_ref,
    edge_ref,
    own_ref,
    lead_ref,
    mix_ref,
    toeplitz_ref,
    dft_ref,
    direct_ref,
    out_ref,
    received_ref,
):
    rows = 2 * HALO
    half = near_ref.shape[1] // 2
    even = lax.axis_index("chan") % 2 == 0
    near, far = near_ref[...].astype(f32), far_ref[...].astype(f32)
    pad = jnp.zeros((HALO, LANES), f32)
    parts = []
    for rim in (jnp.where(even, far, near), jnp.where(even, near, far)):
        parts += [jnp.concatenate([pad, rim[:, :half]], axis=1), rim[:, half - LANES :]]
    received_ref[...] = jnp.concatenate(parts, axis=0).astype(bf16)
    low = lax.broadcasted_iota(jnp.int32, (rows, LANES), 0) < HALO

    def mixed(samples):
        first, last = samples[:, :rows], samples[:, rows:]
        out = [first * mix_ref[0], last * mix_ref[HALO]]
        for lag in range(1, HALO):
            out[0] = out[0] + pltpu.roll(first, rows - lag, 1) * mix_ref[lag]
            out[1] = out[1] + pltpu.roll(last, lag, 1) * mix_ref[HALO + lag]
        return jnp.concatenate(out, axis=1)

    def early(values):
        return jnp.where(low, values[:, :rows], pltpu.roll(values[:, rows:], HALO, 1))

    def late(values):
        return jnp.where(low, pltpu.roll(values[:, :rows], HALO, 1), values[:, rows:])

    spans = [received_ref[:, start : start + NFFT + LANES] for start in range(0, half, NFFT)]
    flat = dot(jnp.concatenate(spans, axis=0), direct_ref[...])
    flat = (flat + pltpu.roll(flat, LANES // 2, 1)).reshape(-1, 2 * rows, LANES)
    parts = [received_ref[:, start : start + 2 * LANES] for start in range(0, half, LANES)]
    out = dot(jnp.concatenate(parts, axis=0), toeplitz_ref[...])
    out = (out[:, :LANES] + out[:, LANES:]).reshape(edge_ref.shape)
    band = mixed(out) + edge_ref[...]
    power = jnp.sum((band * band).reshape(-1, NFFT // LANES, 2 * rows, LANES), axis=1)
    power = jnp.concatenate([early(power), late(power)], axis=0)
    power = jnp.sum(power, axis=2, keepdims=True) * (1.0 / NFFT)
    scale = 1.0 / jnp.sqrt(power + epsilon)
    window = lax.broadcasted_iota(jnp.int32, scale.shape, 0)
    scale = jnp.where(window == 0, 1.0, scale)

    edges = mixed(flat)
    edges = jnp.concatenate([early(edges), late(edges)], axis=0)
    own = own_ref[...]
    edges = (edges + jnp.where(low, own[:, :rows], own[:, rows:])) * scale
    spectra = whole_block(edges, own)
    band = early(band[: NFFT // LANES])

    lead = whole_block(jnp.stack([band[0], remainder(band)]), lead_ref[:2])
    spill = dot(received_ref[:, half:], toeplitz_ref[:LANES, :])
    spill = late(mixed((spill[:, :LANES] + spill[:, LANES:])[None]))[0]
    near = lax.broadcasted_iota(jnp.int32, spill.shape, 0) < HALO
    spill = lead_ref[2] + jnp.concatenate([jnp.where(near, spill, 0.0), jnp.where(near, 0.0, spill)], axis=0)
    change = dot(jnp.concatenate(halves(spill), axis=0), dft_ref[:LANES, :])
    change = change[: 2 * rows] + change[2 * rows :]
    change = change + pltpu.roll(change, LANES // 2, 1)

    def parted(values):
        high = values.astype(bf16).astype(f32)
        return high, values - high

    width = 2 * GROUP
    across = LANES // width
    lane = lax.broadcasted_iota(jnp.int32, spectra.shape[1:], 1)
    slot = lane // width
    samples = parted(jnp.where(lane < LANES // 2, lead[0], pltpu.roll(spill, LANES // 2, 1)))
    change = parted(change)
    rest = parted(lead[1])
    groups = out_ref.shape[0]
    for group in range(groups):
        place = place_of(group, groups)

        def moved(value, to):
            shift = (to - group) * width % LANES
            return pltpu.roll(value, shift, 1) if shift else value

        for outer in range(out_ref.shape[1] - 3):
            tile = moved(spectra[outer * across], 0)
            for inner in range(1, across):
                tile = jnp.where(slot == inner, moved(spectra[outer * across + inner], inner), tile)
            out_ref[place, outer] = tile.astype(bf16)
        extra = [parted(moved(spectra[0], 0))[1], moved(change[0], 1), moved(change[1], 2), *rest]
        tile = extra[0]
        for inner in range(1, len(extra)):
            tile = jnp.where(slot == inner, extra[inner], tile)
        for index, value in enumerate((*samples, tile)):
            out_ref[place, out_ref.shape[1] - 3 + index] = value.astype(bf16)


def merge_kernel(pieces_ref, *refs):
    out_ref = refs[-1]
    parts = [pieces_ref.at[0], *(refs[i] for i in (0, 2, 1))]
    count = pieces_ref.shape[1] - 3
    groups = len(parts)
    here = lax.axis_index("rep")
    lane = lax.broadcasted_iota(jnp.int32, pieces_ref.shape[2:], 1)
    width = 2 * GROUP
    reps, leads, spills, rests, raws, changes = [], [], [], [], [], []
    for step, part in enumerate(parts):
        reps.append(jnp.bitwise_xor(here, step) if groups & (groups - 1) == 0 else lax.rem(here - step + groups, groups))
        samples = part[count].astype(f32) + part[count + 1].astype(f32)
        extra = part[count + 2].astype(f32)
        leads.append(jnp.where(lane < LANES // 2, samples, 0.0))
        spills.append(jnp.where(lane < LANES // 2, pltpu.roll(samples, LANES // 2, 1), 0.0))
        raws.append(part[0].astype(f32))
        changes.append(pltpu.roll(extra, LANES - width, 1) + pltpu.roll(extra, LANES - 2 * width, 1))
        rests.append(extra[:, 3 * width : 3 * width + 1] + extra[:, 4 * width : 4 * width + 1])
        raws[-1] = jnp.where(lane < width, raws[-1] + extra, raws[-1])
    for step, part in enumerate(parts):
        spill = jnp.zeros_like(leads[step])
        change = jnp.zeros_like(leads[step])
        for other in range(groups):
            if other != step:
                before = reps[other] == reps[step] - 1
                spill = jnp.where(before, spills[other], spill)
                change = jnp.where(before, changes[other], change)
        lead = leads[step] + spill
        power = (rests[step] + jnp.sum(lead * lead, axis=1, keepdims=True)) * (1.0 / NFFT)
        first = (raws[step] + change) * (1.0 / jnp.sqrt(power + epsilon))
        out_ref[step * count] = jnp.where(lane < width, first, raws[step]).astype(bf16)
        for index in range(1, count):
            out_ref[step * count + index] = part[index]


def rim_kernel(strain_ref, within_ref, across_ref):
    rows = strain_ref.shape[0]
    even = lax.axis_index("chan") % 2 == 0
    head, tail = strain_ref[:HALO], strain_ref[rows - HALO :]
    within_ref[...] = jnp.where(even, tail, head)
    across_ref[...] = jnp.where(even, head, tail)


def left_kernel(own_ref, left_ref):
    parts, rows, _ = own_ref.shape
    lane = lax.broadcasted_iota(jnp.int32, (GROUP, LANES), 1)
    mask = lane % GROUP == lax.broadcasted_iota(jnp.int32, (GROUP, LANES), 0)
    real_lane = lax.broadcasted_iota(jnp.int32, (rows, LANES), 1) % (2 * GROUP) < GROUP

    for part in range(parts):
        value = own_ref[part].astype(f32)
        turned = jnp.where(real_lane, pltpu.roll(value, LANES - GROUP, 1), -pltpu.roll(value, GROUP, 1))
        for half, source in enumerate((value, turned)):
            spread = [jnp.where(mask, jnp.broadcast_to(source[c : c + 1], (GROUP, LANES)), 0.0) for c in range(rows)]
            left_ref[half, :, part * LANES : (part + 1) * LANES] = jnp.concatenate(spread, axis=0).astype(bf16)


def tile_kernel(scale, left_ref, *refs):
    *partner_refs, out_ref, tile_ref, done = refs
    parts, rows, _ = partner_refs[0].shape
    right = jnp.concatenate(
        [jnp.concatenate([ref[part] for part in range(parts)], axis=1) for ref in partner_refs], axis=0
    )
    real = dot_t(left_ref[0], right) * scale
    imag = dot_t(left_ref[1], right) * scale
    copies = []
    span = rows // 2
    for c in range(rows):
        for s in range(len(partner_refs)):
            a = real[c * GROUP : (c + 1) * GROUP, s * rows : (s + 1) * rows]
            b = imag[c * GROUP : (c + 1) * GROUP, s * rows : (s + 1) * rows]
            tile_ref[c, s] = jnp.concatenate([a, b], axis=1)
        if c % span == span - 1:
            run = slice(c + 1 - span, c + 1)
            copies.append(pltpu.make_async_copy(tile_ref.at[run], out_ref.at[run], done.at[c // span]))
            copies[-1].start()
    for copy in copies:
        copy.wait()


def call(kernel, out_shape, scratch=(), flops=0, bytes_accessed=0, places="v", out_specs=None):
    whole = {"v": pl.BlockSpec(memory_space=pltpu.VMEM), "s": pl.BlockSpec(memory_space=pltpu.SMEM)}
    return pl.pallas_call(
        kernel,
        out_shape=out_shape,
        in_specs=[whole[place] for place in places],
        **({} if out_specs is None else {"out_specs": out_specs}),
        scratch_shapes=list(scratch),
        compiler_params=pltpu.CompilerParams(vmem_limit_bytes=32 * 2**20),
        cost_estimate=pl.CostEstimate(flops=flops, bytes_accessed=bytes_accessed, transcendentals=0),
    )


def per_device(strain, fir_taps, spatial):
    rows, samples = strain.shape
    windows = samples // NFFT
    blocks = samples // LANES
    rep = lax.axis_size("rep")
    chan = lax.axis_size("chan")
    even = lax.axis_index("chan") % 2 == 0
    pairs_within = [(i, i ^ 1) for i in range(chan) if i ^ 1 < chan]
    pairs_across = [(i, j) for i in range(chan) for j in (i + 1 if i % 2 else i - 1,) if 0 <= j < chan]

    rim = jax.ShapeDtypeStruct((HALO, samples), bf16)
    within, across = call(rim_kernel, [rim, rim], bytes_accessed=2**20)(strain)
    near = lax.ppermute(within, "chan", pairs_within)
    far = lax.ppermute(across, "chan", pairs_across)

    table = jnp.asarray(dft_table())
    edge, own, lead, filter_matrix, edge_mix, direct_matrix = call(
        own_kernel,
        [
            jax.ShapeDtypeStruct((blocks // 2, rows, LANES), f32),
            jax.ShapeDtypeStruct((windows, rows, LANES), f32),
            jax.ShapeDtypeStruct((3, rows, LANES), f32),
            jax.ShapeDtypeStruct((2 * LANES, 2 * LANES), bf16),
            jax.ShapeDtypeStruct((2 * HALO, 2 * HALO, LANES), f32),
            jax.ShapeDtypeStruct((LANES + NFFT, LANES), bf16),
        ],
        [
            pltpu.VMEM((2 * rows, LANES + samples), bf16),
            pltpu.VMEM((windows, 2 * rows, NFFT), bf16),
            pltpu.VMEM((windows, rows, LANES), f32),
        ],
        flops=2 * 2 * rows * samples * 512,
        bytes_accessed=4 * 2**20,
        places="vssv",
    )(strain, fir_taps, spatial, table)
    count = windows * 2 * GROUP // LANES
    pieces = call(
        edge_kernel,
        jax.ShapeDtypeStruct((rep, count + 3, rows, LANES), bf16),
        [
            pltpu.VMEM((4 * HALO, LANES + samples // 2), bf16),
        ],
        flops=2 * 2 * rows * samples * 256,
        bytes_accessed=2 * 2**20,
        places="v" * 9,
    )(near, far, edge, own, lead, edge_mix, filter_matrix, table, direct_matrix)
    arrived = []
    for step in range(1, rep):
        to = [(i, i ^ step if rep & (rep - 1) == 0 else (i + step) % rep) for i in range(rep)]
        arrived.append(lax.ppermute(pieces[step], "rep", to))
    gathered = call(
        merge_kernel,
        jax.ShapeDtypeStruct((rep * count, rows, LANES), bf16),
        flops=2**16,
        bytes_accessed=2**18,
        places="v" * rep,
    )(pieces, *(arrived[i] for i in (0, 2, 1)))
    partners = [gathered]
    for step in range(1, STEPS + 1):
        partners.append(lax.ppermute(gathered, "chan", [((i + step) % chan, i) for i in range(chan)]))
    parts = gathered.shape[0]
    left = call(
        left_kernel,
        jax.ShapeDtypeStruct((2, rows * GROUP, parts * LANES), bf16),
        flops=2**20,
        bytes_accessed=2**20,
    )(gathered)
    scale = 1.0 / (windows * rep)
    tiles = (rows, STEPS + 1, BINS // rep, 2 * rows)
    return call(
        lambda *refs: tile_kernel(scale, *refs),
        jax.ShapeDtypeStruct(tiles, f32),
        [pltpu.VMEM(tiles, f32), pltpu.SemaphoreType.DMA((2,))],
        out_specs=pl.BlockSpec(memory_space=pl.ANY),
        flops=2**24,
        bytes_accessed=2**20,
        places="v" * (STEPS + 2),
    )(left, *partners)


def solution(mesh):
    in_specs = (P("chan", "rep"), P(), P())
    out_specs = P("chan", None, "rep", None)
    return jax.shard_map(
        per_device, mesh=mesh, in_specs=in_specs, out_specs=out_specs, check_vma=False
    )
```

```python
import functools
import math

import jax
import jax.numpy as jnp
import numpy as np
from jax import lax
from jax.experimental import pallas as pl
from jax.experimental.pallas import tpu as pltpu
from jax.sharding import PartitionSpec as P

NFFT = 1024
BINS = 32
FIRST_BIN = 16
STEPS = 4
LANES = 128
HALO = 4
GROUP = 8

epsilon = 1e-05

f32 = jnp.float32
bf16 = jnp.bfloat16


def dot(a, b):
    return lax.dot_general(a, b, (((1,), (0,)), ((), ())), preferred_element_type=f32)


def dot_t(a, b):
    return lax.dot_general(a, b, (((1,), (1,)), ((), ())), preferred_element_type=f32)


def halves(values):
    high = values.astype(bf16)
    low = (values - high.astype(f32)).astype(bf16)
    return high, low


def dft_table():
    sample = np.arange(NFFT)[:, None]
    bins = FIRST_BIN + np.arange(BINS)[None, :]
    angle = (sample * bins % NFFT) * (2.0 * math.pi / NFFT)
    scale = 1.0 / math.sqrt(NFFT)
    real = (np.cos(angle) * scale).reshape(NFFT, BINS // GROUP, GROUP)
    imag = (-np.sin(angle) * scale).reshape(NFFT, BINS // GROUP, GROUP)
    table = np.concatenate([real, imag], axis=2).reshape(NFFT, 2 * BINS).astype(np.float32)
    high = table.astype(jnp.bfloat16)
    low = (table - high.astype(np.float32)).astype(jnp.bfloat16)
    return np.concatenate([high, low], axis=1)


def toeplitz(taps_ref):
    lane = lax.broadcasted_iota(jnp.int32, (LANES, LANES), 1)
    row = lax.broadcasted_iota(jnp.int32, (LANES, LANES), 0)
    taps = jnp.zeros((1, LANES), f32)
    for k in range(taps_ref.shape[0]):
        taps = jnp.where(lane[:1] == k, taps_ref[k], taps)
    turned = pltpu.roll(jnp.broadcast_to(taps, (LANES, LANES)), 0, 1, stride=1, stride_axis=0)
    parts = [jnp.where(lane < row, turned, 0.0), jnp.where(lane >= row, turned, 0.0)]
    return jnp.concatenate(halves(jnp.concatenate(parts, axis=0)), axis=1)


def mixing(spatial_ref, lag):
    weight = jnp.zeros(lag.shape, f32)
    for j in range(spatial_ref.shape[0]):
        weight = jnp.where(lag == j, spatial_ref[j], weight)
    high = weight.astype(bf16).astype(f32)
    return jnp.concatenate([high, weight - high], axis=0).astype(bf16)


def direct(toeplitz_ref, dft_ref, out_ref):
    lane = lax.broadcasted_iota(jnp.int32, (LANES, LANES), 1)
    left = [toeplitz_ref[:LANES, :LANES], toeplitz_ref[:LANES, LANES:], toeplitz_ref[LANES:, :LANES], toeplitz_ref[LANES:, LANES:]]
    left = jnp.concatenate(left, axis=0)
    carried = jnp.zeros((LANES, LANES), f32)
    for block in range(NFFT // LANES + 1):
        weights = carried
        if block < NFFT // LANES:
            out = dot(left, dft_ref[block * LANES : (block + 1) * LANES, :])
            out = out + pltpu.roll(out, LANES // 2, 1)
            weights = weights + out[:LANES] + out[LANES : 2 * LANES]
            carried = out[2 * LANES : 3 * LANES] + out[3 * LANES :]
        high = weights.astype(bf16).astype(f32)
        part = jnp.where(lane < LANES // 2, high, weights - high)
        out_ref[block * LANES : (block + 1) * LANES, :] = part.astype(bf16)


def edge_weights(spatial_ref, out_ref):
    row = lax.broadcasted_iota(jnp.int32, out_ref.shape[1:], 0) % HALO
    for lag in range(HALO):
        out_ref[lag] = jnp.where(row < HALO - lag, spatial_ref[lag], 0.0)
        out_ref[HALO + lag] = jnp.where(row >= lag, spatial_ref[2 * HALO - lag], 0.0)


def filtered(mixed_ref, first, count, rows, toeplitz_ref):
    parts = []
    for block in range(count):
        start = pl.multiple_of((first + block) * LANES, LANES)
        parts.append(mixed_ref[:, pl.ds(start, 2 * LANES)])
    out = dot(jnp.concatenate(parts, axis=0), toeplitz_ref[...])
    out = out[:, :LANES] + out[:, LANES:]
    out = out.reshape(count, 2, rows, LANES)
    return out[:, 0] + out[:, 1]


def windowed(band, first_window, rows, split_ref, scale_ref):
    per = NFFT // LANES
    count = band.shape[0] // per
    squares = band * band
    for window in range(count):
        total = squares[window * per]
        for block in range(1, per):
            total = total + squares[window * per + block]
        power = jnp.sum(total, axis=1, keepdims=True) * (1.0 / NFFT)
        scale_ref[first_window + window] = jnp.broadcast_to(1.0 / jnp.sqrt(power + epsilon), (rows, LANES))
    high = band.astype(bf16).astype(f32)
    low = band - high
    both = jnp.concatenate([high, low], axis=1).astype(bf16)
    for window in range(count):
        for block in range(per):
            split_ref[first_window + window, :, block * LANES : (block + 1) * LANES] = both[window * per + block]


def remainder(band):
    squares = band * band
    lane = lax.broadcasted_iota(jnp.int32, squares.shape[1:], 1)
    total = jnp.where(lane < LANES // 2, 0.0, squares[0])
    for block in range(1, NFFT // LANES):
        total = total + squares[block]
    return jnp.broadcast_to(jnp.sum(total, axis=1, keepdims=True), total.shape)


def spill_of(mixed, toeplitz_ref):
    rows = mixed.shape[0] // 2
    out = dot(mixed, toeplitz_ref[:LANES, :])
    out = out[:, :LANES] + out[:, LANES:]
    return out[:rows] + out[rows:]


def spectra_of(split_ref, scale_ref, dft_ref, rows):
    windows = split_ref.shape[0]
    out = dot(split_ref[...].reshape(windows * 2 * rows, NFFT), dft_ref[...])
    out = out + pltpu.roll(out, LANES // 2, 1)
    out = out.reshape(windows, 2, rows, LANES)
    return (out[:, 0] + out[:, 1]) * scale_ref[...]


def own_kernel(
    strain_ref,
    taps_ref,
    spatial_ref,
    dft_ref,
    edge_ref,
    spectra_ref,
    lead_ref,
    toeplitz_ref,
    edge_mix_ref,
    direct_ref,
    mixed_ref,
    split_ref,
    scale_ref,
):
    rows, samples = strain_ref.shape
    source = lax.broadcasted_iota(jnp.int32, (rows, rows), 1)
    weights = mixing(spatial_ref, source + HALO - lax.broadcasted_iota(jnp.int32, (rows, rows), 0))
    toeplitz_ref[...] = toeplitz(taps_ref)
    edge_weights(spatial_ref, edge_mix_ref)
    direct(toeplitz_ref, dft_ref, direct_ref)

    def mix(columns):
        out = dot(weights, columns)
        high, low = halves(out[:rows] + out[rows:])
        return jnp.concatenate([high, low], axis=0)

    mixed_ref[:, :LANES] = jnp.zeros((2 * rows, LANES), bf16)
    step = samples // 2

    def mix_step(i, _):
        start = pl.multiple_of(i * step, step)
        mixed_ref[:, pl.ds(pl.multiple_of(start + LANES, LANES), step)] = mix(strain_ref[:, pl.ds(start, step)])
        return 0

    lax.fori_loop(0, samples // step, mix_step, 0)
    count = step // LANES
    near = lax.broadcasted_iota(jnp.int32, (count, rows // 2, LANES), 1) < HALO

    def filter_step(i, _):
        band = filtered(mixed_ref, i * count, count, rows, toeplitz_ref)
        first, last = band[:, : rows // 2], band[:, rows // 2 :]

        @pl.when(i == 0)
        def _():
            edge_ref[:, : rows // 2] = first
            edge_ref[:, rows // 2 :] = pltpu.roll(last, HALO, 1)

        @pl.when(i > 0)
        def _():
            edge_ref[:, : rows // 2] = jnp.where(near, edge_ref[:, : rows // 2], pltpu.roll(first, HALO, 1))
            edge_ref[:, rows // 2 :] = jnp.where(near, edge_ref[:, rows // 2 :], last)

        windowed(band, i * (step // NFFT), rows, split_ref, scale_ref)

        @pl.when(i == 0)
        def _():
            lead_ref[0] = band[0]
            lead_ref[1] = remainder(band[: NFFT // LANES])
            scale_ref[0] = jnp.ones((rows, LANES), f32)

        return 0

    lax.fori_loop(0, samples // step, filter_step, 0)
    row = lax.broadcasted_iota(jnp.int32, scale_ref.shape, 1)
    inside = (row >= HALO) & (row < rows - HALO)
    scale_ref[...] = jnp.where(inside, scale_ref[...], 1.0)
    spectra_ref[...] = spectra_of(split_ref, scale_ref, dft_ref, rows)
    lead_ref[2] = spill_of(mixed_ref[:, samples:], toeplitz_ref)


def whole_block(edges, own):
    rows = edges.shape[1]
    near = lax.broadcasted_iota(jnp.int32, edges.shape, 1) < HALO
    return jnp.concatenate([jnp.where(near, edges, own[:, :rows]), jnp.where(near, own[:, rows:], edges)], axis=1)


def place_of(group, groups):
    here = lax.axis_index("rep")
    return jnp.bitwise_xor(group, here) if groups & (groups - 1) == 0 else lax.rem(group - here + groups, groups)


def edge_kernel(
    near_ref,
    far_ref,
    edge_ref,
    own_ref,
    lead_ref,
    mix_ref,
    toeplitz_ref,
    dft_ref,
    direct_ref,
    out_ref,
    received_ref,
):
    rows = 2 * HALO
    half = near_ref.shape[1] // 2
    even = lax.axis_index("chan") % 2 == 0
    near, far = near_ref[...].astype(f32), far_ref[...].astype(f32)
    pad = jnp.zeros((HALO, LANES), f32)
    parts = []
    for rim in (jnp.where(even, far, near), jnp.where(even, near, far)):
        parts += [jnp.concatenate([pad, rim[:, :half]], axis=1), rim[:, half - LANES :]]
    received_ref[...] = jnp.concatenate(parts, axis=0).astype(bf16)
    low = lax.broadcasted_iota(jnp.int32, (rows, LANES), 0) < HALO

    def mixed(samples):
        first, last = samples[:, :rows], samples[:, rows:]
        out = [first * mix_ref[0], last * mix_ref[HALO]]
        for lag in range(1, HALO):
            out[0] = out[0] + pltpu.roll(first, rows - lag, 1) * mix_ref[lag]
            out[1] = out[1] + pltpu.roll(last, lag, 1) * mix_ref[HALO + lag]
        return jnp.concatenate(out, axis=1)

    def early(values):
        return jnp.where(low, values[:, :rows], pltpu.roll(values[:, rows:], HALO, 1))

    def late(values):
        return jnp.where(low, pltpu.roll(values[:, :rows], HALO, 1), values[:, rows:])

    spans = [received_ref[:, start : start + NFFT + LANES] for start in range(0, half, NFFT)]
    flat = dot(jnp.concatenate(spans, axis=0), direct_ref[...])
    flat = (flat + pltpu.roll(flat, LANES // 2, 1)).reshape(-1, 2 * rows, LANES)
    parts = [received_ref[:, start : start + 2 * LANES] for start in range(0, half, LANES)]
    out = dot(jnp.concatenate(parts, axis=0), toeplitz_ref[...])
    out = (out[:, :LANES] + out[:, LANES:]).reshape(edge_ref.shape)
    band = mixed(out) + edge_ref[...]
    power = jnp.sum((band * band).reshape(-1, NFFT // LANES, 2 * rows, LANES), axis=1)
    power = jnp.concatenate([early(power), late(power)], axis=0)
    power = jnp.sum(power, axis=2, keepdims=True) * (1.0 / NFFT)
    scale = 1.0 / jnp.sqrt(power + epsilon)
    window = lax.broadcasted_iota(jnp.int32, scale.shape, 0)
    scale = jnp.where(window == 0, 1.0, scale)

    edges = mixed(flat)
    edges = jnp.concatenate([early(edges), late(edges)], axis=0)
    own = own_ref[...]
    edges = (edges + jnp.where(low, own[:, :rows], own[:, rows:])) * scale
    spectra = whole_block(edges, own)
    band = early(band[: NFFT // LANES])

    lead = whole_block(jnp.stack([band[0], remainder(band)]), lead_ref[:2])
    spill = dot(received_ref[:, half:], toeplitz_ref[:LANES, :])
    spill = late(mixed((spill[:, :LANES] + spill[:, LANES:])[None]))[0]
    near = lax.broadcasted_iota(jnp.int32, spill.shape, 0) < HALO
    spill = lead_ref[2] + jnp.concatenate([jnp.where(near, spill, 0.0), jnp.where(near, 0.0, spill)], axis=0)
    change = dot(jnp.concatenate(halves(spill), axis=0), dft_ref[:LANES, :])
    change = change[: 2 * rows] + change[2 * rows :]
    change = change + pltpu.roll(change, LANES // 2, 1)

    def parted(values):
        high = values.astype(bf16).astype(f32)
        return high, values - high

    width = 2 * GROUP
    across = LANES // width
    lane = lax.broadcasted_iota(jnp.int32, spectra.shape[1:], 1)
    slot = lane // width
    samples = parted(jnp.where(lane < LANES // 2, lead[0], pltpu.roll(spill, LANES // 2, 1)))
    change = parted(change)
    rest = parted(lead[1])
    groups = out_ref.shape[0]
    for group in range(groups):
        place = place_of(group, groups)

        def moved(value, to):
            shift = (to - group) * width % LANES
            return pltpu.roll(value, shift, 1) if shift else value

        for outer in range(out_ref.shape[1] - 3):
            tile = moved(spectra[outer * across], 0)
            for inner in range(1, across):
                tile = jnp.where(slot == inner, moved(spectra[outer * across + inner], inner), tile)
            out_ref[place, outer] = tile.astype(bf16)
        extra = [parted(moved(spectra[0], 0))[1], moved(change[0], 1), moved(change[1], 2), *rest]
        tile = extra[0]
        for inner in range(1, len(extra)):
            tile = jnp.where(slot == inner, extra[inner], tile)
        for index, value in enumerate((*samples, tile)):
            out_ref[place, out_ref.shape[1] - 3 + index] = value.astype(bf16)


def merge_kernel(pieces_ref, *refs):
    out_ref = refs[-1]
    parts = [pieces_ref.at[0], *(refs[i] for i in (0, 2, 1))]
    count = pieces_ref.shape[1] - 3
    groups = len(parts)
    here = lax.axis_index("rep")
    lane = lax.broadcasted_iota(jnp.int32, pieces_ref.shape[2:], 1)
    width = 2 * GROUP
    reps, leads, spills, rests, raws, changes = [], [], [], [], [], []
    for step, part in enumerate(parts):
        reps.append(jnp.bitwise_xor(here, step) if groups & (groups - 1) == 0 else lax.rem(here - step + groups, groups))
        samples = part[count].astype(f32) + part[count + 1].astype(f32)
        extra = part[count + 2].astype(f32)
        leads.append(jnp.where(lane < LANES // 2, samples, 0.0))
        spills.append(jnp.where(lane < LANES // 2, pltpu.roll(samples, LANES // 2, 1), 0.0))
        raws.append(part[0].astype(f32))
        changes.append(pltpu.roll(extra, LANES - width, 1) + pltpu.roll(extra, LANES - 2 * width, 1))
        rests.append(extra[:, 3 * width : 3 * width + 1] + extra[:, 4 * width : 4 * width + 1])
        raws[-1] = jnp.where(lane < width, raws[-1] + extra, raws[-1])
    for step, part in enumerate(parts):
        spill = jnp.zeros_like(leads[step])
        change = jnp.zeros_like(leads[step])
        for other in range(groups):
            if other != step:
                before = reps[other] == reps[step] - 1
                spill = jnp.where(before, spills[other], spill)
                change = jnp.where(before, changes[other], change)
        lead = leads[step] + spill
        power = (rests[step] + jnp.sum(lead * lead, axis=1, keepdims=True)) * (1.0 / NFFT)
        first = (raws[step] + change) * (1.0 / jnp.sqrt(power + epsilon))
        out_ref[step * count] = jnp.where(lane < width, first, raws[step]).astype(bf16)
        for index in range(1, count):
            out_ref[step * count + index] = part[index]


def rim_kernel(strain_ref, within_ref, across_ref):
    rows = strain_ref.shape[0]
    even = lax.axis_index("chan") % 2 == 0
    head, tail = strain_ref[:HALO], strain_ref[rows - HALO :]
    within_ref[...] = jnp.where(even, tail, head)
    across_ref[...] = jnp.where(even, head, tail)


def left_kernel(own_ref, left_ref):
    parts, rows, _ = own_ref.shape
    values = jnp.concatenate([own_ref[part] for part in range(parts)], axis=1).astype(f32)
    lane = lax.broadcasted_iota(jnp.int32, values.shape, 1)
    width = values.shape[1]
    turned = jnp.where(lane % (2 * GROUP) < GROUP, pltpu.roll(values, width - GROUP, 1), -pltpu.roll(values, GROUP, 1))
    column = lax.broadcasted_iota(jnp.int32, (rows, rows * GROUP), 1)
    spread = jnp.where(column // GROUP == lax.broadcasted_iota(jnp.int32, column.shape, 0), 1.0, 0.0).astype(bf16)
    shape = (width, rows * GROUP)
    mask = lax.broadcasted_iota(jnp.int32, shape, 0) % GROUP == lax.broadcasted_iota(jnp.int32, shape, 1) % GROUP
    for half, source in enumerate((values, turned)):
        out = lax.dot_general(source.astype(bf16), spread, (((0,), (0,)), ((), ())), preferred_element_type=f32)
        left_ref[:, half * shape[1] : (half + 1) * shape[1]] = jnp.where(mask, out, 0.0).astype(bf16)


def tile_kernel(scale, steps, left_ref, *refs):
    partner_refs, (out_ref, tile_ref, done) = refs[: len(steps)], refs[-3:]
    parts, rows, _ = partner_refs[0].shape
    right = jnp.concatenate(
        [jnp.concatenate([ref[part] for part in range(parts)], axis=1) for ref in partner_refs], axis=0
    )
    out = dot(right, left_ref[...]) * scale
    out = jnp.concatenate([out, jnp.zeros((LANES - out.shape[0], out.shape[1]), f32)], axis=0)
    real, imag = out[:, :LANES].T, out[:, LANES:].T
    copies = []
    for index, step in enumerate(steps):
        for c in range(rows):
            a = real[c * GROUP : (c + 1) * GROUP, index * rows : (index + 1) * rows]
            b = imag[c * GROUP : (c + 1) * GROUP, index * rows : (index + 1) * rows]
            tile_ref[index, c] = jnp.concatenate([a, b], axis=1)
        copies.append(pltpu.make_async_copy(tile_ref.at[index], out_ref.at[:, step], done.at[index]))
        copies[-1].start()
    for copy in copies:
        copy.wait()


def call(kernel, out_shape, scratch=(), flops=0, bytes_accessed=0, places="v", out_specs=None, aliases=None):
    whole = {"v": pltpu.VMEM, "s": pltpu.SMEM, "a": pl.ANY}
    whole = {place: pl.BlockSpec(memory_space=space) for place, space in whole.items()}
    return pl.pallas_call(
        kernel,
        out_shape=out_shape,
        in_specs=[whole[place] for place in places],
        **({} if out_specs is None else {"out_specs": out_specs}),
        scratch_shapes=list(scratch),
        input_output_aliases=aliases or {},
        compiler_params=pltpu.CompilerParams(vmem_limit_bytes=32 * 2**20),
        cost_estimate=pl.CostEstimate(flops=flops, bytes_accessed=bytes_accessed, transcendentals=0),
    )


def per_device(strain, fir_taps, spatial):
    rows, samples = strain.shape
    windows = samples // NFFT
    blocks = samples // LANES
    rep = lax.axis_size("rep")
    chan = lax.axis_size("chan")
    even = lax.axis_index("chan") % 2 == 0
    pairs_within = [(i, i ^ 1) for i in range(chan) if i ^ 1 < chan]
    pairs_across = [(i, j) for i in range(chan) for j in (i + 1 if i % 2 else i - 1,) if 0 <= j < chan]

    rim = jax.ShapeDtypeStruct((HALO, samples), bf16)
    within, across = call(rim_kernel, [rim, rim], bytes_accessed=2**20)(strain)
    near = lax.ppermute(within, "chan", pairs_within)
    far = lax.ppermute(across, "chan", pairs_across)

    table = jnp.asarray(dft_table())
    edge, own, lead, filter_matrix, edge_mix, direct_matrix = call(
        own_kernel,
        [
            jax.ShapeDtypeStruct((blocks // 2, rows, LANES), f32),
            jax.ShapeDtypeStruct((windows, rows, LANES), f32),
            jax.ShapeDtypeStruct((3, rows, LANES), f32),
            jax.ShapeDtypeStruct((2 * LANES, 2 * LANES), bf16),
            jax.ShapeDtypeStruct((2 * HALO, 2 * HALO, LANES), f32),
            jax.ShapeDtypeStruct((LANES + NFFT, LANES), bf16),
        ],
        [
            pltpu.VMEM((2 * rows, LANES + samples), bf16),
            pltpu.VMEM((windows, 2 * rows, NFFT), bf16),
            pltpu.VMEM((windows, rows, LANES), f32),
        ],
        flops=2 * 2 * rows * samples * 512,
        bytes_accessed=4 * 2**20,
        places="vssv",
    )(strain, fir_taps, spatial, table)
    count = windows * 2 * GROUP // LANES
    pieces = call(
        edge_kernel,
        jax.ShapeDtypeStruct((rep, count + 3, rows, LANES), bf16),
        [
            pltpu.VMEM((4 * HALO, LANES + samples // 2), bf16),
        ],
        flops=2 * 2 * rows * samples * 256,
        bytes_accessed=2 * 2**20,
        places="v" * 9,
    )(near, far, edge, own, lead, edge_mix, filter_matrix, table, direct_matrix)
    arrived = []
    for step in range(1, rep):
        to = [(i, i ^ step if rep & (rep - 1) == 0 else (i + step) % rep) for i in range(rep)]
        arrived.append(lax.ppermute(pieces[step], "rep", to))
    gathered = call(
        merge_kernel,
        jax.ShapeDtypeStruct((rep * count, rows, LANES), bf16),
        flops=2**16,
        bytes_accessed=2**18,
        places="v" * rep,
    )(pieces, *(arrived[i] for i in (0, 2, 1)))
    partners = [gathered]
    for step in range(1, STEPS + 1):
        partners.append(lax.ppermute(gathered, "chan", [((i + step) % chan, i) for i in range(chan)]))
    parts = gathered.shape[0]
    left = call(
        left_kernel,
        jax.ShapeDtypeStruct((parts * LANES, 2 * rows * GROUP), bf16),
        flops=2**20,
        bytes_accessed=2**20,
    )(gathered)
    scale = 1.0 / (windows * rep)
    tiles = (rows, STEPS + 1, BINS // rep, 2 * rows)

    def tile_call(steps, *before):
        return call(
            functools.partial(tile_kernel, scale, steps),
            jax.ShapeDtypeStruct(tiles, f32),
            [pltpu.VMEM((len(steps), rows, *tiles[2:]), f32), pltpu.SemaphoreType.DMA((len(steps),))],
            flops=2**24,
            bytes_accessed=2**20,
            places="v" * (len(steps) + 1) + "a" * len(before),
            out_specs=pl.BlockSpec(memory_space=pl.ANY),
            aliases={len(steps) + 1: 0} if before else None,
        )(left, *(partners[step] for step in steps), *before)

    return tile_call((1, 2, 3), tile_call((0, 4)))


def solution(mesh):
    in_specs = (P("chan", "rep"), P(), P())
    out_specs = P("chan", None, "rep", None)
    return jax.shard_map(
        per_device, mesh=mesh, in_specs=in_specs, out_specs=out_specs, check_vma=False
    )
```

```python
import functools
import math

import jax
import jax.numpy as jnp
import numpy as np
from jax import lax
from jax.experimental import pallas as pl
from jax.experimental.pallas import tpu as pltpu
from jax.sharding import PartitionSpec as P

NFFT = 1024
BINS = 32
FIRST_BIN = 16
STEPS = 4
LANES = 128
HALO = 4
GROUP = 8

epsilon = 1e-05

f32 = jnp.float32
bf16 = jnp.bfloat16


def dot(a, b):
    return lax.dot_general(a, b, (((1,), (0,)), ((), ())), preferred_element_type=f32)


def dot_t(a, b):
    return lax.dot_general(a, b, (((1,), (1,)), ((), ())), preferred_element_type=f32)


def halves(values):
    high = values.astype(bf16)
    low = (values - high.astype(f32)).astype(bf16)
    return high, low


def dft_table():
    sample = np.arange(NFFT)[:, None]
    bins = FIRST_BIN + np.arange(BINS)[None, :]
    angle = (sample * bins % NFFT) * (2.0 * math.pi / NFFT)
    scale = 1.0 / math.sqrt(NFFT)
    real = (np.cos(angle) * scale).reshape(NFFT, BINS // GROUP, GROUP)
    imag = (-np.sin(angle) * scale).reshape(NFFT, BINS // GROUP, GROUP)
    table = np.concatenate([real, imag], axis=2).reshape(NFFT, 2 * BINS).astype(np.float32)
    high = table.astype(jnp.bfloat16)
    low = (table - high.astype(np.float32)).astype(jnp.bfloat16)
    return np.concatenate([high, low], axis=1)


def toeplitz(taps_ref):
    lane = lax.broadcasted_iota(jnp.int32, (LANES, LANES), 1)
    row = lax.broadcasted_iota(jnp.int32, (LANES, LANES), 0)
    taps = jnp.zeros((1, LANES), f32)
    for k in range(taps_ref.shape[0]):
        taps = jnp.where(lane[:1] == k, taps_ref[k], taps)
    turned = pltpu.roll(jnp.broadcast_to(taps, (LANES, LANES)), 0, 1, stride=1, stride_axis=0)
    parts = [jnp.where(lane < row, turned, 0.0), jnp.where(lane >= row, turned, 0.0)]
    return jnp.concatenate(halves(jnp.concatenate(parts, axis=0)), axis=1)


def mixing(spatial_ref, lag):
    weight = jnp.zeros(lag.shape, f32)
    for j in range(spatial_ref.shape[0]):
        weight = jnp.where(lag == j, spatial_ref[j], weight)
    high = weight.astype(bf16).astype(f32)
    return jnp.concatenate([high, weight - high], axis=0).astype(bf16)


def direct(toeplitz_ref, dft_ref, out_ref):
    lane = lax.broadcasted_iota(jnp.int32, (LANES, LANES), 1)
    left = [toeplitz_ref[:LANES, :LANES], toeplitz_ref[:LANES, LANES:], toeplitz_ref[LANES:, :LANES], toeplitz_ref[LANES:, LANES:]]
    left = jnp.concatenate(left, axis=0)
    carried = jnp.zeros((LANES, LANES), f32)
    for block in range(NFFT // LANES + 1):
        weights = carried
        if block < NFFT // LANES:
            out = dot(left, dft_ref[block * LANES : (block + 1) * LANES, :])
            out = out + pltpu.roll(out, LANES // 2, 1)
            weights = weights + out[:LANES] + out[LANES : 2 * LANES]
            carried = out[2 * LANES : 3 * LANES] + out[3 * LANES :]
        high = weights.astype(bf16).astype(f32)
        part = jnp.where(lane < LANES // 2, high, weights - high)
        out_ref[block * LANES : (block + 1) * LANES, :] = part.astype(bf16)


def edge_weights(spatial_ref, out_ref):
    row = lax.broadcasted_iota(jnp.int32, out_ref.shape[1:], 0) % HALO
    for lag in range(HALO):
        out_ref[lag] = jnp.where(row < HALO - lag, spatial_ref[lag], 0.0)
        out_ref[HALO + lag] = jnp.where(row >= lag, spatial_ref[2 * HALO - lag], 0.0)


def filtered(mixed_ref, first, count, rows, toeplitz_ref):
    parts = []
    for block in range(count):
        start = pl.multiple_of((first + block) * LANES, LANES)
        parts.append(mixed_ref[:, pl.ds(start, 2 * LANES)])
    out = dot(jnp.concatenate(parts, axis=0), toeplitz_ref[...])
    out = out[:, :LANES] + out[:, LANES:]
    out = out.reshape(count, 2, rows, LANES)
    return out[:, 0] + out[:, 1]


def windowed(band, first_window, rows, split_ref, scale_ref):
    per = NFFT // LANES
    count = band.shape[0] // per
    squares = band * band
    for window in range(count):
        total = squares[window * per]
        for block in range(1, per):
            total = total + squares[window * per + block]
        power = jnp.sum(total, axis=1, keepdims=True) * (1.0 / NFFT)
        scale_ref[first_window + window] = jnp.broadcast_to(1.0 / jnp.sqrt(power + epsilon), (rows, LANES))
    high = band.astype(bf16).astype(f32)
    low = band - high
    both = jnp.concatenate([high, low], axis=1).astype(bf16)
    for window in range(count):
        for block in range(per):
            split_ref[first_window + window, :, block * LANES : (block + 1) * LANES] = both[window * per + block]


def remainder(band):
    squares = band * band
    lane = lax.broadcasted_iota(jnp.int32, squares.shape[1:], 1)
    total = jnp.where(lane < LANES // 2, 0.0, squares[0])
    for block in range(1, NFFT // LANES):
        total = total + squares[block]
    return jnp.broadcast_to(jnp.sum(total, axis=1, keepdims=True), total.shape)


def spill_of(mixed, toeplitz_ref):
    rows = mixed.shape[0] // 2
    out = dot(mixed, toeplitz_ref[:LANES, :])
    out = out[:, :LANES] + out[:, LANES:]
    return out[:rows] + out[rows:]


def spectra_of(split_ref, scale_ref, dft_ref, rows):
    windows = split_ref.shape[0]
    out = dot(split_ref[...].reshape(windows * 2 * rows, NFFT), dft_ref[...])
    out = out + pltpu.roll(out, LANES // 2, 1)
    out = out.reshape(windows, 2, rows, LANES)
    return (out[:, 0] + out[:, 1]) * scale_ref[...]


def own_kernel(
    strain_ref,
    taps_ref,
    spatial_ref,
    dft_ref,
    edge_ref,
    spectra_ref,
    lead_ref,
    toeplitz_ref,
    edge_mix_ref,
    direct_ref,
    packed_ref,
    mixed_ref,
    split_ref,
    scale_ref,
):
    rows, samples = strain_ref.shape
    source = lax.broadcasted_iota(jnp.int32, (rows, rows), 1)
    weights = mixing(spatial_ref, source + HALO - lax.broadcasted_iota(jnp.int32, (rows, rows), 0))
    toeplitz_ref[...] = toeplitz(taps_ref)
    edge_weights(spatial_ref, edge_mix_ref)
    direct(toeplitz_ref, dft_ref, direct_ref)

    def mix(columns):
        out = dot(weights, columns)
        high, low = halves(out[:rows] + out[rows:])
        return jnp.concatenate([high, low], axis=0)

    mixed_ref[:, :LANES] = jnp.zeros((2 * rows, LANES), bf16)
    step = samples // 2

    def mix_step(i, _):
        start = pl.multiple_of(i * step, step)
        mixed_ref[:, pl.ds(pl.multiple_of(start + LANES, LANES), step)] = mix(strain_ref[:, pl.ds(start, step)])
        return 0

    lax.fori_loop(0, samples // step, mix_step, 0)
    count = step // LANES
    near = lax.broadcasted_iota(jnp.int32, (count, rows // 2, LANES), 1) < HALO

    def filter_step(i, _):
        band = filtered(mixed_ref, i * count, count, rows, toeplitz_ref)
        first, last = band[:, : rows // 2], band[:, rows // 2 :]

        @pl.when(i == 0)
        def _():
            edge_ref[:, : rows // 2] = first
            edge_ref[:, rows // 2 :] = pltpu.roll(last, HALO, 1)

        @pl.when(i > 0)
        def _():
            edge_ref[:, : rows // 2] = jnp.where(near, edge_ref[:, : rows // 2], pltpu.roll(first, HALO, 1))
            edge_ref[:, rows // 2 :] = jnp.where(near, edge_ref[:, rows // 2 :], last)

        windowed(band, i * (step // NFFT), rows, split_ref, scale_ref)

        @pl.when(i == 0)
        def _():
            lead_ref[0] = band[0]
            lead_ref[1] = remainder(band[: NFFT // LANES])
            scale_ref[0] = jnp.ones((rows, LANES), f32)

        return 0

    lax.fori_loop(0, samples // step, filter_step, 0)
    row = lax.broadcasted_iota(jnp.int32, scale_ref.shape, 1)
    inside = (row >= HALO) & (row < rows - HALO)
    scale_ref[...] = jnp.where(inside, scale_ref[...], 1.0)
    spectra = spectra_of(split_ref, scale_ref, dft_ref, rows)
    spectra_ref[...] = spectra
    groups = packed_ref.shape[0]
    for group in range(groups):
        for outer, tile in enumerate(tiles_of(spectra, group, groups)):
            packed_ref[group, outer] = tile
    lead_ref[2] = spill_of(mixed_ref[:, samples:], toeplitz_ref)


def whole_block(edges, own):
    rows = edges.shape[1]
    near = lax.broadcasted_iota(jnp.int32, edges.shape, 1) < HALO
    return jnp.concatenate([jnp.where(near, edges, own[:, :rows]), jnp.where(near, own[:, rows:], edges)], axis=1)


def place_of(group, groups):
    here = lax.axis_index("rep")
    return jnp.bitwise_xor(group, here) if groups & (groups - 1) == 0 else lax.rem(group - here + groups, groups)


def tiles_of(spectra, group, groups):
    width = 2 * GROUP
    across = LANES // width
    slot = lax.broadcasted_iota(jnp.int32, spectra.shape[1:], 1) // width
    tiles = []
    for first in range(0, spectra.shape[0], across):
        tile = None
        for inner in range(across):
            shift = (inner - group) % groups * width
            value = spectra[first + inner]
            value = pltpu.roll(value, shift, 1) if shift else value
            tile = value if tile is None else jnp.where(slot == inner, value, tile)
        tiles.append(tile)
    return tiles


def edge_kernel(
    near_ref,
    far_ref,
    edge_ref,
    own_ref,
    lead_ref,
    mix_ref,
    toeplitz_ref,
    dft_ref,
    direct_ref,
    packed_ref,
    out_ref,
    received_ref,
):
    rows = 2 * HALO
    half = near_ref.shape[1] // 2
    even = lax.axis_index("chan") % 2 == 0
    near, far = near_ref[...].astype(f32), far_ref[...].astype(f32)
    pad = jnp.zeros((HALO, LANES), f32)
    parts = []
    for rim in (jnp.where(even, far, near), jnp.where(even, near, far)):
        parts += [jnp.concatenate([pad, rim[:, :half]], axis=1), rim[:, half - LANES :]]
    received_ref[...] = jnp.concatenate(parts, axis=0).astype(bf16)
    low = lax.broadcasted_iota(jnp.int32, (rows, LANES), 0) < HALO

    def mixed(samples):
        first, last = samples[:, :rows], samples[:, rows:]
        out = [first * mix_ref[0], last * mix_ref[HALO]]
        for lag in range(1, HALO):
            out[0] = out[0] + pltpu.roll(first, rows - lag, 1) * mix_ref[lag]
            out[1] = out[1] + pltpu.roll(last, lag, 1) * mix_ref[HALO + lag]
        return jnp.concatenate(out, axis=1)

    def early(values):
        return jnp.where(low, values[:, :rows], pltpu.roll(values[:, rows:], HALO, 1))

    def late(values):
        return jnp.where(low, pltpu.roll(values[:, :rows], HALO, 1), values[:, rows:])

    spans = [received_ref[:, start : start + NFFT + LANES] for start in range(0, half, NFFT)]
    flat = dot(jnp.concatenate(spans, axis=0), direct_ref[...])
    flat = (flat + pltpu.roll(flat, LANES // 2, 1)).reshape(-1, 2 * rows, LANES)
    parts = [received_ref[:, start : start + 2 * LANES] for start in range(0, half, LANES)]
    out = dot(jnp.concatenate(parts, axis=0), toeplitz_ref[...])
    out = (out[:, :LANES] + out[:, LANES:]).reshape(edge_ref.shape)
    band = mixed(out) + edge_ref[...]
    power = jnp.sum((band * band).reshape(-1, NFFT // LANES, 2 * rows, LANES), axis=1)
    power = jnp.concatenate([early(power), late(power)], axis=0)
    power = jnp.sum(power, axis=2, keepdims=True) * (1.0 / NFFT)
    scale = 1.0 / jnp.sqrt(power + epsilon)
    window = lax.broadcasted_iota(jnp.int32, scale.shape, 0)
    scale = jnp.where(window == 0, 1.0, scale)

    edges = mixed(flat)
    edges = jnp.concatenate([early(edges), late(edges)], axis=0)
    own = own_ref[...]
    edges = (edges + jnp.where(low, own[:, :rows], own[:, rows:])) * scale
    spectra = whole_block(edges[:1], own[:1])
    band = early(band[: NFFT // LANES])

    lead = whole_block(jnp.stack([band[0], remainder(band)]), lead_ref[:2])
    spill = dot(received_ref[:, half:], toeplitz_ref[:LANES, :])
    spill = late(mixed((spill[:, :LANES] + spill[:, LANES:])[None]))[0]
    near = lax.broadcasted_iota(jnp.int32, spill.shape, 0) < HALO
    spill = lead_ref[2] + jnp.concatenate([jnp.where(near, spill, 0.0), jnp.where(near, 0.0, spill)], axis=0)
    change = dot(jnp.concatenate(halves(spill), axis=0), dft_ref[:LANES, :])
    change = change[: 2 * rows] + change[2 * rows :]
    change = change + pltpu.roll(change, LANES // 2, 1)

    def parted(values):
        high = values.astype(bf16).astype(f32)
        return high, values - high

    width = 2 * GROUP
    lane = lax.broadcasted_iota(jnp.int32, spectra.shape[1:], 1)
    slot = lane // width
    samples = parted(jnp.where(lane < LANES // 2, lead[0], pltpu.roll(spill, LANES // 2, 1)))
    change = parted(change)
    rest = parted(lead[1])
    groups = out_ref.shape[0]
    for group in range(groups):
        place = place_of(group, groups)

        def moved(value, to):
            shift = (to - group) * width % LANES
            return pltpu.roll(value, shift, 1) if shift else value

        for outer, tile in enumerate(tiles_of(edges, group, groups)):
            inside = packed_ref[group, outer]
            whole = [jnp.where(low, tile, inside[:rows]), jnp.where(low, inside[rows:], tile)]
            out_ref[place, outer] = jnp.concatenate(whole, axis=0).astype(bf16)
        extra = [parted(moved(spectra[0], 0))[1], moved(change[0], 1), moved(change[1], 2), *rest]
        tile = extra[0]
        for inner in range(1, len(extra)):
            tile = jnp.where(slot == inner, extra[inner], tile)
        for index, value in enumerate((*samples, tile)):
            out_ref[place, out_ref.shape[1] - 3 + index] = value.astype(bf16)


def merge_kernel(pieces_ref, *refs):
    out_ref = refs[-1]
    parts = [pieces_ref.at[0], *(refs[i] for i in (0, 2, 1))]
    count = pieces_ref.shape[1] - 3
    groups = len(parts)
    here = lax.axis_index("rep")
    lane = lax.broadcasted_iota(jnp.int32, pieces_ref.shape[2:], 1)
    width = 2 * GROUP
    reps, leads, spills, rests, raws, changes = [], [], [], [], [], []
    for step, part in enumerate(parts):
        reps.append(jnp.bitwise_xor(here, step) if groups & (groups - 1) == 0 else lax.rem(here - step + groups, groups))
        samples = part[count].astype(f32) + part[count + 1].astype(f32)
        extra = part[count + 2].astype(f32)
        leads.append(jnp.where(lane < LANES // 2, samples, 0.0))
        spills.append(jnp.where(lane < LANES // 2, pltpu.roll(samples, LANES // 2, 1), 0.0))
        raws.append(part[0].astype(f32))
        changes.append(pltpu.roll(extra, LANES - width, 1) + pltpu.roll(extra, LANES - 2 * width, 1))
        rests.append(extra[:, 3 * width : 3 * width + 1] + extra[:, 4 * width : 4 * width + 1])
        raws[-1] = jnp.where(lane < width, raws[-1] + extra, raws[-1])
    for step, part in enumerate(parts):
        spill = jnp.zeros_like(leads[step])
        change = jnp.zeros_like(leads[step])
        for other in range(groups):
            if other != step:
                before = reps[other] == reps[step] - 1
                spill = jnp.where(before, spills[other], spill)
                change = jnp.where(before, changes[other], change)
        lead = leads[step] + spill
        power = (rests[step] + jnp.sum(lead * lead, axis=1, keepdims=True)) * (1.0 / NFFT)
        first = (raws[step] + change) * (1.0 / jnp.sqrt(power + epsilon))
        out_ref[step * count] = jnp.where(lane < width, first, raws[step]).astype(bf16)
        for index in range(1, count):
            out_ref[step * count + index] = part[index]


def rim_kernel(strain_ref, within_ref, across_ref):
    rows = strain_ref.shape[0]
    even = lax.axis_index("chan") % 2 == 0
    head, tail = strain_ref[:HALO], strain_ref[rows - HALO :]
    within_ref[...] = jnp.where(even, tail, head)
    across_ref[...] = jnp.where(even, head, tail)


def left_kernel(own_ref, left_ref):
    parts, rows, _ = own_ref.shape
    values = jnp.concatenate([own_ref[part] for part in range(parts)], axis=1).astype(f32)
    lane = lax.broadcasted_iota(jnp.int32, values.shape, 1)
    width = values.shape[1]
    turned = jnp.where(lane % (2 * GROUP) < GROUP, pltpu.roll(values, width - GROUP, 1), -pltpu.roll(values, GROUP, 1))
    column = lax.broadcasted_iota(jnp.int32, (rows, rows * GROUP), 1)
    spread = jnp.where(column // GROUP == lax.broadcasted_iota(jnp.int32, column.shape, 0), 1.0, 0.0).astype(bf16)
    shape = (width, rows * GROUP)
    mask = lax.broadcasted_iota(jnp.int32, shape, 0) % GROUP == lax.broadcasted_iota(jnp.int32, shape, 1) % GROUP
    for half, source in enumerate((values, turned)):
        out = lax.dot_general(source.astype(bf16), spread, (((0,), (0,)), ((), ())), preferred_element_type=f32)
        left_ref[:, half * shape[1] : (half + 1) * shape[1]] = jnp.where(mask, out, 0.0).astype(bf16)


def tile_kernel(scale, steps, left_ref, *refs):
    partner_refs, (out_ref, tile_ref, done) = refs[: len(steps)], refs[-3:]
    parts, rows, _ = partner_refs[0].shape
    right = jnp.concatenate(
        [jnp.concatenate([ref[part] for part in range(parts)], axis=1) for ref in partner_refs], axis=0
    )
    out = dot(right, left_ref[...]) * scale
    out = jnp.concatenate([out, jnp.zeros((LANES - out.shape[0], out.shape[1]), f32)], axis=0)
    real, imag = out[:, :LANES].T, out[:, LANES:].T
    copies = []
    for index, step in enumerate(steps):
        for c in range(rows):
            a = real[c * GROUP : (c + 1) * GROUP, index * rows : (index + 1) * rows]
            b = imag[c * GROUP : (c + 1) * GROUP, index * rows : (index + 1) * rows]
            tile_ref[index, c] = jnp.concatenate([a, b], axis=1)
        copies.append(pltpu.make_async_copy(tile_ref.at[index], out_ref.at[:, step], done.at[index]))
        copies[-1].start()
    for copy in copies:
        copy.wait()


def call(kernel, out_shape, scratch=(), flops=0, bytes_accessed=0, places="v", out_specs=None, aliases=None):
    whole = {"v": pltpu.VMEM, "s": pltpu.SMEM, "a": pl.ANY}
    whole = {place: pl.BlockSpec(memory_space=space) for place, space in whole.items()}
    return pl.pallas_call(
        kernel,
        out_shape=out_shape,
        in_specs=[whole[place] for place in places],
        **({} if out_specs is None else {"out_specs": out_specs}),
        scratch_shapes=list(scratch),
        input_output_aliases=aliases or {},
        compiler_params=pltpu.CompilerParams(vmem_limit_bytes=32 * 2**20),
        cost_estimate=pl.CostEstimate(flops=flops, bytes_accessed=bytes_accessed, transcendentals=0),
    )


def per_device(strain, fir_taps, spatial):
    rows, samples = strain.shape
    windows = samples // NFFT
    blocks = samples // LANES
    rep = lax.axis_size("rep")
    chan = lax.axis_size("chan")
    even = lax.axis_index("chan") % 2 == 0
    pairs_within = [(i, i ^ 1) for i in range(chan) if i ^ 1 < chan]
    pairs_across = [(i, j) for i in range(chan) for j in (i + 1 if i % 2 else i - 1,) if 0 <= j < chan]

    rim = jax.ShapeDtypeStruct((HALO, samples), bf16)
    within, across = call(rim_kernel, [rim, rim], bytes_accessed=2**20)(strain)
    near = lax.ppermute(within, "chan", pairs_within)
    far = lax.ppermute(across, "chan", pairs_across)

    table = jnp.asarray(dft_table())
    edge, own, lead, filter_matrix, edge_mix, direct_matrix, inside = call(
        own_kernel,
        [
            jax.ShapeDtypeStruct((blocks // 2, rows, LANES), f32),
            jax.ShapeDtypeStruct((windows, rows, LANES), f32),
            jax.ShapeDtypeStruct((3, rows, LANES), f32),
            jax.ShapeDtypeStruct((2 * LANES, 2 * LANES), bf16),
            jax.ShapeDtypeStruct((2 * HALO, 2 * HALO, LANES), f32),
            jax.ShapeDtypeStruct((LANES + NFFT, LANES), bf16),
            jax.ShapeDtypeStruct((rep, windows * 2 * GROUP // LANES, rows, LANES), f32),
        ],
        [
            pltpu.VMEM((2 * rows, LANES + samples), bf16),
            pltpu.VMEM((windows, 2 * rows, NFFT), bf16),
            pltpu.VMEM((windows, rows, LANES), f32),
        ],
        flops=2 * 2 * rows * samples * 512,
        bytes_accessed=4 * 2**20,
        places="vssv",
    )(strain, fir_taps, spatial, table)
    count = windows * 2 * GROUP // LANES
    pieces = call(
        edge_kernel,
        jax.ShapeDtypeStruct((rep, count + 3, rows, LANES), bf16),
        [
            pltpu.VMEM((4 * HALO, LANES + samples // 2), bf16),
        ],
        flops=2 * 2 * rows * samples * 256,
        bytes_accessed=2 * 2**20,
        places="v" * 10,
    )(near, far, edge, own, lead, edge_mix, filter_matrix, table, direct_matrix, inside)
    arrived = []
    for step in range(1, rep):
        to = [(i, i ^ step if rep & (rep - 1) == 0 else (i + step) % rep) for i in range(rep)]
        arrived.append(lax.ppermute(pieces[step], "rep", to))
    gathered = call(
        merge_kernel,
        jax.ShapeDtypeStruct((rep * count, rows, LANES), bf16),
        flops=2**16,
        bytes_accessed=2**18,
        places="v" * rep,
    )(pieces, *(arrived[i] for i in (0, 2, 1)))
    partners = [gathered]
    for step in range(1, STEPS + 1):
        partners.append(lax.ppermute(gathered, "chan", [((i + step) % chan, i) for i in range(chan)]))
    parts = gathered.shape[0]
    left = call(
        left_kernel,
        jax.ShapeDtypeStruct((parts * LANES, 2 * rows * GROUP), bf16),
        flops=2**20,
        bytes_accessed=2**20,
    )(gathered)
    scale = 1.0 / (windows * rep)
    tiles = (rows, STEPS + 1, BINS // rep, 2 * rows)

    def tile_call(steps, *before):
        return call(
            functools.partial(tile_kernel, scale, steps),
            jax.ShapeDtypeStruct(tiles, f32),
            [pltpu.VMEM((len(steps), rows, *tiles[2:]), f32), pltpu.SemaphoreType.DMA((len(steps),))],
            flops=2**24,
            bytes_accessed=2**20,
            places="v" * (len(steps) + 1) + "a" * len(before),
            out_specs=pl.BlockSpec(memory_space=pl.ANY),
            aliases={len(steps) + 1: 0} if before else None,
        )(left, *(partners[step] for step in steps), *before)

    return tile_call((1, 2, 3), tile_call((0, 4)))


def solution(mesh):
    in_specs = (P("chan", "rep"), P(), P())
    out_specs = P("chan", None, "rep", None)
    return jax.shard_map(
        per_device, mesh=mesh, in_specs=in_specs, out_specs=out_specs, check_vma=False
    )
```

```python
import math

import jax
import jax.numpy as jnp
import numpy as np
from jax import lax
from jax.experimental import pallas as pl
from jax.experimental.pallas import tpu as pltpu
from jax.sharding import PartitionSpec as P

NFFT = 1024
BINS = 32
FIRST_BIN = 16
STEPS = 4
LANES = 128
HALO = 4
GROUP = 8

epsilon = 1e-05

f32 = jnp.float32
bf16 = jnp.bfloat16


def dot(a, b):
    return lax.dot_general(a, b, (((1,), (0,)), ((), ())), preferred_element_type=f32)


def dot_t(a, b):
    return lax.dot_general(a, b, (((1,), (1,)), ((), ())), preferred_element_type=f32)


def halves(values):
    high = values.astype(bf16)
    low = (values - high.astype(f32)).astype(bf16)
    return high, low


def dft_table():
    sample = np.arange(NFFT)[:, None]
    bins = FIRST_BIN + np.arange(BINS)[None, :]
    angle = (sample * bins % NFFT) * (2.0 * math.pi / NFFT)
    scale = 1.0 / math.sqrt(NFFT)
    real = (np.cos(angle) * scale).reshape(NFFT, BINS // GROUP, GROUP)
    imag = (-np.sin(angle) * scale).reshape(NFFT, BINS // GROUP, GROUP)
    table = np.concatenate([real, imag], axis=2).reshape(NFFT, 2 * BINS).astype(np.float32)
    high = table.astype(jnp.bfloat16)
    low = (table - high.astype(np.float32)).astype(jnp.bfloat16)
    return np.concatenate([high, low], axis=1)


def toeplitz(taps_ref):
    lane = lax.broadcasted_iota(jnp.int32, (LANES, LANES), 1)
    row = lax.broadcasted_iota(jnp.int32, (LANES, LANES), 0)
    taps = jnp.zeros((1, LANES), f32)
    for k in range(taps_ref.shape[0]):
        taps = jnp.where(lane[:1] == k, taps_ref[k], taps)
    turned = pltpu.roll(jnp.broadcast_to(taps, (LANES, LANES)), 0, 1, stride=1, stride_axis=0)
    parts = [jnp.where(lane < row, turned, 0.0), jnp.where(lane >= row, turned, 0.0)]
    return jnp.concatenate(halves(jnp.concatenate(parts, axis=0)), axis=1)


def mixing(spatial_ref, lag):
    weight = jnp.zeros(lag.shape, f32)
    for j in range(spatial_ref.shape[0]):
        weight = jnp.where(lag == j, spatial_ref[j], weight)
    high = weight.astype(bf16).astype(f32)
    return jnp.concatenate([high, weight - high], axis=0).astype(bf16)


def direct(toeplitz_ref, dft_ref, out_ref):
    lane = lax.broadcasted_iota(jnp.int32, (LANES, LANES), 1)
    left = [toeplitz_ref[:LANES, :LANES], toeplitz_ref[:LANES, LANES:], toeplitz_ref[LANES:, :LANES], toeplitz_ref[LANES:, LANES:]]
    left = jnp.concatenate(left, axis=0)
    carried = jnp.zeros((LANES, LANES), f32)
    for block in range(NFFT // LANES + 1):
        weights = carried
        if block < NFFT // LANES:
            out = dot(left, dft_ref[block * LANES : (block + 1) * LANES, :])
            out = out + pltpu.roll(out, LANES // 2, 1)
            weights = weights + out[:LANES] + out[LANES : 2 * LANES]
            carried = out[2 * LANES : 3 * LANES] + out[3 * LANES :]
        high = weights.astype(bf16).astype(f32)
        part = jnp.where(lane < LANES // 2, high, weights - high)
        out_ref[block * LANES : (block + 1) * LANES, :] = part.astype(bf16)


def edge_weights(spatial_ref, out_ref):
    row = lax.broadcasted_iota(jnp.int32, out_ref.shape[1:], 0) % HALO
    for lag in range(HALO):
        out_ref[lag] = jnp.where(row < HALO - lag, spatial_ref[lag], 0.0)
        out_ref[HALO + lag] = jnp.where(row >= lag, spatial_ref[2 * HALO - lag], 0.0)


def filtered(mixed_ref, first, count, rows, toeplitz_ref):
    parts = []
    for block in range(count):
        start = pl.multiple_of((first + block) * LANES, LANES)
        parts.append(mixed_ref[:, pl.ds(start, 2 * LANES)])
    out = dot(jnp.concatenate(parts, axis=0), toeplitz_ref[...])
    out = out[:, :LANES] + out[:, LANES:]
    out = out.reshape(count, 2, rows, LANES)
    return out[:, 0] + out[:, 1]


def windowed(band, first_window, rows, split_ref, scale_ref):
    per = NFFT // LANES
    count = band.shape[0] // per
    squares = band * band
    for window in range(count):
        total = squares[window * per]
        for block in range(1, per):
            total = total + squares[window * per + block]
        power = jnp.sum(total, axis=1, keepdims=True) * (1.0 / NFFT)
        scale_ref[first_window + window] = jnp.broadcast_to(1.0 / jnp.sqrt(power + epsilon), (rows, LANES))
    high = band.astype(bf16).astype(f32)
    low = band - high
    both = jnp.concatenate([high, low], axis=1).astype(bf16)
    for window in range(count):
        for block in range(per):
            split_ref[first_window + window, :, block * LANES : (block + 1) * LANES] = both[window * per + block]


def remainder(band):
    squares = band * band
    lane = lax.broadcasted_iota(jnp.int32, squares.shape[1:], 1)
    total = jnp.where(lane < LANES // 2, 0.0, squares[0])
    for block in range(1, NFFT // LANES):
        total = total + squares[block]
    return jnp.broadcast_to(jnp.sum(total, axis=1, keepdims=True), total.shape)


def spill_of(mixed, toeplitz_ref):
    rows = mixed.shape[0] // 2
    out = dot(mixed, toeplitz_ref[:LANES, :])
    out = out[:, :LANES] + out[:, LANES:]
    return out[:rows] + out[rows:]


def spectra_of(split_ref, scale_ref, dft_ref, rows):
    windows = split_ref.shape[0]
    out = dot(split_ref[...].reshape(windows * 2 * rows, NFFT), dft_ref[...])
    out = out + pltpu.roll(out, LANES // 2, 1)
    out = out.reshape(windows, 2, rows, LANES)
    return (out[:, 0] + out[:, 1]) * scale_ref[...]


def own_kernel(
    strain_ref,
    taps_ref,
    spatial_ref,
    dft_ref,
    edge_ref,
    spectra_ref,
    lead_ref,
    toeplitz_ref,
    edge_mix_ref,
    direct_ref,
    mixed_ref,
    split_ref,
    scale_ref,
):
    rows, samples = strain_ref.shape
    source = lax.broadcasted_iota(jnp.int32, (rows, rows), 1)
    weights = mixing(spatial_ref, source + HALO - lax.broadcasted_iota(jnp.int32, (rows, rows), 0))
    toeplitz_ref[...] = toeplitz(taps_ref)
    edge_weights(spatial_ref, edge_mix_ref)
    direct(toeplitz_ref, dft_ref, direct_ref)

    def mix(columns):
        out = dot(weights, columns)
        high, low = halves(out[:rows] + out[rows:])
        return jnp.concatenate([high, low], axis=0)

    mixed_ref[:, :LANES] = jnp.zeros((2 * rows, LANES), bf16)
    step = samples // 2

    def mix_step(i, _):
        start = pl.multiple_of(i * step, step)
        mixed_ref[:, pl.ds(pl.multiple_of(start + LANES, LANES), step)] = mix(strain_ref[:, pl.ds(start, step)])
        return 0

    lax.fori_loop(0, samples // step, mix_step, 0)
    count = step // LANES
    near = lax.broadcasted_iota(jnp.int32, (count, rows // 2, LANES), 1) < HALO

    def filter_step(i, _):
        band = filtered(mixed_ref, i * count, count, rows, toeplitz_ref)
        first, last = band[:, : rows // 2], band[:, rows // 2 :]

        @pl.when(i == 0)
        def _():
            edge_ref[:, : rows // 2] = first
            edge_ref[:, rows // 2 :] = pltpu.roll(last, HALO, 1)

        @pl.when(i > 0)
        def _():
            edge_ref[:, : rows // 2] = jnp.where(near, edge_ref[:, : rows // 2], pltpu.roll(first, HALO, 1))
            edge_ref[:, rows // 2 :] = jnp.where(near, edge_ref[:, rows // 2 :], last)

        windowed(band, i * (step // NFFT), rows, split_ref, scale_ref)

        @pl.when(i == 0)
        def _():
            lead_ref[0] = band[0]
            lead_ref[1] = remainder(band[: NFFT // LANES])
            scale_ref[0] = jnp.ones((rows, LANES), f32)

        return 0

    lax.fori_loop(0, samples // step, filter_step, 0)
    row = lax.broadcasted_iota(jnp.int32, scale_ref.shape, 1)
    inside = (row >= HALO) & (row < rows - HALO)
    scale_ref[...] = jnp.where(inside, scale_ref[...], 1.0)
    spectra_ref[...] = spectra_of(split_ref, scale_ref, dft_ref, rows)
    lead_ref[2] = spill_of(mixed_ref[:, samples:], toeplitz_ref)


def whole_block(edges, own):
    rows = edges.shape[1]
    near = lax.broadcasted_iota(jnp.int32, edges.shape, 1) < HALO
    return jnp.concatenate([jnp.where(near, edges, own[:, :rows]), jnp.where(near, own[:, rows:], edges)], axis=1)


def place_of(group, groups):
    here = lax.axis_index("rep")
    return jnp.bitwise_xor(group, here) if groups & (groups - 1) == 0 else lax.rem(group - here + groups, groups)


def edge_kernel(
    far_ref,
    near_ref,
    edge_ref,
    own_ref,
    lead_ref,
    mix_ref,
    toeplitz_ref,
    dft_ref,
    direct_ref,
    out_ref,
    received_ref,
):
    rows = 2 * HALO
    half = near_ref.shape[1] // 2
    even = lax.axis_index("chan") % 2 == 0
    near, far = near_ref[...].astype(f32), far_ref[...].astype(f32)
    pad = jnp.zeros((HALO, LANES), f32)
    parts = []
    for rim in (jnp.where(even, far, near), jnp.where(even, near, far)):
        parts += [jnp.concatenate([pad, rim[:, :half]], axis=1), rim[:, half - LANES :]]
    received_ref[...] = jnp.concatenate(parts, axis=0).astype(bf16)
    low = lax.broadcasted_iota(jnp.int32, (rows, LANES), 0) < HALO

    def mixed(samples):
        first, last = samples[:, :rows], samples[:, rows:]
        out = [first * mix_ref[0], last * mix_ref[HALO]]
        for lag in range(1, HALO):
            out[0] = out[0] + pltpu.roll(first, rows - lag, 1) * mix_ref[lag]
            out[1] = out[1] + pltpu.roll(last, lag, 1) * mix_ref[HALO + lag]
        return jnp.concatenate(out, axis=1)

    def early(values):
        return jnp.where(low, values[:, :rows], pltpu.roll(values[:, rows:], HALO, 1))

    def late(values):
        return jnp.where(low, pltpu.roll(values[:, :rows], HALO, 1), values[:, rows:])

    spans = [received_ref[:, start : start + NFFT + LANES] for start in range(0, half, NFFT)]
    flat = dot(jnp.concatenate(spans, axis=0), direct_ref[...])
    flat = (flat + pltpu.roll(flat, LANES // 2, 1)).reshape(-1, 2 * rows, LANES)
    parts = [received_ref[:, start : start + 2 * LANES] for start in range(0, half, LANES)]
    out = dot(jnp.concatenate(parts, axis=0), toeplitz_ref[...])
    out = (out[:, :LANES] + out[:, LANES:]).reshape(edge_ref.shape)
    band = mixed(out) + edge_ref[...]
    power = jnp.sum((band * band).reshape(-1, NFFT // LANES, 2 * rows, LANES), axis=1)
    power = jnp.concatenate([early(power), late(power)], axis=0)
    power = jnp.sum(power, axis=2, keepdims=True) * (1.0 / NFFT)
    scale = 1.0 / jnp.sqrt(power + epsilon)
    window = lax.broadcasted_iota(jnp.int32, scale.shape, 0)
    scale = jnp.where(window == 0, 1.0, scale)

    edges = mixed(flat)
    edges = jnp.concatenate([early(edges), late(edges)], axis=0)
    own = own_ref[...]
    edges = (edges + jnp.where(low, own[:, :rows], own[:, rows:])) * scale
    spectra = whole_block(edges, own)
    band = early(band[: NFFT // LANES])

    lead = whole_block(jnp.stack([band[0], remainder(band)]), lead_ref[:2])
    spill = dot(received_ref[:, half:], toeplitz_ref[:LANES, :])
    spill = late(mixed((spill[:, :LANES] + spill[:, LANES:])[None]))[0]
    near = lax.broadcasted_iota(jnp.int32, spill.shape, 0) < HALO
    spill = lead_ref[2] + jnp.concatenate([jnp.where(near, spill, 0.0), jnp.where(near, 0.0, spill)], axis=0)
    change = dot(jnp.concatenate(halves(spill), axis=0), dft_ref[:LANES, :])
    change = change[: 2 * rows] + change[2 * rows :]
    change = change + pltpu.roll(change, LANES // 2, 1)

    def parted(values):
        high = values.astype(bf16).astype(f32)
        return high, values - high

    width = 2 * GROUP
    across = LANES // width
    lane = lax.broadcasted_iota(jnp.int32, spectra.shape[1:], 1)
    slot = lane // width
    samples = parted(jnp.where(lane < LANES // 2, lead[0], pltpu.roll(spill, LANES // 2, 1)))
    change = parted(change)
    rest = parted(lead[1])
    groups = out_ref.shape[0]
    for group in range(groups):
        place = place_of(group, groups)

        def moved(value, to):
            shift = (to - group) * width % LANES
            return pltpu.roll(value, shift, 1) if shift else value

        for outer in range(out_ref.shape[1] - 3):
            tile = moved(spectra[outer * across], 0)
            for inner in range(1, across):
                tile = jnp.where(slot == inner, moved(spectra[outer * across + inner], inner), tile)
            out_ref[place, outer] = tile.astype(bf16)
        extra = [parted(moved(spectra[0], 0))[1], moved(change[0], 1), moved(change[1], 2), *rest]
        tile = extra[0]
        for inner in range(1, len(extra)):
            tile = jnp.where(slot == inner, extra[inner], tile)
        for index, value in enumerate((*samples, tile)):
            out_ref[place, out_ref.shape[1] - 3 + index] = value.astype(bf16)


def merge_kernel(pieces_ref, *refs):
    out_ref = refs[-1]
    parts = [pieces_ref.at[0], *(refs[i] for i in (0, 2, 1))]
    count = pieces_ref.shape[1] - 3
    groups = len(parts)
    here = lax.axis_index("rep")
    lane = lax.broadcasted_iota(jnp.int32, pieces_ref.shape[2:], 1)
    width = 2 * GROUP
    reps, leads, spills, rests, raws, changes = [], [], [], [], [], []
    for step, part in enumerate(parts):
        reps.append(jnp.bitwise_xor(here, step) if groups & (groups - 1) == 0 else lax.rem(here - step + groups, groups))
        samples = part[count].astype(f32) + part[count + 1].astype(f32)
        extra = part[count + 2].astype(f32)
        leads.append(jnp.where(lane < LANES // 2, samples, 0.0))
        spills.append(jnp.where(lane < LANES // 2, pltpu.roll(samples, LANES // 2, 1), 0.0))
        raws.append(part[0].astype(f32))
        changes.append(pltpu.roll(extra, LANES - width, 1) + pltpu.roll(extra, LANES - 2 * width, 1))
        rests.append(extra[:, 3 * width : 3 * width + 1] + extra[:, 4 * width : 4 * width + 1])
        raws[-1] = jnp.where(lane < width, raws[-1] + extra, raws[-1])
    for step, part in enumerate(parts):
        spill = jnp.zeros_like(leads[step])
        change = jnp.zeros_like(leads[step])
        for other in range(groups):
            if other != step:
                before = reps[other] == reps[step] - 1
                spill = jnp.where(before, spills[other], spill)
                change = jnp.where(before, changes[other], change)
        lead = leads[step] + spill
        power = (rests[step] + jnp.sum(lead * lead, axis=1, keepdims=True)) * (1.0 / NFFT)
        first = (raws[step] + change) * (1.0 / jnp.sqrt(power + epsilon))
        out_ref[step * count] = jnp.where(lane < width, first, raws[step]).astype(bf16)
        for index in range(1, count):
            out_ref[step * count + index] = part[index]


def rim_kernel(last_if_even, strain_ref, *refs):
    rim_ref = refs[-1]
    rows = strain_ref.shape[0]
    last = (lax.axis_index("chan") % 2 == 0) == last_if_even
    rim_ref[...] = jnp.where(last, strain_ref[rows - HALO :], strain_ref[:HALO])


def left_kernel(own_ref, left_ref):
    parts, rows, _ = own_ref.shape
    lane = lax.broadcasted_iota(jnp.int32, (GROUP, LANES), 1)
    mask = lane % GROUP == lax.broadcasted_iota(jnp.int32, (GROUP, LANES), 0)
    real_lane = lax.broadcasted_iota(jnp.int32, (rows, LANES), 1) % (2 * GROUP) < GROUP

    for part in range(parts):
        value = own_ref[part].astype(f32)
        turned = jnp.where(real_lane, pltpu.roll(value, LANES - GROUP, 1), -pltpu.roll(value, GROUP, 1))
        for half, source in enumerate((value, turned)):
            spread = [jnp.where(mask, jnp.broadcast_to(source[c : c + 1], (GROUP, LANES)), 0.0) for c in range(rows)]
            left_ref[half, :, part * LANES : (part + 1) * LANES] = jnp.concatenate(spread, axis=0).astype(bf16)


def tile_kernel(scale, left_ref, *refs):
    *partner_refs, out_ref, tile_ref, done = refs
    parts, rows, _ = partner_refs[0].shape
    right = jnp.concatenate(
        [jnp.concatenate([ref[part] for part in range(parts)], axis=1) for ref in partner_refs], axis=0
    )
    real = dot_t(left_ref[0], right) * scale
    imag = dot_t(left_ref[1], right) * scale
    copies = []
    span = rows // 2
    for c in range(rows):
        for s in range(len(partner_refs)):
            a = real[c * GROUP : (c + 1) * GROUP, s * rows : (s + 1) * rows]
            b = imag[c * GROUP : (c + 1) * GROUP, s * rows : (s + 1) * rows]
            tile_ref[c, s] = jnp.concatenate([a, b], axis=1)
        if c % span == span - 1:
            run = slice(c + 1 - span, c + 1)
            copies.append(pltpu.make_async_copy(tile_ref.at[run], out_ref.at[run], done.at[c // span]))
            copies[-1].start()
    for copy in copies:
        copy.wait()


def call(kernel, out_shape, scratch=(), flops=0, bytes_accessed=0, places="v", out_specs=None):
    whole = {"v": pl.BlockSpec(memory_space=pltpu.VMEM), "s": pl.BlockSpec(memory_space=pltpu.SMEM)}
    return pl.pallas_call(
        kernel,
        out_shape=out_shape,
        in_specs=[whole[place] for place in places],
        **({} if out_specs is None else {"out_specs": out_specs}),
        scratch_shapes=list(scratch),
        compiler_params=pltpu.CompilerParams(vmem_limit_bytes=32 * 2**20),
        cost_estimate=pl.CostEstimate(flops=flops, bytes_accessed=bytes_accessed, transcendentals=0),
    )


def per_device(strain, fir_taps, spatial):
    rows, samples = strain.shape
    windows = samples // NFFT
    blocks = samples // LANES
    rep = lax.axis_size("rep")
    chan = lax.axis_size("chan")
    even = lax.axis_index("chan") % 2 == 0
    pairs_within = [(i, i ^ 1) for i in range(chan) if i ^ 1 < chan]
    pairs_across = [(i, j) for i in range(chan) for j in (i + 1 if i % 2 else i - 1,) if 0 <= j < chan]

    rim = jax.ShapeDtypeStruct((HALO, samples), bf16)
    within = call(lambda *refs: rim_kernel(True, *refs), rim, bytes_accessed=2**20)(strain)
    across = call(lambda *refs: rim_kernel(False, *refs), rim, bytes_accessed=2**20)(strain)
    near = lax.ppermute(within, "chan", pairs_within)
    far = lax.ppermute(across, "chan", pairs_across)

    table = jnp.asarray(dft_table())
    edge, own, lead, filter_matrix, edge_mix, direct_matrix = call(
        own_kernel,
        [
            jax.ShapeDtypeStruct((blocks // 2, rows, LANES), f32),
            jax.ShapeDtypeStruct((windows, rows, LANES), f32),
            jax.ShapeDtypeStruct((3, rows, LANES), f32),
            jax.ShapeDtypeStruct((2 * LANES, 2 * LANES), bf16),
            jax.ShapeDtypeStruct((2 * HALO, 2 * HALO, LANES), f32),
            jax.ShapeDtypeStruct((LANES + NFFT, LANES), bf16),
        ],
        [
            pltpu.VMEM((2 * rows, LANES + samples), bf16),
            pltpu.VMEM((windows, 2 * rows, NFFT), bf16),
            pltpu.VMEM((windows, rows, LANES), f32),
        ],
        flops=2 * 2 * rows * samples * 512,
        bytes_accessed=4 * 2**20,
        places="vssv",
    )(strain, fir_taps, spatial, table)
    count = windows * 2 * GROUP // LANES
    pieces = call(
        edge_kernel,
        jax.ShapeDtypeStruct((rep, count + 3, rows, LANES), bf16),
        [
            pltpu.VMEM((4 * HALO, LANES + samples // 2), bf16),
        ],
        flops=2 * 2 * rows * samples * 256,
        bytes_accessed=2 * 2**20,
        places="v" * 9,
    )(far, near, edge, own, lead, edge_mix, filter_matrix, table, direct_matrix)
    arrived = []
    for step in range(1, rep):
        to = [(i, i ^ step if rep & (rep - 1) == 0 else (i + step) % rep) for i in range(rep)]
        arrived.append(lax.ppermute(pieces[step], "rep", to))
    gathered = call(
        merge_kernel,
        jax.ShapeDtypeStruct((rep * count, rows, LANES), bf16),
        flops=2**16,
        bytes_accessed=2**18,
        places="v" * rep,
    )(pieces, *(arrived[i] for i in (0, 2, 1)))
    partners = [gathered]
    for step in range(1, STEPS + 1):
        partners.append(lax.ppermute(gathered, "chan", [((i + step) % chan, i) for i in range(chan)]))
    parts = gathered.shape[0]
    left = call(
        left_kernel,
        jax.ShapeDtypeStruct((2, rows * GROUP, parts * LANES), bf16),
        flops=2**20,
        bytes_accessed=2**20,
    )(gathered)
    scale = 1.0 / (windows * rep)
    tiles = (rows, STEPS + 1, BINS // rep, 2 * rows)
    return call(
        lambda *refs: tile_kernel(scale, *refs),
        jax.ShapeDtypeStruct(tiles, f32),
        [pltpu.VMEM(tiles, f32), pltpu.SemaphoreType.DMA((2,))],
        out_specs=pl.BlockSpec(memory_space=pl.ANY),
        flops=2**24,
        bytes_accessed=2**20,
        places="v" * (STEPS + 2),
    )(left, *partners)


def solution(mesh):
    in_specs = (P("chan", "rep"), P(), P())
    out_specs = P("chan", None, "rep", None)
    return jax.shard_map(
        per_device, mesh=mesh, in_specs=in_specs, out_specs=out_specs, check_vma=False
    )
```
